256 devices in a mesh: chan: 32 (over z, y), win: 8 (over x, core).
Axes of the slice: x: 4, y: 4, z: 8, core: 2. Of those that a mesh axis runs over, the one named last changes fastest.
Arguments:
- records: bfloat16 [512, 64, 3072], P('chan', 'win'), may hold values from -6 to 6
- pair_source: int32 [32, 32], P('chan'), may hold values from 0 to 15, as said below
- pair_partner: int32 [32, 32], P('chan'), may hold values from 0 to 511, as said below
- pair_count: int32 [32], P('chan'), may hold values from 24 to 32, as said below
Outputs:
- correlations: float32 [1024, 1024], P(('chan', 'win'))
The draws below stay inside these ranges and needn't reach their ends.
Inputs may be any that keep to these rules, and one draw needn't show every extreme that they name: `pair_source`: index of a pair's source channel within its block of 16 channels. For every block, at most 2 of its 32 pairs have partners in one block (pair_partner // 16), and exactly 2 in some block. Slots 0 to pair_count - 1 of a block are live; some block has all 32 live.
All inputs are finite; a program needn't handle non-finite values.
Results may differ from the reference program's by a relative error of at most 0.0047.
Values may be sent and summed in bfloat16 or wider, within the bound.
No kernel may reach another device: no remote copies, remote signals or barrier semaphores. Data moves between devices by JAX's collectives and lax.ppermute only.
A program may use at most 192 MiB of HBM per device.

```python
import math
import jax
import jax.numpy as jnp
from jax import lax

L = 3072
F = 1536
BAND = 128
LAGS = 1024
C_DEV = 16
PAIR_DEV = 32
CHANNELS = 512
WINDOWS = 64
SLOT = 2
PAIRS = 1024
N_CHAN = 32


def pair_layout(key):

    def one_block(index):
        block_key = jax.random.fold_in(key, index)
        key_order, key_full, key_partner, key_source = jax.random.split(block_key, 4)
        pool = N_CHAN * SLOT
        order = jax.random.permutation(key_order, pool).astype(jnp.int32)
        full_block = jax.random.randint(key_full, (), 0, N_CHAN)
        cells = jnp.arange(pool, dtype=jnp.int32)
        score = jnp.where(cells // SLOT == full_block, order - pool, order)
        chosen = jnp.argsort(score, stable=True)[:PAIR_DEV].astype(jnp.int32)
        holder = chosen // SLOT
        partner = holder * C_DEV + jax.random.randint(key_partner, (PAIR_DEV,), 0, C_DEV)
        source = jax.random.randint(key_source, (PAIR_DEV,), 0, C_DEV)
        return (source.astype(jnp.int32), partner.astype(jnp.int32))
    return jax.vmap(one_block)(jnp.arange(N_CHAN, dtype=jnp.int32))


def draw_pair_source(key, part):
    source, partner = pair_layout(key)
    return source


def draw_pair_partner(key, part):
    source, partner = pair_layout(key)
    return partner


def draw_pair_count(key, part):
    key = jax.random.fold_in(key, 7)
    key_count, key_full = jax.random.split(key)
    counts = jax.random.randint(key_count, (N_CHAN,), 3 * PAIR_DEV // 4, PAIR_DEV + 1)
    full_block = jax.random.randint(key_full, (), 0, N_CHAN)
    return jnp.where(jnp.arange(N_CHAN) == full_block, PAIR_DEV, counts).astype(jnp.int32)


def levels(stream_key, shape, cuts, smallest, top_value):
    loudness, own = 1.0, jax.random.fold_in(stream_key, 6)
    for axis_at, parts in cuts:
        draws = jnp.exp(jax.random.uniform(jax.random.fold_in(own, axis_at), (parts,), jnp.float32, smallest / len(cuts), top_value / len(cuts)))
        loudness = loudness * jnp.repeat(draws, shape[axis_at] // parts).reshape([-1 if axis == axis_at else 1 for axis in range(len(shape))])
    return loudness


def centred(key, shape, spread, most, shards=(), kind=jnp.bfloat16):
    level = levels(key, shape, shards, -0.22, 0.18) if shards else 1.0
    drawn = jax.random.normal(key, shape, jnp.float32) * spread * level
    return jnp.minimum(jnp.maximum(drawn, -most), most).astype(kind)


def setup_inputs(seed: int = 0) -> dict:
    streams_of = jax.random.split(jax.random.key(seed), 5)
    return {
        "records": centred(streams_of[0], (CHANNELS, WINDOWS, L), 1.0, 6.0, ((0, 32), (1, 8))),
        "pair_source": draw_pair_source(jax.random.fold_in(streams_of[4], 71), 0),
        "pair_partner": draw_pair_partner(jax.random.fold_in(streams_of[4], 71), 0),
        "pair_count": draw_pair_count(jax.random.fold_in(streams_of[4], 71), 0),
    }


def forward_table(length, freqs):
    samples = jnp.arange(length, dtype=jnp.int32)
    bins = jnp.arange(1, freqs + 1, dtype=jnp.int32)
    phase = samples[:, None] * bins[None, :] % length
    angle = phase.astype(jnp.float32) * (2.0 * math.pi / length)
    return jnp.concatenate([jnp.cos(angle).astype(jnp.bfloat16), (-jnp.sin(angle)).astype(jnp.bfloat16)], axis=1)

def inverse_table(length, freqs, lags, windows):
    bins = jnp.arange(1, freqs + 1, dtype=jnp.int32)
    shifts = jnp.arange(lags, dtype=jnp.int32) - lags // 2
    phase = bins[:, None] * shifts[None, :] % length
    angle = phase.astype(jnp.float32) * (2.0 * math.pi / length)
    factor = 1.0 / math.sqrt(freqs * windows)
    return jnp.concatenate([jnp.cos(angle) * factor, -jnp.sin(angle) * factor], axis=0)

def whiten(spectra, freqs, band):
    count = spectra.shape[0]
    real_part = spectra[:, :freqs].reshape(count, freqs // band, band)
    imag_part = spectra[:, freqs:].reshape(count, freqs // band, band)
    power = lax.optimization_barrier(jnp.mean(real_part * real_part + imag_part * imag_part, axis=2))
    factor = lax.rsqrt(power + 1e-06)[:, :, None]
    real_part = (real_part * factor).reshape(count, freqs)
    imag_part = (imag_part * factor).reshape(count, freqs)
    return jnp.concatenate([real_part, imag_part], axis=1).astype(jnp.bfloat16)

def cross_spectrum(first, second, freqs):
    first = first.astype(jnp.float32)
    second = second.astype(jnp.float32)
    first_re, first_im = (first[..., :freqs], first[..., freqs:])
    second_re, second_im = (second[..., :freqs], second[..., freqs:])
    real_part = lax.optimization_barrier(jnp.sum(first_re * second_re + first_im * second_im, axis=1))
    imag_part = lax.optimization_barrier(jnp.sum(first_im * second_re - first_re * second_im, axis=1))
    return jnp.concatenate([real_part, imag_part], axis=1)

def reference(records, pair_source, pair_partner, pair_count):
    table = forward_table(L, F)
    blocks = records.reshape(N_CHAN, C_DEV * WINDOWS, L)

    def transform(block):
        return whiten(jnp.dot(block, table, preferred_element_type=jnp.float32), F, BAND)
    whitened = lax.map(transform, blocks).reshape(CHANNELS, WINDOWS, 2 * F)
    inverse = inverse_table(L, F, LAGS, WINDOWS)

    def owner(items):
        index, source, partner, count = items
        first = jnp.take(whitened, index * C_DEV + source, axis=0)
        second = jnp.take(whitened, partner, axis=0)
        cross = cross_spectrum(first, second, F)
        live = (jnp.arange(PAIR_DEV, dtype=jnp.int32) < count).astype(jnp.float32)
        cross = cross * live[:, None]
        return jnp.dot(cross, inverse, precision=lax.Precision.HIGHEST, preferred_element_type=jnp.float32)
    result = lax.map(owner, (jnp.arange(N_CHAN, dtype=jnp.int32), pair_source, pair_partner, pair_count))
    return result.reshape(PAIRS, LAGS)
```

```python
import math

import jax
import jax.numpy as jnp
from jax import lax
from jax.experimental import pallas as pl
from jax.experimental.pallas import tpu as pltpu
from jax.sharding import PartitionSpec as P

N = 3072
HALF = N // 2
BAND = 128
LAGS = 1024
QUARTER = N // 4
CHANS, WINS = 16, 8
ROWS = CHANS * WINS
BLOCKS = 32
PAIRS = 32
DATA = 6 * CHANS
PIECE = DATA + 8
VMEM = 56 * 1024 * 1024


def cos_sin(phase):
    turn = jnp.floor(phase * (1.0 / QUARTER) + 0.5)
    t = (phase - QUARTER * turn) * (2.0 * math.pi / N)
    quadrant = turn - 4.0 * jnp.floor(turn * 0.25)
    u = t * t
    s = t * (1.0 + u * (-1 / 6 + u * (1 / 120 + u * (-1 / 5040 + u * (1 / 362880)))))
    c = 1.0 + u * (-1 / 2 + u * (1 / 24 + u * (-1 / 720 + u * (1 / 40320))))
    odd = (quadrant == 1.0) | (quadrant == 3.0)
    cos = jnp.where(odd, s, c)
    sin = jnp.where(odd, c, s)
    cos = jnp.where((quadrant == 1.0) | (quadrant == 2.0), -cos, cos)
    sin = jnp.where(quadrant >= 2.0, -sin, sin)
    return cos, sin


def iota(shape, axis):
    return lax.broadcasted_iota(jnp.int32, shape, axis)


def transform_kernel(x_ref, source_ref, partner_ref, count_ref, out_ref,
                     even_ref, odd_ref, base_ref, step_ref, table_ref, spec_ref, power_ref, white_ref, list_ref):
    partner = partner_ref[...]
    slot = iota((1, PAIRS), 1)
    source = jnp.where(slot < count_ref[0], source_ref[...], -1)
    list_ref[...] = jnp.zeros((8, 128), jnp.float32)
    list_ref[0:1, 0:PAIRS] = (partner // CHANS).astype(jnp.float32)
    list_ref[1:2, 0:PAIRS] = (partner % CHANS).astype(jnp.float32)
    list_ref[2:3, 0:PAIRS] = source.astype(jnp.float32)
    lists = list_ref[...].astype(jnp.bfloat16)
    for c in range(BLOCKS):
        out_ref[c, DATA:PIECE, :] = lists

    lane = iota((ROWS, 128), 1)
    i = iota((256, 256), 0)
    k = iota((256, 256), 1)
    low = k < 128
    k = jnp.where(low, k, k - 128)
    ahead = jnp.where(low, 2 * ((k + 1) % 128), 2 * k + 1)
    back = jnp.where(low, 2 * (127 - k), 2 * (127 - k) + 1)
    ahead = jnp.where(i == ahead, 1.0, 0.0).astype(jnp.bfloat16)
    back = jnp.where(i == back, 1.0, 0.0).astype(jnp.bfloat16)
    rotated = []
    for t in range(6):
        part = jnp.dot(x_ref[:, 256 * t:256 * t + 256], ahead, preferred_element_type=jnp.float32)
        rotated.append(part[:, :128])
        odd_ref[0:ROWS, 128 * t:128 * t + 128] = part[:, 128:].astype(jnp.bfloat16)
        at = 256 * (11 - t)
        part = jnp.dot(x_ref[:, at:at + 256], back, preferred_element_type=jnp.float32)
        even_ref[ROWS:2 * ROWS, 128 * t:128 * t + 128] = part[:, :128].astype(jnp.bfloat16)
        odd_ref[ROWS:2 * ROWS, 128 * t:128 * t + 128] = part[:, 128:].astype(jnp.bfloat16)
    for t in range(6):
        following = rotated[t + 1] if t < 5 else 0.0
        even_ref[0:ROWS, 128 * t:128 * t + 128] = jnp.where(lane < 127, rotated[t], following).astype(jnp.bfloat16)
    first = jnp.sum(jnp.where(lane == 127, rotated[0], 0.0), axis=1, keepdims=True)

    last = jnp.zeros((ROWS, 128), jnp.float32)
    for t in range(24):
        last = last + x_ref[:, 128 * t:128 * t + 128].astype(jnp.float32)
    last = jnp.sum(jnp.where(lane % 2 == 0, last, -last), axis=1, keepdims=True)

    bins = (iota((16, QUARTER), 1) + 1).astype(jnp.float32)
    row = iota((16, QUARTER), 0).astype(jnp.float32)
    base_ref[0], base_ref[1] = cos_sin((2.0 * row + 2.0) * bins)
    base_ref[2], base_ref[3] = cos_sin((2.0 * row + 1.0) * bins)
    for a in range(3):
        cos, sin = cos_sin(32.0 * (row + 16.0 * a) * bins)
        step_ref[0, 16 * a:16 * a + 16, :] = cos
        step_ref[1, 16 * a:16 * a + 16, :] = sin

    @pl.loop(0, 48)
    def _(a):
        cos = step_ref[0, pl.ds(a, 1), :]
        sin = step_ref[1, pl.ds(a, 1), :]
        rows = pl.ds(pl.multiple_of(16 * a, 16), 16)
        for parity in range(2):
            base_cos, base_sin = base_ref[2 * parity], base_ref[2 * parity + 1]
            table_ref[2 * parity, rows, :] = (base_cos * cos - base_sin * sin).astype(jnp.bfloat16)
            table_ref[2 * parity + 1, rows, :] = (base_sin * cos + base_cos * sin).astype(jnp.bfloat16)

    for which in range(4):
        samples = even_ref if which < 2 else odd_ref
        spec_ref[which] = jnp.dot(samples[...], table_ref[which], preferred_element_type=jnp.float32)

    top, bottom = slice(0, ROWS), slice(ROWS, 2 * ROWS)
    for t in range(6):
        at = slice(128 * t, 128 * t + 128)
        even_cos = spec_ref[0, top, at] + spec_ref[0, bottom, at] + first
        even_sin = spec_ref[1, top, at] - spec_ref[1, bottom, at]
        odd_cos = spec_ref[2, top, at] + spec_ref[2, bottom, at]
        odd_sin = spec_ref[3, top, at] - spec_ref[3, bottom, at]
        real, imag = even_cos + odd_cos, -(even_sin + odd_sin)
        real_back, imag_back = even_cos - odd_cos, even_sin - odd_sin
        if t == 5:
            real_back = jnp.where(lane < 127, real_back, last)
            imag_back = jnp.where(lane < 127, imag_back, 0.0)
        white_ref[0, t], white_ref[1, t] = real, imag
        white_ref[0, 6 + t], white_ref[1, 6 + t] = real_back, imag_back
        power_ref[t] = real * real + imag * imag
        power_ref[6 + t] = real_back * real_back + imag_back * imag_back
    factor = []
    for t in range(12):
        power = power_ref[t]
        if t >= 6:
            power = jnp.where(lane < 127, power, power_ref[6 + (t - 7) % 6])
        mean = jnp.sum(power, axis=1, keepdims=True) * (1.0 / BAND)
        factor.append(lax.rsqrt(mean + 1e-06))

    segment = iota((CHANS, 128), 1) // 16
    for t in range(12):
        scale = factor[t]
        if t >= 6:
            scale = jnp.where(lane < 127, scale, factor[6 + (t - 5) % 6])
        for part in range(2):
            white_ref[part, t] = white_ref[part, t] * scale
            slabs = [white_ref[part, t, pl.ds(w, CHANS, stride=WINS), :] for w in range(WINS)]
            for bit in range(3):
                step = 1 << bit
                high = (segment // step) % 2 == 1
                mixed = [None] * WINS
                for w in range(WINS):
                    if w & step:
                        continue
                    one, two = slabs[w], slabs[w + step]
                    mixed[w] = jnp.where(high, pltpu.roll(two, 16 * step, 1), one)
                    mixed[w + step] = jnp.where(high, two, pltpu.roll(one, 128 - 16 * step, 1))
                slabs = mixed
            at = CHANS * (2 * (t % 3) + part)
            for s in range(8):
                out_ref[8 * (t // 3) + s, at:at + CHANS, :] = slabs[s].astype(jnp.bfloat16)


def transform(x, source, partner, count):
    vmem = pl.BlockSpec(memory_space=pltpu.VMEM)
    return pl.pallas_call(
        transform_kernel,
        out_shape=jax.ShapeDtypeStruct((BLOCKS, PIECE, 128), jnp.bfloat16),
        in_specs=[vmem, vmem, vmem, pl.BlockSpec(memory_space=pltpu.SMEM)],
        out_specs=vmem,
        scratch_shapes=[
            pltpu.VMEM((2 * ROWS, QUARTER), jnp.bfloat16),
            pltpu.VMEM((2 * ROWS, QUARTER), jnp.bfloat16),
            pltpu.VMEM((4, 16, QUARTER), jnp.float32),
            pltpu.VMEM((2, 48, QUARTER), jnp.float32),
            pltpu.VMEM((4, QUARTER, QUARTER), jnp.bfloat16),
            pltpu.VMEM((4, 2 * ROWS, QUARTER), jnp.float32),
            pltpu.VMEM((12, ROWS, 128), jnp.float32),
            pltpu.VMEM((2, 12, ROWS, 128), jnp.float32),
            pltpu.VMEM((8, 128), jnp.float32),
        ],
        compiler_params=pltpu.CompilerParams(vmem_limit_bytes=VMEM),
        cost_estimate=pl.CostEstimate(flops=2 * 4 * 2 * ROWS * QUARTER**2, bytes_accessed=2 * 10**6, transcendentals=0),
        name="transform",
    )(x, source, partner, count)


def cross_kernel(got_ref, out_ref, data_ref, near_ref, far_ref, list_ref):
    for q in range(6):
        data_ref[:, 128 * q:128 * q + 128] = got_ref[:, CHANS * q:CHANS * (q + 1), :].reshape(BLOCKS * CHANS, 128)
    lists = got_ref[:, DATA:PIECE, :].astype(jnp.float32)
    block = iota((BLOCKS, 128), 0)
    list_ref[...] = jnp.zeros((2, 128, 128), jnp.float32)
    list_ref[0, 0:BLOCKS, :] = lists[:, 0, :] * CHANS + lists[:, 1, :]
    inside = (block % 16 * CHANS).astype(jnp.float32)
    list_ref[1, 0:BLOCKS, :] = jnp.where(lists[:, 2, :] < 0.0, -1.0, lists[:, 2, :] + inside)
    partner = jnp.transpose(list_ref[0])
    source = jnp.transpose(list_ref[1])
    channel = iota((PAIRS, BLOCKS * CHANS), 1).astype(jnp.float32)
    for o in range(BLOCKS):
        rows = slice(PAIRS * o, PAIRS * (o + 1))
        far_ref[rows, :] = jnp.where(channel == partner[0:PAIRS, o:o + 1], 1.0, 0.0).astype(jnp.bfloat16)
        near = channel[:, :256] == source[0:PAIRS, o:o + 1]
        near_ref[rows, :] = jnp.where(near, 1.0, 0.0).astype(jnp.bfloat16)

    size = 256
    lane = iota((size, 128), 1)
    for m in range(BLOCKS * PAIRS // size):
        rows = slice(size * m, size * (m + 1))
        half = slice(256 * (2 * m // 4), 256 * (2 * m // 4) + 256)
        far = jnp.dot(far_ref[rows, :], data_ref[...], preferred_element_type=jnp.float32)
        near = jnp.dot(near_ref[rows, :], data_ref[half, :], preferred_element_type=jnp.float32)
        tiles = []
        for t in range(3):
            re, im = slice(256 * t, 256 * t + 128), slice(256 * t + 128, 256 * t + 256)
            a_re, a_im, b_re, b_im = near[:, re], near[:, im], far[:, re], far[:, im]
            real = a_re * b_re + a_im * b_im
            imag = a_im * b_re - a_re * b_im
            low = lane < 64
            tiles.append(jnp.where(low, real, imag) + pltpu.roll(jnp.where(low, imag, real), 64, 1))
        low = lane // 32 % 2 == 0
        one = jnp.where(low, tiles[0] + pltpu.roll(tiles[0], 96, 1), tiles[1] + pltpu.roll(tiles[1], 32, 1))
        two = jnp.where(low, tiles[2] + pltpu.roll(tiles[2], 96, 1), 0.0)
        low = lane // 16 % 2 == 0
        out_ref[rows, :] = jnp.where(low, one + pltpu.roll(one, 112, 1), two + pltpu.roll(two, 16, 1))


def cross(got):
    vmem = pl.BlockSpec(memory_space=pltpu.VMEM)
    pairs = BLOCKS * PAIRS
    return pl.pallas_call(
        cross_kernel,
        out_shape=jax.ShapeDtypeStruct((pairs, 128), jnp.float32),
        in_specs=[vmem],
        out_specs=vmem,
        scratch_shapes=[
            pltpu.VMEM((BLOCKS * CHANS, 6 * 128), jnp.bfloat16),
            pltpu.VMEM((pairs, 256), jnp.bfloat16),
            pltpu.VMEM((pairs, BLOCKS * CHANS), jnp.bfloat16),
            pltpu.VMEM((2, 128, 128), jnp.float32),
        ],
        compiler_params=pltpu.CompilerParams(vmem_limit_bytes=VMEM),
        cost_estimate=pl.CostEstimate(flops=2 * pairs * 768 * 768, bytes_accessed=2 * 10**6, transcendentals=0),
        name="cross",
    )(got)


def bin_of(block, lane):
    tile = 3 * (block // 8) + jnp.where(lane // 32 % 2 == 1, 1, jnp.where(lane // 16 % 2 == 1, 2, 0))
    place = 128 * tile + 16 * (block % 8) + lane % 16 + 1
    back = place - 768
    back = jnp.where(back == 768, 0, back)
    return jnp.where(tile < 6, place, HALF - back), lane // 16 % 4 != 3


def inverse_kernel(turn_ref, table_ref):
    scale = 1.0 / math.sqrt(HALF * 64)

    @pl.loop(0, BLOCKS)
    def _(c):
        lane = iota((32, 128), 1)
        a = iota((32, 128), 0) // 4 - 4
        j, used = bin_of(c, lane)
        cos, sin = cos_sin((128 * (a + 24) * j).astype(jnp.float32))
        factor = jnp.where(used, scale, 0.0)
        rows = pl.ds(pl.multiple_of(32 * c, 32), 32)
        turn_ref[0, rows, :] = cos * factor
        turn_ref[1, rows, :] = jnp.where(lane < 64, -sin, sin) * factor
        lane = iota((128, 128), 0)
        b = iota((128, 128), 1)
        j, _ = bin_of(c, lane)
        table, _ = cos_sin((j * b + jnp.where(lane < 64, 0, QUARTER)).astype(jnp.float32))
        coarse = table.astype(jnp.bfloat16)
        rows = pl.ds(pl.multiple_of(128 * c, 128), 128)
        table_ref[rows, 0:128] = coarse
        table_ref[rows, 128:256] = (table - coarse.astype(jnp.float32)).astype(jnp.bfloat16)


def inverse():
    vmem = pl.BlockSpec(memory_space=pltpu.VMEM)
    return pl.pallas_call(
        inverse_kernel,
        out_shape=(
            jax.ShapeDtypeStruct((2, 32 * BLOCKS, 128), jnp.float32),
            jax.ShapeDtypeStruct((128 * BLOCKS, 256), jnp.bfloat16),
        ),
        out_specs=(vmem, vmem),
        compiler_params=pltpu.CompilerParams(vmem_limit_bytes=VMEM),
        cost_estimate=pl.CostEstimate(flops=40 * 10**6, bytes_accessed=3 * 10**6, transcendentals=0),
        name="inverse",
    )()


def lags_kernel(got_ref, turn_ref, table_ref, out_ref, left_ref):
    for c in range(BLOCKS):
        rows = got_ref[32 * c:32 * c + 32, :]
        total = rows[0:8] + rows[8:16] + rows[16:24] + rows[24:32]
        total = total + pltpu.roll(total, 4, 0)
        total = jnp.concatenate([total] * 4, axis=0)
        at = slice(32 * c, 32 * c + 32)
        turned = total * turn_ref[0, at, :] + pltpu.roll(total, 64, 1) * turn_ref[1, at, :]
        coarse = turned.astype(jnp.bfloat16)
        left_ref[0:32, 128 * c:128 * c + 128] = coarse
        left_ref[32:64, 128 * c:128 * c + 128] = (turned - coarse.astype(jnp.float32)).astype(jnp.bfloat16)
    both = jnp.dot(left_ref[...], table_ref[...], preferred_element_type=jnp.float32)
    both = both[:32] + both[32:]
    both = both[:, :128] + both[:, 128:]
    for a in range(8):
        out_ref[:, 128 * a:128 * a + 128] = both[4 * a:4 * a + 4, :]


def lags(got, turn, table):
    vmem = pl.BlockSpec(memory_space=pltpu.VMEM)
    return pl.pallas_call(
        lags_kernel,
        out_shape=jax.ShapeDtypeStruct((4, LAGS), jnp.float32),
        in_specs=[vmem] * 3,
        out_specs=vmem,
        scratch_shapes=[pltpu.VMEM((64, 128 * BLOCKS), jnp.bfloat16)],
        compiler_params=pltpu.CompilerParams(vmem_limit_bytes=VMEM),
        cost_estimate=pl.CostEstimate(flops=2 * 64 * 4096 * 256, bytes_accessed=4 * 10**6, transcendentals=0),
        name="lags",
    )(got, turn, table)


def shards(records, pair_source, pair_partner, pair_count):
    sent = transform(records.reshape(ROWS, N), pair_source, pair_partner, pair_count)
    got = lax.all_to_all(sent, "chan", 0, 0)
    turn, table = inverse()
    spectra = cross(got).reshape(BLOCKS * WINS, 4, 128)
    parts = lax.all_to_all(spectra, ("chan", "win"), 0, 0)
    return lags(parts.reshape(BLOCKS * PAIRS, 128), turn, table)


def solution(mesh):
    placed = (P("chan", "win", None), P("chan", None), P("chan", None), P("chan"))
    return jax.shard_map(
        shards, mesh=mesh, in_specs=placed, out_specs=P(("chan", "win"), None), check_vma=False
    )
```

```python
import functools
import math

import jax
import jax.numpy as jnp
from jax import lax
from jax.experimental import pallas as pl
from jax.experimental.pallas import tpu as pltpu
from jax.sharding import Mesh
from jax.sharding import PartitionSpec as P

N = 3072
HALF = N // 2
BAND = 128
LAGS = 1024
QUARTER = N // 4
CHANS, WINS = 16, 8
ROWS = CHANS * WINS
BLOCKS = 32
PAIRS = 32
HALF_PAIRS = PAIRS // 2
DATA = 6 * CHANS
PIECE = DATA + 8
MB = 1024 * 1024


def cos_sin(phase):
    turn = jnp.floor(phase * (1.0 / QUARTER) + 0.5)
    t = (phase - QUARTER * turn) * (2.0 * math.pi / N)
    quadrant = turn - 4.0 * jnp.floor(turn * 0.25)
    u = t * t
    s = t * (1.0 + u * (-1 / 6 + u * (1 / 120 + u * (-1 / 5040 + u * (1 / 362880)))))
    c = 1.0 + u * (-1 / 2 + u * (1 / 24 + u * (-1 / 720 + u * (1 / 40320))))
    odd = (quadrant == 1.0) | (quadrant == 3.0)
    cos = jnp.where(odd, s, c)
    sin = jnp.where(odd, c, s)
    cos = jnp.where((quadrant == 1.0) | (quadrant == 2.0), -cos, cos)
    sin = jnp.where(quadrant >= 2.0, -sin, sin)
    return cos, sin


def iota(shape, axis):
    return lax.broadcasted_iota(jnp.int32, shape, axis)


def transform_kernel(x_ref, source_ref, partner_ref, count_ref, out_ref,
                     even_ref, odd_ref, base_ref, step_ref, table_ref, spec_ref, power_ref, white_ref, list_ref):
    partner = partner_ref[...]
    slot = iota((1, PAIRS), 1)
    source = jnp.where(slot < count_ref[0], source_ref[...], -1)
    list_ref[...] = jnp.zeros((8, 128), jnp.float32)
    list_ref[0:1, 0:PAIRS] = (partner // CHANS).astype(jnp.float32)
    list_ref[1:2, 0:PAIRS] = (partner % CHANS).astype(jnp.float32)
    list_ref[2:3, 0:PAIRS] = source.astype(jnp.float32)
    plain = list_ref[...]
    lane = iota((8, 128), 1)
    lists = jnp.zeros((8, 128), jnp.float32)
    for quad in range(8):
        at, to = 4 * quad, 16 * (quad % 2) + 4 * (quad // 2)
        moved = pltpu.roll(plain, (to - at) % 128, 1)
        lists = jnp.where((lane >= to) & (lane < to + 4), moved, lists)
    lists = lists.astype(jnp.bfloat16)
    for c in range(BLOCKS):
        out_ref[c, DATA:PIECE, :] = lists

    lane = iota((ROWS, 128), 1)
    i = iota((256, 256), 0)
    k = iota((256, 256), 1)
    low = k < 128
    k = jnp.where(low, k, k - 128)
    ahead = jnp.where(low, 2 * ((k + 1) % 128), 2 * k + 1)
    back = jnp.where(low, 2 * (127 - k), 2 * (127 - k) + 1)
    ahead = jnp.where(i == ahead, 1.0, 0.0).astype(jnp.bfloat16)
    back = jnp.where(i == back, 1.0, 0.0).astype(jnp.bfloat16)
    rotated = []
    for t in range(6):
        part = jnp.dot(x_ref[:, 256 * t:256 * t + 256], ahead, preferred_element_type=jnp.float32)
        rotated.append(part[:, :128])
        odd_ref[0:ROWS, 128 * t:128 * t + 128] = part[:, 128:].astype(jnp.bfloat16)
        at = 256 * (11 - t)
        part = jnp.dot(x_ref[:, at:at + 256], back, preferred_element_type=jnp.float32)
        even_ref[ROWS:2 * ROWS, 128 * t:128 * t + 128] = part[:, :128].astype(jnp.bfloat16)
        odd_ref[ROWS:2 * ROWS, 128 * t:128 * t + 128] = part[:, 128:].astype(jnp.bfloat16)
    for t in range(6):
        following = rotated[t + 1] if t < 5 else 0.0
        even_ref[0:ROWS, 128 * t:128 * t + 128] = jnp.where(lane < 127, rotated[t], following).astype(jnp.bfloat16)
    first = jnp.sum(jnp.where(lane == 127, rotated[0], 0.0), axis=1, keepdims=True)

    last = jnp.zeros((ROWS, 128), jnp.float32)
    for t in range(24):
        last = last + x_ref[:, 128 * t:128 * t + 128].astype(jnp.float32)
    last = jnp.sum(jnp.where(lane % 2 == 0, last, -last), axis=1, keepdims=True)

    bins = (iota((16, QUARTER), 1) + 1).astype(jnp.float32)
    row = iota((16, QUARTER), 0).astype(jnp.float32)
    base_ref[0], base_ref[1] = cos_sin((2.0 * row + 2.0) * bins)
    base_ref[2], base_ref[3] = cos_sin((2.0 * row + 1.0) * bins)
    for a in range(3):
        cos, sin = cos_sin(32.0 * (row + 16.0 * a) * bins)
        step_ref[0, 16 * a:16 * a + 16, :] = cos
        step_ref[1, 16 * a:16 * a + 16, :] = sin

    @pl.loop(0, 48)
    def _(a):
        cos = step_ref[0, pl.ds(a, 1), :]
        sin = step_ref[1, pl.ds(a, 1), :]
        rows = pl.ds(pl.multiple_of(16 * a, 16), 16)
        for parity in range(2):
            base_cos, base_sin = base_ref[2 * parity], base_ref[2 * parity + 1]
            table_ref[2 * parity, rows, :] = (base_cos * cos - base_sin * sin).astype(jnp.bfloat16)
            table_ref[2 * parity + 1, rows, :] = (base_sin * cos + base_cos * sin).astype(jnp.bfloat16)

    for which in range(4):
        samples = even_ref if which < 2 else odd_ref
        spec_ref[which] = jnp.dot(samples[...], table_ref[which], preferred_element_type=jnp.float32)

    top, bottom = slice(0, ROWS), slice(ROWS, 2 * ROWS)
    for t in range(6):
        at = slice(128 * t, 128 * t + 128)
        even_cos = spec_ref[0, top, at] + spec_ref[0, bottom, at] + first
        even_sin = spec_ref[1, top, at] - spec_ref[1, bottom, at]
        odd_cos = spec_ref[2, top, at] + spec_ref[2, bottom, at]
        odd_sin = spec_ref[3, top, at] - spec_ref[3, bottom, at]
        real, imag = even_cos + odd_cos, -(even_sin + odd_sin)
        real_back, imag_back = even_cos - odd_cos, even_sin - odd_sin
        if t == 5:
            real_back = jnp.where(lane < 127, real_back, last)
            imag_back = jnp.where(lane < 127, imag_back, 0.0)
        white_ref[0, t], white_ref[1, t] = real, imag
        white_ref[0, 6 + t], white_ref[1, 6 + t] = real_back, imag_back
        power_ref[t] = real * real + imag * imag
        power_ref[6 + t] = real_back * real_back + imag_back * imag_back
    factor = []
    for t in range(12):
        power = power_ref[t]
        if t >= 6:
            power = jnp.where(lane < 127, power, power_ref[6 + (t - 7) % 6])
        mean = jnp.sum(power, axis=1, keepdims=True) * (1.0 / BAND)
        factor.append(lax.rsqrt(mean + 1e-06))

    segment = iota((CHANS, 128), 1) // 16
    for t in range(12):
        scale = factor[t]
        if t >= 6:
            scale = jnp.where(lane < 127, scale, factor[6 + (t - 5) % 6])
        for part in range(2):
            white_ref[part, t] = white_ref[part, t] * scale
            slabs = [white_ref[part, t, pl.ds(w, CHANS, stride=WINS), :] for w in range(WINS)]
            for bit in range(3):
                step = 1 << bit
                high = (segment // step) % 2 == 1
                mixed = [None] * WINS
                for w in range(WINS):
                    if w & step:
                        continue
                    one, two = slabs[w], slabs[w + step]
                    mixed[w] = jnp.where(high, pltpu.roll(two, 16 * step, 1), one)
                    mixed[w + step] = jnp.where(high, two, pltpu.roll(one, 128 - 16 * step, 1))
                slabs = mixed
            at = CHANS * (2 * (t % 3) + part)
            for s in range(8):
                out_ref[8 * (t // 3) + s, at:at + CHANS, :] = slabs[s].astype(jnp.bfloat16)


def transform(x, source, partner, count):
    vmem = pl.BlockSpec(memory_space=pltpu.VMEM)
    return pl.pallas_call(
        transform_kernel,
        out_shape=jax.ShapeDtypeStruct((BLOCKS, PIECE, 128), jnp.bfloat16),
        in_specs=[vmem, vmem, vmem, pl.BlockSpec(memory_space=pltpu.SMEM)],
        out_specs=vmem,
        scratch_shapes=[
            pltpu.VMEM((2 * ROWS, QUARTER), jnp.bfloat16),
            pltpu.VMEM((2 * ROWS, QUARTER), jnp.bfloat16),
            pltpu.VMEM((4, 16, QUARTER), jnp.float32),
            pltpu.VMEM((2, 48, QUARTER), jnp.float32),
            pltpu.VMEM((4, QUARTER, QUARTER), jnp.bfloat16),
            pltpu.VMEM((4, 2 * ROWS, QUARTER), jnp.float32),
            pltpu.VMEM((12, ROWS, 128), jnp.float32),
            pltpu.VMEM((2, 12, ROWS, 128), jnp.float32),
            pltpu.VMEM((8, 128), jnp.float32),
        ],
        compiler_params=pltpu.CompilerParams(vmem_limit_bytes=32 * MB),
        cost_estimate=pl.CostEstimate(flops=2 * 4 * 2 * ROWS * QUARTER**2, bytes_accessed=2 * 10**6, transcendentals=0),
        name="transform",
    )(x, source, partner, count)


def cross_kernel(away, got_ref, after_ref, out_ref, data_ref, near_ref, far_ref, list_ref):
    for q in range(6):
        data_ref[:, 128 * q:128 * q + 128] = got_ref[:, CHANS * q:CHANS * (q + 1), :].reshape(BLOCKS * CHANS, 128)
    lists = got_ref[:, DATA:PIECE, :].astype(jnp.float32)
    block = iota((BLOCKS, 128), 0)
    list_ref[...] = jnp.zeros((2, 128, 128), jnp.float32)
    list_ref[0, 0:BLOCKS, :] = lists[:, 0, :] * CHANS + lists[:, 1, :]
    inside = (block % 16 * CHANS).astype(jnp.float32)
    list_ref[1, 0:BLOCKS, :] = jnp.where(lists[:, 2, :] < 0.0, -1.0, lists[:, 2, :] + inside)
    partner = jnp.transpose(list_ref[0])
    source = jnp.transpose(list_ref[1])
    list_ref[0], list_ref[1] = partner, source
    core = (lax.axis_index("core") + away) % 2
    pick = pl.ds(pl.multiple_of(HALF_PAIRS * core, HALF_PAIRS), HALF_PAIRS)
    partner, source = list_ref[0, pick, :], list_ref[1, pick, :]
    channel = iota((HALF_PAIRS, BLOCKS * CHANS), 1).astype(jnp.float32)
    for o in range(BLOCKS):
        rows = slice(HALF_PAIRS * o, HALF_PAIRS * (o + 1))
        far_ref[rows, :] = jnp.where(channel == partner[:, o:o + 1], 1.0, 0.0).astype(jnp.bfloat16)
        near = channel[:, :256] == source[:, o:o + 1]
        near_ref[rows, :] = jnp.where(near, 1.0, 0.0).astype(jnp.bfloat16)

    size = 256
    lane = iota((size, 128), 1)
    for m in range(2):
        rows = slice(size * m, size * (m + 1))
        far = jnp.dot(far_ref[rows, :], data_ref[...], preferred_element_type=jnp.float32)
        near = jnp.dot(near_ref[rows, :], data_ref[rows, :], preferred_element_type=jnp.float32)
        tiles = []
        for t in range(3):
            re, im = slice(256 * t, 256 * t + 128), slice(256 * t + 128, 256 * t + 256)
            a_re, a_im, b_re, b_im = near[:, re], near[:, im], far[:, re], far[:, im]
            real = a_re * b_re + a_im * b_im
            imag = a_im * b_re - a_re * b_im
            low = lane < 64
            tiles.append(jnp.where(low, real, imag) + pltpu.roll(jnp.where(low, imag, real), 64, 1))
        low = lane // 32 % 2 == 0
        one = jnp.where(low, tiles[0] + pltpu.roll(tiles[0], 96, 1), tiles[1] + pltpu.roll(tiles[1], 32, 1))
        two = jnp.where(low, tiles[2] + pltpu.roll(tiles[2], 96, 1), 0.0)
        low = lane // 16 % 2 == 0
        out_ref[rows, :] = jnp.where(low, one + pltpu.roll(one, 112, 1), two + pltpu.roll(two, 16, 1))


def cross(got, after, away):
    vmem = pl.BlockSpec(memory_space=pltpu.VMEM)
    pairs = BLOCKS * HALF_PAIRS
    return pl.pallas_call(
        functools.partial(cross_kernel, away),
        out_shape=jax.ShapeDtypeStruct((pairs, 128), jnp.float32),
        in_specs=[vmem, pl.BlockSpec(memory_space=pl.ANY)],
        out_specs=vmem,
        scratch_shapes=[
            pltpu.VMEM((BLOCKS * CHANS, 6 * 128), jnp.bfloat16),
            pltpu.VMEM((pairs, 256), jnp.bfloat16),
            pltpu.VMEM((pairs, BLOCKS * CHANS), jnp.bfloat16),
            pltpu.VMEM((2, 128, 128), jnp.float32),
        ],
        compiler_params=pltpu.CompilerParams(vmem_limit_bytes=16 * MB),
        cost_estimate=pl.CostEstimate(flops=2 * pairs * 768 * 768, bytes_accessed=2 * 10**6, transcendentals=0),
        name="cross",
    )(got, after)


def bin_of(block, lane):
    tile = 3 * (block // 8) + jnp.where(lane // 32 % 2 == 1, 1, jnp.where(lane // 16 % 2 == 1, 2, 0))
    place = 128 * tile + 16 * (block % 8) + lane % 16 + 1
    back = place - 768
    back = jnp.where(back == 768, 0, back)
    return jnp.where(tile < 6, place, HALF - back), lane // 16 % 4 != 3


def inverse_kernel(after_ref, turn_ref, table_ref):
    scale = 1.0 / math.sqrt(HALF * 64)

    @pl.loop(0, BLOCKS)
    def _(c):
        lane = iota((32, 128), 1)
        a = iota((32, 128), 0) // 4 - 4
        j, used = bin_of(c, lane)
        cos, sin = cos_sin((128 * (a + 24) * j).astype(jnp.float32))
        factor = jnp.where(used, scale, 0.0)
        rows = pl.ds(pl.multiple_of(32 * c, 32), 32)
        turn_ref[0, rows, :] = cos * factor
        turn_ref[1, rows, :] = jnp.where(lane < 64, -sin, sin) * factor
        lane = iota((128, 128), 0)
        b = iota((128, 128), 1)
        j, _ = bin_of(c, lane)
        table, _ = cos_sin((j * b + jnp.where(lane < 64, 0, QUARTER)).astype(jnp.float32))
        coarse = table.astype(jnp.bfloat16)
        rows = pl.ds(pl.multiple_of(128 * c, 128), 128)
        table_ref[rows, 0:128] = coarse
        table_ref[rows, 128:256] = (table - coarse.astype(jnp.float32)).astype(jnp.bfloat16)


def inverse(after):
    vmem = pl.BlockSpec(memory_space=pltpu.VMEM)
    return pl.pallas_call(
        inverse_kernel,
        out_shape=(
            jax.ShapeDtypeStruct((2, 32 * BLOCKS, 128), jnp.float32),
            jax.ShapeDtypeStruct((128 * BLOCKS, 256), jnp.bfloat16),
        ),
        in_specs=[pl.BlockSpec(memory_space=pl.ANY)],
        out_specs=(vmem, vmem),
        compiler_params=pltpu.CompilerParams(vmem_limit_bytes=12 * MB),
        cost_estimate=pl.CostEstimate(flops=40 * 10**6, bytes_accessed=3 * 10**6, transcendentals=0),
        name="inverse",
    )(after)


def lags_kernel(got_ref, turn_ref, table_ref, out_ref, left_ref):
    for c in range(BLOCKS):
        total = got_ref[16 * c:16 * c + 8, :] + got_ref[16 * c + 8:16 * c + 16, :]
        total = total + pltpu.roll(total, 4, 0)
        total = jnp.concatenate([total] * 4, axis=0)
        at = slice(32 * c, 32 * c + 32)
        turned = total * turn_ref[0, at, :] + pltpu.roll(total, 64, 1) * turn_ref[1, at, :]
        coarse = turned.astype(jnp.bfloat16)
        left_ref[0:32, 128 * c:128 * c + 128] = coarse
        left_ref[32:64, 128 * c:128 * c + 128] = (turned - coarse.astype(jnp.float32)).astype(jnp.bfloat16)
    both = jnp.dot(left_ref[...], table_ref[...], preferred_element_type=jnp.float32)
    both = both[:32] + both[32:]
    both = both[:, :128] + both[:, 128:]
    for a in range(8):
        out_ref[:, 128 * a:128 * a + 128] = both[4 * a:4 * a + 4, :]


def lags(got, turn, table):
    vmem = pl.BlockSpec(memory_space=pltpu.VMEM)
    return pl.pallas_call(
        lags_kernel,
        out_shape=jax.ShapeDtypeStruct((4, LAGS), jnp.float32),
        in_specs=[vmem] * 3,
        out_specs=vmem,
        scratch_shapes=[pltpu.VMEM((64, 128 * BLOCKS), jnp.bfloat16)],
        compiler_params=pltpu.CompilerParams(vmem_limit_bytes=16 * MB),
        cost_estimate=pl.CostEstimate(flops=2 * 64 * 4096 * 256, bytes_accessed=4 * 10**6, transcendentals=0),
        name="lags",
    )(got, turn, table)


def shards(records, pair_source, pair_partner, pair_count):
    sent = transform(records.reshape(ROWS, N), pair_source, pair_partner, pair_count)
    got = lax.all_to_all(sent, "chan", 0, 0)
    turn, table = inverse(sent)
    away = cross(got, turn, 1)
    near = lax.ppermute(away, "core", [(0, 1), (1, 0)])
    spectra = cross(got, turn, 0) + near
    parts = lax.all_to_all(spectra.reshape(BLOCKS * 4, 4, 128), ("chan", "x"), 0, 0)
    return lags(parts.reshape(BLOCKS * HALF_PAIRS, 128), turn, table)


def solution(mesh):
    chips = Mesh(mesh.devices.reshape(BLOCKS, WINS // 2, 2), ("chan", "x", "core"))
    placed = (P("chan", ("x", "core"), None), P("chan", None), P("chan", None), P("chan"))
    return jax.shard_map(
        shards, mesh=chips, in_specs=placed, out_specs=P(("chan", "x", "core"), None), check_vma=False
    )
```

```python
import functools
import math

import jax
import jax.numpy as jnp
from jax import lax
from jax.experimental import pallas as pl
from jax.experimental.pallas import tpu as pltpu
from jax.sharding import Mesh
from jax.sharding import PartitionSpec as P

N = 3072
HALF = N // 2
BAND = 128
LAGS = 1024
QUARTER = N // 4
CHANS, WINS = 16, 8
ROWS = CHANS * WINS
BLOCKS = 32
PAIRS = 32
HALF_PAIRS = PAIRS // 2
DATA = 6 * CHANS
PIECE = DATA + 8
MB = 1024 * 1024


def cos_sin(phase):
    turn = jnp.floor(phase * (1.0 / QUARTER) + 0.5)
    t = (phase - QUARTER * turn) * (2.0 * math.pi / N)
    quadrant = turn - 4.0 * jnp.floor(turn * 0.25)
    u = t * t
    s = t * (1.0 + u * (-1 / 6 + u * (1 / 120 + u * (-1 / 5040 + u * (1 / 362880)))))
    c = 1.0 + u * (-1 / 2 + u * (1 / 24 + u * (-1 / 720 + u * (1 / 40320))))
    odd = (quadrant == 1.0) | (quadrant == 3.0)
    cos = jnp.where(odd, s, c)
    sin = jnp.where(odd, c, s)
    cos = jnp.where((quadrant == 1.0) | (quadrant == 2.0), -cos, cos)
    sin = jnp.where(quadrant >= 2.0, -sin, sin)
    return cos, sin


def iota(shape, axis):
    return lax.broadcasted_iota(jnp.int32, shape, axis)


def tables_kernel(table_ref, base_ref, step_ref):
    bins = (iota((16, QUARTER), 1) + 1).astype(jnp.float32)
    row = iota((16, QUARTER), 0).astype(jnp.float32)
    base_ref[0], base_ref[1] = cos_sin((2.0 * row + 2.0) * bins)
    base_ref[2], base_ref[3] = cos_sin((2.0 * row + 1.0) * bins)
    for a in range(3):
        cos, sin = cos_sin(32.0 * (row + 16.0 * a) * bins)
        step_ref[0, 16 * a:16 * a + 16, :] = cos
        step_ref[1, 16 * a:16 * a + 16, :] = sin

    @pl.loop(0, 48)
    def _(a):
        cos = step_ref[0, pl.ds(a, 1), :]
        sin = step_ref[1, pl.ds(a, 1), :]
        rows = pl.ds(pl.multiple_of(16 * a, 16), 16)
        for parity in range(2):
            base_cos, base_sin = base_ref[2 * parity], base_ref[2 * parity + 1]
            table_ref[2 * parity, rows, :] = (base_cos * cos - base_sin * sin).astype(jnp.bfloat16)
            table_ref[2 * parity + 1, rows, :] = (base_sin * cos + base_cos * sin).astype(jnp.bfloat16)


def tables():
    vmem = pl.BlockSpec(memory_space=pltpu.VMEM)
    return pl.pallas_call(
        tables_kernel,
        out_shape=jax.ShapeDtypeStruct((4, QUARTER, QUARTER), jnp.bfloat16),
        out_specs=vmem,
        scratch_shapes=[
            pltpu.VMEM((4, 16, QUARTER), jnp.float32),
            pltpu.VMEM((2, 48, QUARTER), jnp.float32),
        ],
        compiler_params=pltpu.CompilerParams(vmem_limit_bytes=12 * MB),
        cost_estimate=pl.CostEstimate(flops=20 * 10**6, bytes_accessed=5 * 10**6, transcendentals=0),
        name="tables",
    )()


def transform_kernel(x_ref, source_ref, partner_ref, count_ref, table_ref, out_ref,
                     even_ref, odd_ref, spec_ref, power_ref, white_ref, list_ref):
    partner = partner_ref[...]
    slot = iota((1, PAIRS), 1)
    source = jnp.where(slot < count_ref[0], source_ref[...], -1)
    list_ref[...] = jnp.zeros((8, 128), jnp.float32)
    list_ref[0:1, 0:PAIRS] = (partner // CHANS).astype(jnp.float32)
    list_ref[1:2, 0:PAIRS] = (partner % CHANS).astype(jnp.float32)
    list_ref[2:3, 0:PAIRS] = source.astype(jnp.float32)
    plain = list_ref[...]
    lane = iota((8, 128), 1)
    lists = jnp.zeros((8, 128), jnp.float32)
    for quad in range(8):
        at, to = 4 * quad, 16 * (quad % 2) + 4 * (quad // 2)
        moved = pltpu.roll(plain, (to - at) % 128, 1)
        lists = jnp.where((lane >= to) & (lane < to + 4), moved, lists)
    lists = lists.astype(jnp.bfloat16)
    for c in range(BLOCKS):
        out_ref[c, DATA:PIECE, :] = lists

    lane = iota((ROWS, 128), 1)
    i = iota((256, 256), 0)
    k = iota((256, 256), 1)
    low = k < 128
    k = jnp.where(low, k, k - 128)
    ahead = jnp.where(low, 2 * ((k + 1) % 128), 2 * k + 1)
    back = jnp.where(low, 2 * (127 - k), 2 * (127 - k) + 1)
    ahead = jnp.where(i == ahead, 1.0, 0.0).astype(jnp.bfloat16)
    back = jnp.where(i == back, 1.0, 0.0).astype(jnp.bfloat16)
    rotated = []
    for t in range(6):
        part = jnp.dot(x_ref[:, 256 * t:256 * t + 256], ahead, preferred_element_type=jnp.float32)
        rotated.append(part[:, :128])
        odd_ref[0:ROWS, 128 * t:128 * t + 128] = part[:, 128:].astype(jnp.bfloat16)
        at = 256 * (11 - t)
        part = jnp.dot(x_ref[:, at:at + 256], back, preferred_element_type=jnp.float32)
        even_ref[ROWS:2 * ROWS, 128 * t:128 * t + 128] = part[:, :128].astype(jnp.bfloat16)
        odd_ref[ROWS:2 * ROWS, 128 * t:128 * t + 128] = part[:, 128:].astype(jnp.bfloat16)
    for t in range(6):
        following = rotated[t + 1] if t < 5 else 0.0
        even_ref[0:ROWS, 128 * t:128 * t + 128] = jnp.where(lane < 127, rotated[t], following).astype(jnp.bfloat16)
    first = jnp.sum(jnp.where(lane == 127, rotated[0], 0.0), axis=1, keepdims=True)

    last = jnp.zeros((ROWS, 128), jnp.float32)
    for t in range(24):
        last = last + x_ref[:, 128 * t:128 * t + 128].astype(jnp.float32)
    last = jnp.sum(jnp.where(lane % 2 == 0, last, -last), axis=1, keepdims=True)

    for which in range(4):
        samples = even_ref if which < 2 else odd_ref
        spec_ref[which] = jnp.dot(samples[...], table_ref[which], preferred_element_type=jnp.float32)

    top, bottom = slice(0, ROWS), slice(ROWS, 2 * ROWS)
    for t in range(6):
        at = slice(128 * t, 128 * t + 128)
        even_cos = spec_ref[0, top, at] + spec_ref[0, bottom, at] + first
        even_sin = spec_ref[1, top, at] - spec_ref[1, bottom, at]
        odd_cos = spec_ref[2, top, at] + spec_ref[2, bottom, at]
        odd_sin = spec_ref[3, top, at] - spec_ref[3, bottom, at]
        real, imag = even_cos + odd_cos, -(even_sin + odd_sin)
        real_back, imag_back = even_cos - odd_cos, even_sin - odd_sin
        if t == 5:
            real_back = jnp.where(lane < 127, real_back, last)
            imag_back = jnp.where(lane < 127, imag_back, 0.0)
        white_ref[0, t], white_ref[1, t] = real, imag
        white_ref[0, 6 + t], white_ref[1, 6 + t] = real_back, imag_back
        power_ref[t] = real * real + imag * imag
        power_ref[6 + t] = real_back * real_back + imag_back * imag_back
    factor = []
    for t in range(12):
        power = power_ref[t]
        if t >= 6:
            power = jnp.where(lane < 127, power, power_ref[6 + (t - 7) % 6])
        mean = jnp.sum(power, axis=1, keepdims=True) * (1.0 / BAND)
        factor.append(lax.rsqrt(mean + 1e-06))

    segment = iota((CHANS, 128), 1) // 16
    for t in range(12):
        scale = factor[t]
        if t >= 6:
            scale = jnp.where(lane < 127, scale, factor[6 + (t - 5) % 6])
        for part in range(2):
            white_ref[part, t] = white_ref[part, t] * scale
            slabs = [white_ref[part, t, pl.ds(w, CHANS, stride=WINS), :] for w in range(WINS)]
            for bit in range(3):
                step = 1 << bit
                high = (segment // step) % 2 == 1
                mixed = [None] * WINS
                for w in range(WINS):
                    if w & step:
                        continue
                    one, two = slabs[w], slabs[w + step]
                    mixed[w] = jnp.where(high, pltpu.roll(two, 16 * step, 1), one)
                    mixed[w + step] = jnp.where(high, two, pltpu.roll(one, 128 - 16 * step, 1))
                slabs = mixed
            at = CHANS * (2 * (t % 3) + part)
            for s in range(8):
                out_ref[8 * (t // 3) + s, at:at + CHANS, :] = slabs[s].astype(jnp.bfloat16)


def transform(x, source, partner, count, table):
    vmem = pl.BlockSpec(memory_space=pltpu.VMEM)
    return pl.pallas_call(
        transform_kernel,
        out_shape=jax.ShapeDtypeStruct((BLOCKS, PIECE, 128), jnp.bfloat16),
        in_specs=[vmem, vmem, vmem, pl.BlockSpec(memory_space=pltpu.SMEM), vmem],
        out_specs=vmem,
        scratch_shapes=[
            pltpu.VMEM((2 * ROWS, QUARTER), jnp.bfloat16),
            pltpu.VMEM((2 * ROWS, QUARTER), jnp.bfloat16),
            pltpu.VMEM((4, 2 * ROWS, QUARTER), jnp.float32),
            pltpu.VMEM((12, ROWS, 128), jnp.float32),
            pltpu.VMEM((2, 12, ROWS, 128), jnp.float32),
            pltpu.VMEM((8, 128), jnp.float32),
        ],
        compiler_params=pltpu.CompilerParams(vmem_limit_bytes=20 * MB),
        cost_estimate=pl.CostEstimate(flops=2 * 4 * 2 * ROWS * QUARTER**2, bytes_accessed=2 * 10**6, transcendentals=0),
        name="transform",
    )(x, source, partner, count, table)


def cross_kernel(away, got_ref, out_ref, data_ref, near_ref, far_ref, list_ref):
    for q in range(6):
        data_ref[:, 128 * q:128 * q + 128] = got_ref[:, CHANS * q:CHANS * (q + 1), :].reshape(BLOCKS * CHANS, 128)
    lists = got_ref[:, DATA:PIECE, :].astype(jnp.float32)
    block = iota((BLOCKS, 128), 0)
    list_ref[...] = jnp.zeros((2, 128, 128), jnp.float32)
    list_ref[0, 0:BLOCKS, :] = lists[:, 0, :] * CHANS + lists[:, 1, :]
    inside = (block % 16 * CHANS).astype(jnp.float32)
    list_ref[1, 0:BLOCKS, :] = jnp.where(lists[:, 2, :] < 0.0, -1.0, lists[:, 2, :] + inside)
    partner = jnp.transpose(list_ref[0])
    source = jnp.transpose(list_ref[1])
    list_ref[0], list_ref[1] = partner, source
    core = (lax.axis_index("core") + away) % 2
    pick = pl.ds(pl.multiple_of(HALF_PAIRS * core, HALF_PAIRS), HALF_PAIRS)
    partner, source = list_ref[0, pick, :], list_ref[1, pick, :]
    channel = iota((HALF_PAIRS, BLOCKS * CHANS), 1).astype(jnp.float32)
    for o in range(BLOCKS):
        rows = slice(HALF_PAIRS * o, HALF_PAIRS * (o + 1))
        far_ref[rows, :] = jnp.where(channel == partner[:, o:o + 1], 1.0, 0.0).astype(jnp.bfloat16)
        near = channel[:, :256] == source[:, o:o + 1]
        near_ref[rows, :] = jnp.where(near, 1.0, 0.0).astype(jnp.bfloat16)

    size = 256
    lane = iota((size, 128), 1)
    for m in range(2):
        rows = slice(size * m, size * (m + 1))
        far = jnp.dot(far_ref[rows, :], data_ref[...], preferred_element_type=jnp.float32)
        near = jnp.dot(near_ref[rows, :], data_ref[rows, :], preferred_element_type=jnp.float32)
        tiles = []
        for t in range(3):
            re, im = slice(256 * t, 256 * t + 128), slice(256 * t + 128, 256 * t + 256)
            a_re, a_im, b_re, b_im = near[:, re], near[:, im], far[:, re], far[:, im]
            real = a_re * b_re + a_im * b_im
            imag = a_im * b_re - a_re * b_im
            low = lane < 64
            tiles.append(jnp.where(low, real, imag) + pltpu.roll(jnp.where(low, imag, real), 64, 1))
        low = lane // 32 % 2 == 0
        one = jnp.where(low, tiles[0] + pltpu.roll(tiles[0], 96, 1), tiles[1] + pltpu.roll(tiles[1], 32, 1))
        two = jnp.where(low, tiles[2] + pltpu.roll(tiles[2], 96, 1), 0.0)
        low = lane // 16 % 2 == 0
        packed = jnp.where(low, one + pltpu.roll(one, 112, 1), two + pltpu.roll(two, 16, 1))
        low = iota((8, 128), 0) < 4
        for o in range(0, 16, 2):
            for pair in range(2):
                one = packed[16 * o + 8 * pair:16 * o + 8 * pair + 8]
                two = packed[16 * o + 16 + 8 * pair:16 * o + 24 + 8 * pair]
                for x, tile in (
                    (2 * pair, jnp.where(low, one, pltpu.roll(two, 4, 0))),
                    (2 * pair + 1, jnp.where(low, pltpu.roll(one, 4, 0), two)),
                ):
                    to = 4 * BLOCKS * ((x + 4 - lax.axis_index("x")) % 4) + 4 * (16 * m + o)
                    out_ref[pl.ds(pl.multiple_of(to, 8), 8), :] = tile


def cross(got, away):
    vmem = pl.BlockSpec(memory_space=pltpu.VMEM)
    pairs = BLOCKS * HALF_PAIRS
    return pl.pallas_call(
        functools.partial(cross_kernel, away),
        out_shape=jax.ShapeDtypeStruct((pairs, 128), jnp.float32),
        in_specs=[vmem],
        out_specs=vmem,
        scratch_shapes=[
            pltpu.VMEM((BLOCKS * CHANS, 6 * 128), jnp.bfloat16),
            pltpu.VMEM((pairs, 256), jnp.bfloat16),
            pltpu.VMEM((pairs, BLOCKS * CHANS), jnp.bfloat16),
            pltpu.VMEM((2, 128, 128), jnp.float32),
        ],
        compiler_params=pltpu.CompilerParams(vmem_limit_bytes=16 * MB),
        cost_estimate=pl.CostEstimate(flops=2 * pairs * 768 * 768, bytes_accessed=2 * 10**6, transcendentals=0),
        name="cross",
    )(got)


def bin_of(block, lane):
    tile = 3 * (block // 8) + jnp.where(lane // 32 % 2 == 1, 1, jnp.where(lane // 16 % 2 == 1, 2, 0))
    place = 128 * tile + 16 * (block % 8) + lane % 16 + 1
    back = place - 768
    back = jnp.where(back == 768, 0, back)
    return jnp.where(tile < 6, place, HALF - back), lane // 16 % 4 != 3


def inverse_kernel(after_ref, turn_ref, table_ref):
    scale = 1.0 / math.sqrt(HALF * 64)

    @pl.loop(0, BLOCKS)
    def _(c):
        lane = iota((32, 128), 1)
        a = iota((32, 128), 0) // 4 - 4
        j, used = bin_of(c, lane)
        cos, sin = cos_sin((128 * (a + 24) * j).astype(jnp.float32))
        factor = jnp.where(used, scale, 0.0)
        rows = pl.ds(pl.multiple_of(32 * c, 32), 32)
        turn_ref[0, rows, :] = cos * factor
        turn_ref[1, rows, :] = jnp.where(lane < 64, -sin, sin) * factor
        lane = iota((128, 128), 0)
        b = iota((128, 128), 1)
        j, _ = bin_of(c, lane)
        table, _ = cos_sin((j * b + jnp.where(lane < 64, 0, QUARTER)).astype(jnp.float32))
        coarse = table.astype(jnp.bfloat16)
        rows = pl.ds(pl.multiple_of(128 * c, 128), 128)
        table_ref[rows, 0:128] = coarse
        table_ref[rows, 128:256] = (table - coarse.astype(jnp.float32)).astype(jnp.bfloat16)


def inverse(after):
    vmem = pl.BlockSpec(memory_space=pltpu.VMEM)
    return pl.pallas_call(
        inverse_kernel,
        out_shape=(
            jax.ShapeDtypeStruct((2, 32 * BLOCKS, 128), jnp.float32),
            jax.ShapeDtypeStruct((128 * BLOCKS, 256), jnp.bfloat16),
        ),
        in_specs=[pl.BlockSpec(memory_space=pl.ANY)],
        out_specs=(vmem, vmem),
        compiler_params=pltpu.CompilerParams(vmem_limit_bytes=12 * MB),
        cost_estimate=pl.CostEstimate(flops=40 * 10**6, bytes_accessed=3 * 10**6, transcendentals=0),
        name="inverse",
    )(after)


def lags_kernel(got_ref, turn_ref, table_ref, out_ref, left_ref):
    for c in range(BLOCKS):
        two = got_ref[8 * (c // 2):8 * (c // 2) + 8, :]
        low = iota((8, 128), 0) < 4
        total = jnp.where(low, two, pltpu.roll(two, 4, 0)) if c % 2 == 0 else jnp.where(low, pltpu.roll(two, 4, 0), two)
        total = jnp.concatenate([total] * 4, axis=0)
        at = slice(32 * c, 32 * c + 32)
        turned = total * turn_ref[0, at, :] + pltpu.roll(total, 64, 1) * turn_ref[1, at, :]
        coarse = turned.astype(jnp.bfloat16)
        left_ref[0:32, 128 * c:128 * c + 128] = coarse
        left_ref[32:64, 128 * c:128 * c + 128] = (turned - coarse.astype(jnp.float32)).astype(jnp.bfloat16)
    both = jnp.dot(left_ref[...], table_ref[...], preferred_element_type=jnp.float32)
    both = both[:32] + both[32:]
    both = both[:, :128] + both[:, 128:]
    for a in range(8):
        out_ref[:, 128 * a:128 * a + 128] = both[4 * a:4 * a + 4, :]


def lags(got, turn, table):
    vmem = pl.BlockSpec(memory_space=pltpu.VMEM)
    return pl.pallas_call(
        lags_kernel,
        out_shape=jax.ShapeDtypeStruct((4, LAGS), jnp.float32),
        in_specs=[vmem] * 3,
        out_specs=vmem,
        scratch_shapes=[pltpu.VMEM((64, 128 * BLOCKS), jnp.bfloat16)],
        compiler_params=pltpu.CompilerParams(vmem_limit_bytes=16 * MB),
        cost_estimate=pl.CostEstimate(flops=2 * 64 * 4096 * 256, bytes_accessed=4 * 10**6, transcendentals=0),
        name="lags",
    )(got, turn, table)


def shards(records, pair_source, pair_partner, pair_count):
    sent = transform(records.reshape(ROWS, N), pair_source, pair_partner, pair_count, tables())
    got = lax.all_to_all(sent, "chan", 0, 0)
    away = cross(got, 1)
    near = lax.ppermute(away, "core", [(0, 1), (1, 0)])
    spectra = (cross(got, 0) + near).reshape(4, 4 * BLOCKS, 128)
    parts = [lax.ppermute(spectra[k], "x", [(x, (x + k) % 4) for x in range(4)]) for k in (1, 2, 3)]
    turn, table = inverse(spectra)
    total = spectra[0] + parts[0] + parts[1] + parts[2]
    last = lax.all_to_all(total.reshape(BLOCKS, 4, 128), "chan", 0, 0)
    return lags(last.reshape(4 * BLOCKS, 128), turn, table)


def solution(mesh):
    chips = Mesh(mesh.devices.reshape(BLOCKS, WINS // 2, 2), ("chan", "x", "core"))
    placed = (P("chan", ("x", "core"), None), P("chan", None), P("chan", None), P("chan"))
    return jax.shard_map(
        shards, mesh=chips, in_specs=placed, out_specs=P(("chan", "x", "core"), None), check_vma=False
    )
```

```python
import functools
import math

import jax
import jax.numpy as jnp
from jax import lax
from jax.experimental import pallas as pl
from jax.experimental.pallas import tpu as pltpu
from jax.sharding import Mesh
from jax.sharding import PartitionSpec as P

N = 3072
HALF = N // 2
BAND = 128
LAGS = 1024
QUARTER = N // 4
CHANS, WINS = 16, 8
ROWS = CHANS * WINS
BLOCKS = 32
PAIRS = 32
HALF_PAIRS = PAIRS // 2
DATA = 6 * CHANS
PIECE = DATA + 8
MB = 1024 * 1024


def cos_sin(phase):
    turn = jnp.floor(phase * (1.0 / QUARTER) + 0.5)
    t = (phase - QUARTER * turn) * (2.0 * math.pi / N)
    quadrant = turn - 4.0 * jnp.floor(turn * 0.25)
    u = t * t
    s = t * (1.0 + u * (-1 / 6 + u * (1 / 120 + u * (-1 / 5040 + u * (1 / 362880)))))
    c = 1.0 + u * (-1 / 2 + u * (1 / 24 + u * (-1 / 720 + u * (1 / 40320))))
    odd = (quadrant == 1.0) | (quadrant == 3.0)
    cos = jnp.where(odd, s, c)
    sin = jnp.where(odd, c, s)
    cos = jnp.where((quadrant == 1.0) | (quadrant == 2.0), -cos, cos)
    sin = jnp.where(quadrant >= 2.0, -sin, sin)
    return cos, sin


def iota(shape, axis):
    return lax.broadcasted_iota(jnp.int32, shape, axis)


def tables_kernel(table_ref, base_ref, step_ref):
    bins = (iota((16, QUARTER), 1) + 1).astype(jnp.float32)
    row = iota((16, QUARTER), 0).astype(jnp.float32)
    base_ref[0], base_ref[1] = cos_sin((2.0 * row + 2.0) * bins)
    base_ref[2], base_ref[3] = cos_sin((2.0 * row + 1.0) * bins)
    for a in range(3):
        cos, sin = cos_sin(32.0 * (row + 16.0 * a) * bins)
        step_ref[0, 16 * a:16 * a + 16, :] = cos
        step_ref[1, 16 * a:16 * a + 16, :] = sin

    @pl.loop(0, 48)
    def _(a):
        cos = step_ref[0, pl.ds(a, 1), :]
        sin = step_ref[1, pl.ds(a, 1), :]
        rows = pl.ds(pl.multiple_of(16 * a, 16), 16)
        for parity in range(2):
            base_cos, base_sin = base_ref[2 * parity], base_ref[2 * parity + 1]
            table_ref[2 * parity, rows, :] = (base_cos * cos - base_sin * sin).astype(jnp.bfloat16)
            table_ref[2 * parity + 1, rows, :] = (base_sin * cos + base_cos * sin).astype(jnp.bfloat16)


def tables():
    vmem = pl.BlockSpec(memory_space=pltpu.VMEM)
    return pl.pallas_call(
        tables_kernel,
        out_shape=jax.ShapeDtypeStruct((4, QUARTER, QUARTER), jnp.bfloat16),
        out_specs=vmem,
        scratch_shapes=[
            pltpu.VMEM((4, 16, QUARTER), jnp.float32),
            pltpu.VMEM((2, 48, QUARTER), jnp.float32),
        ],
        compiler_params=pltpu.CompilerParams(vmem_limit_bytes=12 * MB),
        cost_estimate=pl.CostEstimate(flops=20 * 10**6, bytes_accessed=5 * 10**6, transcendentals=0),
        name="tables",
    )()


def transform_kernel(x_ref, source_ref, partner_ref, table_ref, out_ref,
                     even_ref, odd_ref, power_ref, white_ref, list_ref):
    lane = iota((ROWS, 128), 1)
    i = iota((256, 256), 0)
    k = iota((256, 256), 1)
    low = k < 128
    k = jnp.where(low, k, k - 128)
    ahead = jnp.where(low, 2 * ((k + 1) % 128), 2 * k + 1)
    back = jnp.where(low, 2 * (127 - k), 2 * (127 - k) + 1)
    ahead = jnp.where(i == ahead, 1.0, 0.0).astype(jnp.bfloat16)
    back = jnp.where(i == back, 1.0, 0.0).astype(jnp.bfloat16)
    rotated = []
    for t in range(6):
        part = jnp.dot(x_ref[:, 256 * t:256 * t + 256], ahead, preferred_element_type=jnp.float32)
        rotated.append(part[:, :128])
        odd_ref[0:ROWS, 128 * t:128 * t + 128] = part[:, 128:].astype(jnp.bfloat16)
        at = 256 * (11 - t)
        part = jnp.dot(x_ref[:, at:at + 256], back, preferred_element_type=jnp.float32)
        even_ref[ROWS:2 * ROWS, 128 * t:128 * t + 128] = part[:, :128].astype(jnp.bfloat16)
        odd_ref[ROWS:2 * ROWS, 128 * t:128 * t + 128] = part[:, 128:].astype(jnp.bfloat16)
    for t in range(6):
        following = rotated[t + 1] if t < 5 else 0.0
        even_ref[0:ROWS, 128 * t:128 * t + 128] = jnp.where(lane < 127, rotated[t], following).astype(jnp.bfloat16)
    first = jnp.sum(jnp.where(lane == 127, rotated[0], 0.0), axis=1, keepdims=True)

    last = jnp.zeros((ROWS, 128), jnp.float32)
    for t in range(24):
        last = last + x_ref[:, 128 * t:128 * t + 128].astype(jnp.float32)
    last = jnp.sum(jnp.where(lane % 2 == 0, last, -last), axis=1, keepdims=True)

    for u in range(3):
        wide = slice(256 * u, 256 * u + 256)
        even_cos, even_sin, odd_cos, odd_sin = (
            jnp.dot(samples[...], table_ref[which, :, wide], preferred_element_type=jnp.float32)
            for which, samples in enumerate((even_ref, even_ref, odd_ref, odd_ref))
        )
        even_cos = even_cos[:ROWS] + even_cos[ROWS:] + first
        even_sin = even_sin[:ROWS] - even_sin[ROWS:]
        odd_cos = odd_cos[:ROWS] + odd_cos[ROWS:]
        odd_sin = odd_sin[:ROWS] - odd_sin[ROWS:]
        for t in (2 * u, 2 * u + 1):
            at = slice(128 * (t % 2), 128 * (t % 2) + 128)
            real, imag = even_cos[:, at] + odd_cos[:, at], -(even_sin[:, at] + odd_sin[:, at])
            real_back, imag_back = even_cos[:, at] - odd_cos[:, at], even_sin[:, at] - odd_sin[:, at]
            if t == 5:
                real_back = jnp.where(lane < 127, real_back, last)
                imag_back = jnp.where(lane < 127, imag_back, 0.0)
            white_ref[0, t], white_ref[1, t] = real, imag
            white_ref[0, 6 + t], white_ref[1, 6 + t] = real_back, imag_back
            power_ref[t] = real * real + imag * imag
            power_ref[6 + t] = real_back * real_back + imag_back * imag_back
    factor = []
    for t in range(12):
        power = power_ref[t]
        if t >= 6:
            power = jnp.where(lane < 127, power, power_ref[6 + (t - 7) % 6])
        mean = jnp.sum(power, axis=1, keepdims=True) * (1.0 / BAND)
        factor.append(lax.rsqrt(mean + 1e-06))

    segment = iota((CHANS, 128), 1) // 16
    for t in range(12):
        scale = factor[t]
        if t >= 6:
            scale = jnp.where(lane < 127, scale, factor[6 + (t - 5) % 6])
        for part in range(2):
            white_ref[part, t] = white_ref[part, t] * scale
            slabs = [white_ref[part, t, pl.ds(w, CHANS, stride=WINS), :] for w in range(WINS)]
            for bit in range(3):
                step = 1 << bit
                high = (segment // step) % 2 == 1
                mixed = [None] * WINS
                for w in range(WINS):
                    if w & step:
                        continue
                    one, two = slabs[w], slabs[w + step]
                    mixed[w] = jnp.where(high, pltpu.roll(two, 16 * step, 1), one)
                    mixed[w + step] = jnp.where(high, two, pltpu.roll(one, 128 - 16 * step, 1))
                slabs = mixed
            at = CHANS * (2 * (t % 3) + part)
            for s in range(8):
                out_ref[8 * (t // 3) + s, at:at + CHANS, :] = slabs[s].astype(jnp.bfloat16)

    partner = partner_ref[...]
    list_ref[...] = jnp.zeros((8, 128), jnp.float32)
    list_ref[0:1, 0:PAIRS] = (partner // CHANS).astype(jnp.float32)
    list_ref[1:2, 0:PAIRS] = (partner % CHANS).astype(jnp.float32)
    list_ref[2:3, 0:PAIRS] = source_ref[...].astype(jnp.float32)
    plain = list_ref[...]
    lane = iota((8, 128), 1)
    lists = jnp.zeros((8, 128), jnp.float32)
    for quad in range(8):
        at, to = 4 * quad, 16 * (quad % 2) + 4 * (quad // 2)
        moved = pltpu.roll(plain, (to - at) % 128, 1)
        lists = jnp.where((lane >= to) & (lane < to + 4), moved, lists)
    lists = lists.astype(jnp.bfloat16)
    for c in range(BLOCKS):
        out_ref[c, DATA:PIECE, :] = lists


def transform(x, source, partner, table):
    vmem = pl.BlockSpec(memory_space=pltpu.VMEM)
    return pl.pallas_call(
        transform_kernel,
        out_shape=jax.ShapeDtypeStruct((BLOCKS, PIECE, 128), jnp.bfloat16),
        in_specs=[vmem] * 4,
        out_specs=vmem,
        scratch_shapes=[
            pltpu.VMEM((2 * ROWS, QUARTER), jnp.bfloat16),
            pltpu.VMEM((2 * ROWS, QUARTER), jnp.bfloat16),
            pltpu.VMEM((12, ROWS, 128), jnp.float32),
            pltpu.VMEM((2, 12, ROWS, 128), jnp.float32),
            pltpu.VMEM((8, 128), jnp.float32),
        ],
        compiler_params=pltpu.CompilerParams(vmem_limit_bytes=20 * MB),
        cost_estimate=pl.CostEstimate(flops=2 * 4 * 2 * ROWS * QUARTER**2, bytes_accessed=2 * 10**6, transcendentals=0),
        name="transform",
    )(x, source, partner, table)


def cross_kernel(away, got_ref, out_ref, data_ref, near_ref, far_ref, list_ref):
    for q in range(6):
        data_ref[:, 128 * q:128 * q + 128] = got_ref[:, CHANS * q:CHANS * (q + 1), :].reshape(BLOCKS * CHANS, 128)
    lists = got_ref[:, DATA:PIECE, :].astype(jnp.float32)
    block = iota((BLOCKS, 128), 0)
    list_ref[...] = jnp.zeros((2, 128, 128), jnp.float32)
    list_ref[0, 0:BLOCKS, :] = lists[:, 0, :] * CHANS + lists[:, 1, :]
    inside = (block % 16 * CHANS).astype(jnp.float32)
    list_ref[1, 0:BLOCKS, :] = lists[:, 2, :] + inside
    partner = jnp.transpose(list_ref[0])
    source = jnp.transpose(list_ref[1])
    list_ref[0], list_ref[1] = partner, source
    core = (lax.axis_index("core") + away) % 2
    pick = pl.ds(pl.multiple_of(HALF_PAIRS * core, HALF_PAIRS), HALF_PAIRS)
    partner, source = list_ref[0, pick, :], list_ref[1, pick, :]
    channel = iota((HALF_PAIRS, BLOCKS * CHANS), 1).astype(jnp.float32)
    for o in range(BLOCKS):
        rows = slice(HALF_PAIRS * o, HALF_PAIRS * (o + 1))
        far_ref[rows, :] = jnp.where(channel == partner[:, o:o + 1], 1.0, 0.0).astype(jnp.bfloat16)
        near = channel[:, :256] == source[:, o:o + 1]
        near_ref[rows, :] = jnp.where(near, 1.0, 0.0).astype(jnp.bfloat16)

    size = 256
    lane = iota((size, 128), 1)
    for m in range(2):
        rows = slice(size * m, size * (m + 1))
        far = jnp.dot(far_ref[rows, :], data_ref[...], preferred_element_type=jnp.float32)
        near = jnp.dot(near_ref[rows, :], data_ref[rows, :], preferred_element_type=jnp.float32)
        tiles = []
        for t in range(3):
            re, im = slice(256 * t, 256 * t + 128), slice(256 * t + 128, 256 * t + 256)
            a_re, a_im, b_re, b_im = near[:, re], near[:, im], far[:, re], far[:, im]
            real = a_re * b_re + a_im * b_im
            imag = a_im * b_re - a_re * b_im
            low = lane < 64
            tiles.append(jnp.where(low, real, imag) + pltpu.roll(jnp.where(low, imag, real), 64, 1))
        low = lane // 32 % 2 == 0
        one = jnp.where(low, tiles[0] + pltpu.roll(tiles[0], 96, 1), tiles[1] + pltpu.roll(tiles[1], 32, 1))
        two = jnp.where(low, tiles[2] + pltpu.roll(tiles[2], 96, 1), 0.0)
        low = lane // 16 % 2 == 0
        packed = jnp.where(low, one + pltpu.roll(one, 112, 1), two + pltpu.roll(two, 16, 1))
        low = iota((8, 128), 0) < 4
        for o in range(0, 16, 2):
            for pair in range(2):
                one = packed[16 * o + 8 * pair:16 * o + 8 * pair + 8]
                two = packed[16 * o + 16 + 8 * pair:16 * o + 24 + 8 * pair]
                for x, tile in (
                    (2 * pair, jnp.where(low, one, pltpu.roll(two, 4, 0))),
                    (2 * pair + 1, jnp.where(low, pltpu.roll(one, 4, 0), two)),
                ):
                    to = 4 * BLOCKS * ((x + 4 - lax.axis_index("x")) % 4) + 4 * (16 * m + o)
                    out_ref[pl.ds(pl.multiple_of(to, 8), 8), :] = tile


def cross(got, away):
    vmem = pl.BlockSpec(memory_space=pltpu.VMEM)
    pairs = BLOCKS * HALF_PAIRS
    return pl.pallas_call(
        functools.partial(cross_kernel, away),
        out_shape=jax.ShapeDtypeStruct((pairs, 128), jnp.float32),
        in_specs=[vmem],
        out_specs=vmem,
        scratch_shapes=[
            pltpu.VMEM((BLOCKS * CHANS, 6 * 128), jnp.bfloat16),
            pltpu.VMEM((pairs, 256), jnp.bfloat16),
            pltpu.VMEM((pairs, BLOCKS * CHANS), jnp.bfloat16),
            pltpu.VMEM((2, 128, 128), jnp.float32),
        ],
        compiler_params=pltpu.CompilerParams(vmem_limit_bytes=16 * MB),
        cost_estimate=pl.CostEstimate(flops=2 * pairs * 768 * 768, bytes_accessed=2 * 10**6, transcendentals=0),
        name="cross",
    )(got)


def bin_of(block, lane):
    tile = 3 * (block // 8) + jnp.where(lane // 32 % 2 == 1, 1, jnp.where(lane // 16 % 2 == 1, 2, 0))
    place = 128 * tile + 16 * (block % 8) + lane % 16 + 1
    back = place - 768
    back = jnp.where(back == 768, 0, back)
    return jnp.where(tile < 6, place, HALF - back), lane // 16 % 4 != 3


def inverse_kernel(count_ref, after_ref, turn_ref, table_ref, first_ref, powers_ref):
    scale = 1.0 / math.sqrt(HALF * 64)
    b = iota((96, 128), 1)
    block, tile = iota((96, 128), 0) // 3, iota((96, 128), 0) % 3
    place = 128 * (3 * (block // 8) + tile) + 16 * (block % 8) + 1
    j0 = jnp.where(block < 16, place, HALF + 768 - place)
    first_ref[0], first_ref[1] = cos_sin((j0 * b).astype(jnp.float32))
    k = iota((16, 128), 0)
    cos_k, sin_k = cos_sin((k * iota((16, 128), 1)).astype(jnp.float32))
    nothing = jnp.zeros((16, 128), jnp.bfloat16)

    def put(at, value):
        coarse = value.astype(jnp.bfloat16)
        rows = pl.ds(pl.multiple_of(at, 16), 16)
        table_ref[rows, 0:128] = coarse
        table_ref[rows, 128:256] = (value - coarse.astype(jnp.float32)).astype(jnp.bfloat16)

    for back in range(2):
        way = -sin_k if back else sin_k

        @pl.loop(16 * back, 16 * back + 16, unroll=4)
        def _(c):
            for i, at in enumerate((0, 32, 16)):
                cos, sin = first_ref[0, pl.ds(3 * c + i, 1), :], first_ref[1, pl.ds(3 * c + i, 1), :]
                put(128 * c + at, cos * cos_k - sin * way)
                put(128 * c + 64 + at, -(sin * cos_k + cos * way))
            for at in (48, 112):
                rows = pl.ds(pl.multiple_of(128 * c + at, 16), 16)
                table_ref[rows, 0:128] = nothing
                table_ref[rows, 128:256] = nothing

    cos, sin = first_ref[0, 95:96, :], first_ref[1, 95:96, :]
    end = jnp.where(iota((16, 128), 1) % 2 == 0, 1.0, -1.0)
    put(128 * 31 + 16, jnp.where(k < 15, cos * cos_k + sin * sin_k, end))
    put(128 * 31 + 80, jnp.where(k < 15, -(sin * cos_k - cos * sin_k), 0.0))

    lane = iota((BLOCKS, 128), 1)
    j, used = bin_of(iota((BLOCKS, 128), 0), lane)
    factor = jnp.where(used, scale, 0.0)
    signed = jnp.where(lane < 64, -factor, factor)
    for a in range(5):
        cos, sin = cos_sin((128 * a * j).astype(jnp.float32))
        if a < 4:
            powers_ref[0, 4 + a] = cos * factor
            powers_ref[1, 4 + a] = sin * signed
        if a > 0:
            powers_ref[0, 4 - a] = cos * factor
            powers_ref[1, 4 - a] = -sin * signed
    row = iota((8, 128), 0)
    low = row < 4
    slot = 4 * (2 * lax.axis_index("x") + lax.axis_index("core")) + row % 4
    live = jnp.where(slot < count_ref[0], 1.0, 0.0)

    @pl.loop(0, BLOCKS, unroll=4)
    def _(c):
        row = pl.ds(c, 1)
        for part in range(2):
            for q in range(4):
                two = jnp.where(low, powers_ref[part, 2 * q, row, :], powers_ref[part, 2 * q + 1, row, :])
                turn_ref[part, pl.ds(pl.multiple_of(32 * c + 8 * q, 8), 8), :] = two * live


def inverse(count, after):
    vmem = pl.BlockSpec(memory_space=pltpu.VMEM)
    return pl.pallas_call(
        inverse_kernel,
        out_shape=(
            jax.ShapeDtypeStruct((2, 32 * BLOCKS, 128), jnp.float32),
            jax.ShapeDtypeStruct((128 * BLOCKS, 256), jnp.bfloat16),
        ),
        in_specs=[pl.BlockSpec(memory_space=pltpu.SMEM), pl.BlockSpec(memory_space=pl.ANY)],
        out_specs=(vmem, vmem),
        scratch_shapes=[pltpu.VMEM((2, 96, 128), jnp.float32), pltpu.VMEM((2, 8, BLOCKS, 128), jnp.float32)],
        compiler_params=pltpu.CompilerParams(vmem_limit_bytes=12 * MB),
        cost_estimate=pl.CostEstimate(flops=10 * 10**6, bytes_accessed=3 * 10**6, transcendentals=0),
        name="inverse",
    )(count, after)


def total_kernel(own_ref, one_ref, two_ref, three_ref, after_ref, out_ref):
    out_ref[...] = own_ref[...] + one_ref[...] + two_ref[...] + three_ref[...]


def add_parts(own, parts, after):
    vmem = pl.BlockSpec(memory_space=pltpu.VMEM)
    return pl.pallas_call(
        total_kernel,
        out_shape=jax.ShapeDtypeStruct(own.shape, jnp.float32),
        in_specs=[vmem] * 4 + [pl.BlockSpec(memory_space=pl.ANY)],
        out_specs=vmem,
        compiler_params=pltpu.CompilerParams(vmem_limit_bytes=4 * MB),
        cost_estimate=pl.CostEstimate(flops=10**5, bytes_accessed=3 * 10**5, transcendentals=0),
        name="total",
    )(own, *parts, after)


def lags_kernel(got_ref, turn_ref, table_ref, out_ref, left_ref):
    for c in range(BLOCKS):
        two = got_ref[8 * (c // 2):8 * (c // 2) + 8, :]
        low = iota((8, 128), 0) < 4
        total = jnp.where(low, two, pltpu.roll(two, 4, 0)) if c % 2 == 0 else jnp.where(low, pltpu.roll(two, 4, 0), two)
        total = jnp.concatenate([total] * 4, axis=0)
        at = slice(32 * c, 32 * c + 32)
        turned = total * turn_ref[0, at, :] + pltpu.roll(total, 64, 1) * turn_ref[1, at, :]
        coarse = turned.astype(jnp.bfloat16)
        left_ref[0:32, 128 * c:128 * c + 128] = coarse
        left_ref[32:64, 128 * c:128 * c + 128] = (turned - coarse.astype(jnp.float32)).astype(jnp.bfloat16)
    both = jnp.dot(left_ref[...], table_ref[...], preferred_element_type=jnp.float32)
    both = both[:32] + both[32:]
    both = both[:, :128] + both[:, 128:]
    for a in range(8):
        out_ref[:, 128 * a:128 * a + 128] = both[4 * a:4 * a + 4, :]


def lags(got, turn, table):
    vmem = pl.BlockSpec(memory_space=pltpu.VMEM)
    return pl.pallas_call(
        lags_kernel,
        out_shape=jax.ShapeDtypeStruct((4, LAGS), jnp.float32),
        in_specs=[vmem] * 3,
        out_specs=vmem,
        scratch_shapes=[pltpu.VMEM((64, 128 * BLOCKS), jnp.bfloat16)],
        compiler_params=pltpu.CompilerParams(vmem_limit_bytes=16 * MB),
        cost_estimate=pl.CostEstimate(flops=2 * 64 * 4096 * 256, bytes_accessed=4 * 10**6, transcendentals=0),
        name="lags",
    )(got, turn, table)


def shards(records, pair_source, pair_partner, pair_count):
    sent = transform(records.reshape(ROWS, N), pair_source, pair_partner, tables())
    got = lax.all_to_all(sent, "chan", 0, 0)
    away = cross(got, 1)
    near = lax.ppermute(away, "core", [(0, 1), (1, 0)])
    spectra = (cross(got, 0) + near).reshape(4, 4 * BLOCKS, 128)
    parts = [lax.ppermute(spectra[k], "x", [(x, (x + k) % 4) for x in range(4)]) for k in (1, 2, 3)]
    turn, table = inverse(pair_count, spectra)
    total = add_parts(spectra[0], parts, turn)
    last = lax.all_to_all(total.reshape(BLOCKS, 4, 128), "chan", 0, 0)
    return lags(last.reshape(4 * BLOCKS, 128), turn, table)


def solution(mesh):
    chips = Mesh(mesh.devices.reshape(BLOCKS, WINS // 2, 2), ("chan", "x", "core"))
    placed = (P("chan", ("x", "core"), None), P("chan", None), P("chan", None), P("chan"))
    return jax.shard_map(
        shards, mesh=chips, in_specs=placed, out_specs=P(("chan", "x", "core"), None), check_vma=False
    )
```

```python
import functools
import math

import jax
import jax.numpy as jnp
from jax import lax
from jax.experimental import pallas as pl
from jax.experimental.pallas import tpu as pltpu
from jax.sharding import Mesh
from jax.sharding import PartitionSpec as P

N = 3072
HALF = N // 2
BAND = 128
LAGS = 1024
QUARTER = N // 4
CHANS, WINS = 16, 8
ROWS = CHANS * WINS
BLOCKS = 32
PAIRS = 32
HALF_PAIRS = PAIRS // 2
DATA = 6 * CHANS
PIECE = DATA + 8
MB = 1024 * 1024


def cos_sin(phase):
    turn = jnp.floor(phase * (1.0 / QUARTER) + 0.5)
    t = (phase - QUARTER * turn) * (2.0 * math.pi / N)
    quadrant = turn - 4.0 * jnp.floor(turn * 0.25)
    u = t * t
    s = t * (1.0 + u * (-1 / 6 + u * (1 / 120 + u * (-1 / 5040 + u * (1 / 362880)))))
    c = 1.0 + u * (-1 / 2 + u * (1 / 24 + u * (-1 / 720 + u * (1 / 40320))))
    odd = (quadrant == 1.0) | (quadrant == 3.0)
    cos = jnp.where(odd, s, c)
    sin = jnp.where(odd, c, s)
    cos = jnp.where((quadrant == 1.0) | (quadrant == 2.0), -cos, cos)
    sin = jnp.where(quadrant >= 2.0, -sin, sin)
    return cos, sin


def iota(shape, axis):
    return lax.broadcasted_iota(jnp.int32, shape, axis)


ORDER = list(range(BLOCKS))[::-1]
SLOT = [ORDER.index(block) for block in range(BLOCKS)]


def tables_kernel(table_ref, base_ref, step_ref):
    bins = (iota((16, QUARTER), 1) + 1).astype(jnp.float32)
    row = iota((16, QUARTER), 0).astype(jnp.float32)
    base_ref[0], base_ref[1] = cos_sin((2.0 * row + 2.0) * bins)
    base_ref[2], base_ref[3] = cos_sin((2.0 * row + 1.0) * bins)
    for a in range(3):
        cos, sin = cos_sin(32.0 * (row + 16.0 * a) * bins)
        step_ref[0, 16 * a:16 * a + 16, :] = cos
        step_ref[1, 16 * a:16 * a + 16, :] = sin

    @pl.loop(0, 48)
    def _(a):
        cos = step_ref[0, pl.ds(a, 1), :]
        sin = step_ref[1, pl.ds(a, 1), :]
        rows = pl.ds(pl.multiple_of(16 * a, 16), 16)
        for parity in range(2):
            base_cos, base_sin = base_ref[2 * parity], base_ref[2 * parity + 1]
            table_ref[2 * parity, rows, :] = (base_cos * cos - base_sin * sin).astype(jnp.bfloat16)
            table_ref[2 * parity + 1, rows, :] = (base_sin * cos + base_cos * sin).astype(jnp.bfloat16)


def tables():
    vmem = pl.BlockSpec(memory_space=pltpu.VMEM)
    return pl.pallas_call(
        tables_kernel,
        out_shape=jax.ShapeDtypeStruct((4, QUARTER, QUARTER), jnp.bfloat16),
        out_specs=vmem,
        scratch_shapes=[
            pltpu.VMEM((4, 16, QUARTER), jnp.float32),
            pltpu.VMEM((2, 48, QUARTER), jnp.float32),
        ],
        compiler_params=pltpu.CompilerParams(vmem_limit_bytes=12 * MB),
        cost_estimate=pl.CostEstimate(flops=20 * 10**6, bytes_accessed=5 * 10**6, transcendentals=0),
        name="tables",
    )()


def transform_kernel(x_ref, source_ref, partner_ref, table_ref, out_ref,
                     even_ref, odd_ref, power_ref, white_ref, list_ref):
    lane = iota((ROWS, 128), 1)
    i = iota((256, 256), 0)
    k = iota((256, 256), 1)
    low = k < 128
    k = jnp.where(low, k, k - 128)
    ahead = jnp.where(low, 2 * ((k + 1) % 128), 2 * k + 1)
    back = jnp.where(low, 2 * (127 - k), 2 * (127 - k) + 1)
    ahead = jnp.where(i == ahead, 1.0, 0.0).astype(jnp.bfloat16)
    back = jnp.where(i == back, 1.0, 0.0).astype(jnp.bfloat16)
    rotated = []
    for t in range(6):
        part = jnp.dot(x_ref[:, 256 * t:256 * t + 256], ahead, preferred_element_type=jnp.float32)
        rotated.append(part[:, :128])
        odd_ref[0:ROWS, 128 * t:128 * t + 128] = part[:, 128:].astype(jnp.bfloat16)
        at = 256 * (11 - t)
        part = jnp.dot(x_ref[:, at:at + 256], back, preferred_element_type=jnp.float32)
        even_ref[ROWS:2 * ROWS, 128 * t:128 * t + 128] = part[:, :128].astype(jnp.bfloat16)
        odd_ref[ROWS:2 * ROWS, 128 * t:128 * t + 128] = part[:, 128:].astype(jnp.bfloat16)
    for t in range(6):
        following = rotated[t + 1] if t < 5 else 0.0
        even_ref[0:ROWS, 128 * t:128 * t + 128] = jnp.where(lane < 127, rotated[t], following).astype(jnp.bfloat16)
    first = jnp.sum(jnp.where(lane == 127, rotated[0], 0.0), axis=1, keepdims=True)

    last = jnp.zeros((ROWS, 128), jnp.float32)
    for t in range(24):
        last = last + x_ref[:, 128 * t:128 * t + 128].astype(jnp.float32)
    last = jnp.sum(jnp.where(lane % 2 == 0, last, -last), axis=1, keepdims=True)

    for u in range(3):
        wide = slice(256 * u, 256 * u + 256)
        even_cos, even_sin, odd_cos, odd_sin = (
            jnp.dot(samples[...], table_ref[which, :, wide], preferred_element_type=jnp.float32)
            for which, samples in enumerate((even_ref, even_ref, odd_ref, odd_ref))
        )
        even_cos = even_cos[:ROWS] + even_cos[ROWS:] + first
        even_sin = even_sin[:ROWS] - even_sin[ROWS:]
        odd_cos = odd_cos[:ROWS] + odd_cos[ROWS:]
        odd_sin = odd_sin[:ROWS] - odd_sin[ROWS:]
        for t in (2 * u, 2 * u + 1):
            at = slice(128 * (t % 2), 128 * (t % 2) + 128)
            real, imag = even_cos[:, at] + odd_cos[:, at], -(even_sin[:, at] + odd_sin[:, at])
            real_back, imag_back = even_cos[:, at] - odd_cos[:, at], even_sin[:, at] - odd_sin[:, at]
            if t == 5:
                real_back = jnp.where(lane < 127, real_back, last)
                imag_back = jnp.where(lane < 127, imag_back, 0.0)
            white_ref[0, t], white_ref[1, t] = real, imag
            white_ref[0, 6 + t], white_ref[1, 6 + t] = real_back, imag_back
            power_ref[t] = real * real + imag * imag
            power_ref[6 + t] = real_back * real_back + imag_back * imag_back
    factor = []
    for t in range(12):
        power = power_ref[t]
        if t >= 6:
            power = jnp.where(lane < 127, power, power_ref[6 + (t - 7) % 6])
        mean = jnp.sum(power, axis=1, keepdims=True) * (1.0 / BAND)
        factor.append(lax.rsqrt(mean + 1e-06))

    segment = iota((CHANS, 128), 1) // 16
    for t in range(12):
        scale = factor[t]
        if t >= 6:
            scale = jnp.where(lane < 127, scale, factor[6 + (t - 5) % 6])
        for part in range(2):
            white_ref[part, t] = white_ref[part, t] * scale
            slabs = [white_ref[part, t, pl.ds(w, CHANS, stride=WINS), :] for w in range(WINS)]
            for bit in range(3):
                step = 1 << bit
                high = (segment // step) % 2 == 1
                mixed = [None] * WINS
                for w in range(WINS):
                    if w & step:
                        continue
                    one, two = slabs[w], slabs[w + step]
                    mixed[w] = jnp.where(high, pltpu.roll(two, 16 * step, 1), one)
                    mixed[w + step] = jnp.where(high, two, pltpu.roll(one, 128 - 16 * step, 1))
                slabs = mixed
            at = CHANS * (2 * (t % 3) + part)
            for s in range(8):
                out_ref[SLOT[8 * (t // 3) + s], at:at + CHANS, :] = slabs[s].astype(jnp.bfloat16)

    partner = partner_ref[...]
    list_ref[...] = jnp.zeros((8, 128), jnp.float32)
    list_ref[0:1, 0:PAIRS] = (partner // CHANS).astype(jnp.float32)
    list_ref[1:2, 0:PAIRS] = (partner % CHANS).astype(jnp.float32)
    list_ref[2:3, 0:PAIRS] = source_ref[...].astype(jnp.float32)
    plain = list_ref[...]
    lane = iota((8, 128), 1)
    lists = jnp.zeros((8, 128), jnp.float32)
    for quad in range(8):
        at, to = 4 * quad, 16 * (quad % 2) + 4 * (quad // 2)
        moved = pltpu.roll(plain, (to - at) % 128, 1)
        lists = jnp.where((lane >= to) & (lane < to + 4), moved, lists)
    lists = lists.astype(jnp.bfloat16)
    for c in range(BLOCKS):
        out_ref[c, DATA:PIECE, :] = lists


def transform(x, source, partner, table):
    vmem = pl.BlockSpec(memory_space=pltpu.VMEM)
    return pl.pallas_call(
        transform_kernel,
        out_shape=jax.ShapeDtypeStruct((BLOCKS, PIECE, 128), jnp.bfloat16),
        in_specs=[vmem] * 4,
        out_specs=vmem,
        scratch_shapes=[
            pltpu.VMEM((2 * ROWS, QUARTER), jnp.bfloat16),
            pltpu.VMEM((2 * ROWS, QUARTER), jnp.bfloat16),
            pltpu.VMEM((12, ROWS, 128), jnp.float32),
            pltpu.VMEM((2, 12, ROWS, 128), jnp.float32),
            pltpu.VMEM((8, 128), jnp.float32),
        ],
        compiler_params=pltpu.CompilerParams(vmem_limit_bytes=20 * MB),
        cost_estimate=pl.CostEstimate(flops=2 * 4 * 2 * ROWS * QUARTER**2, bytes_accessed=2 * 10**6, transcendentals=0),
        name="transform",
    )(x, source, partner, table)


def cross_kernel(away, got_ref, out_ref, data_ref, near_ref, far_ref, list_ref):
    for o in range(BLOCKS):
        for q in range(6):
            rows = slice(CHANS * o, CHANS * (o + 1))
            data_ref[rows, 128 * q:128 * q + 128] = got_ref[SLOT[o], CHANS * q:CHANS * (q + 1), :]
    lists = got_ref[:, DATA:PIECE, :].astype(jnp.float32)
    list_ref[...] = jnp.zeros((2, 128, 128), jnp.float32)
    list_ref[0, 0:BLOCKS, :] = lists[:, 0, :] * CHANS + lists[:, 1, :]
    list_ref[1, 0:BLOCKS, :] = lists[:, 2, :]
    partner = jnp.transpose(list_ref[0])
    source = jnp.transpose(list_ref[1])
    list_ref[0], list_ref[1] = partner, source
    core = (lax.axis_index("core") + away) % 2
    pick = pl.ds(pl.multiple_of(HALF_PAIRS * core, HALF_PAIRS), HALF_PAIRS)
    partner, source = list_ref[0, pick, :], list_ref[1, pick, :]
    channel = iota((HALF_PAIRS, BLOCKS * CHANS), 1).astype(jnp.float32)
    for o in range(BLOCKS):
        at = SLOT[o]
        rows = slice(HALF_PAIRS * o, HALF_PAIRS * (o + 1))
        far_ref[rows, :] = jnp.where(channel == partner[:, at:at + 1], 1.0, 0.0).astype(jnp.bfloat16)
        near = channel[:, :256] == source[:, at:at + 1] + float(CHANS * (o % 16))
        near_ref[rows, :] = jnp.where(near, 1.0, 0.0).astype(jnp.bfloat16)

    size = 256
    lane = iota((size, 128), 1)
    for m in range(2):
        rows = slice(size * m, size * (m + 1))
        far = jnp.dot(far_ref[rows, :], data_ref[...], preferred_element_type=jnp.float32)
        near = jnp.dot(near_ref[rows, :], data_ref[rows, :], preferred_element_type=jnp.float32)
        tiles = []
        for t in range(3):
            re, im = slice(256 * t, 256 * t + 128), slice(256 * t + 128, 256 * t + 256)
            a_re, a_im, b_re, b_im = near[:, re], near[:, im], far[:, re], far[:, im]
            real = a_re * b_re + a_im * b_im
            imag = a_im * b_re - a_re * b_im
            low = lane < 64
            tiles.append(jnp.where(low, real, imag) + pltpu.roll(jnp.where(low, imag, real), 64, 1))
        low = lane // 32 % 2 == 0
        one = jnp.where(low, tiles[0] + pltpu.roll(tiles[0], 96, 1), tiles[1] + pltpu.roll(tiles[1], 32, 1))
        two = jnp.where(low, tiles[2] + pltpu.roll(tiles[2], 96, 1), 0.0)
        low = lane // 16 % 2 == 0
        packed = jnp.where(low, one + pltpu.roll(one, 112, 1), two + pltpu.roll(two, 16, 1))
        low = iota((8, 128), 0) < 4
        for o in range(0, 16, 2):
            slots = SLOT[16 * m + o], SLOT[16 * m + o + 1]
            for pair in range(2):
                one = packed[16 * o + 8 * pair:16 * o + 8 * pair + 8]
                two = packed[16 * o + 16 + 8 * pair:16 * o + 24 + 8 * pair]
                if slots[0] > slots[1]:
                    one, two = two, one
                for x, tile in (
                    (2 * pair, jnp.where(low, one, pltpu.roll(two, 4, 0))),
                    (2 * pair + 1, jnp.where(low, pltpu.roll(one, 4, 0), two)),
                ):
                    to = 4 * BLOCKS * ((x + 4 - lax.axis_index("x")) % 4) + 4 * min(slots)
                    out_ref[pl.ds(pl.multiple_of(to, 8), 8), :] = tile


def cross(got, away):
    vmem = pl.BlockSpec(memory_space=pltpu.VMEM)
    pairs = BLOCKS * HALF_PAIRS
    return pl.pallas_call(
        functools.partial(cross_kernel, away),
        out_shape=jax.ShapeDtypeStruct((pairs, 128), jnp.float32),
        in_specs=[vmem],
        out_specs=vmem,
        scratch_shapes=[
            pltpu.VMEM((BLOCKS * CHANS, 6 * 128), jnp.bfloat16),
            pltpu.VMEM((pairs, 256), jnp.bfloat16),
            pltpu.VMEM((pairs, BLOCKS * CHANS), jnp.bfloat16),
            pltpu.VMEM((2, 128, 128), jnp.float32),
        ],
        compiler_params=pltpu.CompilerParams(vmem_limit_bytes=16 * MB),
        cost_estimate=pl.CostEstimate(flops=2 * pairs * 768 * 768, bytes_accessed=2 * 10**6, transcendentals=0),
        name="cross",
    )(got)


def bin_of(block, lane):
    tile = 3 * (block // 8) + jnp.where(lane // 32 % 2 == 1, 1, jnp.where(lane // 16 % 2 == 1, 2, 0))
    place = 128 * tile + 16 * (block % 8) + lane % 16 + 1
    back = place - 768
    back = jnp.where(back == 768, 0, back)
    return jnp.where(tile < 6, place, HALF - back), lane // 16 % 4 != 3


def inverse_kernel(count_ref, after_ref, turn_ref, table_ref, first_ref, powers_ref):
    scale = 1.0 / math.sqrt(HALF * 64)
    b = iota((96, 128), 1)
    block, tile = iota((96, 128), 0) // 3, iota((96, 128), 0) % 3
    place = 128 * (3 * (block // 8) + tile) + 16 * (block % 8) + 1
    j0 = jnp.where(block < 16, place, HALF + 768 - place)
    first_ref[0], first_ref[1] = cos_sin((j0 * b).astype(jnp.float32))
    k = iota((16, 128), 0)
    cos_k, sin_k = cos_sin((k * iota((16, 128), 1)).astype(jnp.float32))
    nothing = jnp.zeros((16, 128), jnp.bfloat16)

    def put(at, value):
        coarse = value.astype(jnp.bfloat16)
        rows = pl.ds(pl.multiple_of(at, 16), 16)
        table_ref[rows, 0:128] = coarse
        table_ref[rows, 128:256] = (value - coarse.astype(jnp.float32)).astype(jnp.bfloat16)

    for back in range(2):
        way = -sin_k if back else sin_k

        @pl.loop(16 * back, 16 * back + 16, unroll=4)
        def _(c):
            for i, at in enumerate((0, 32, 16)):
                cos, sin = first_ref[0, pl.ds(3 * c + i, 1), :], first_ref[1, pl.ds(3 * c + i, 1), :]
                put(128 * c + at, cos * cos_k - sin * way)
                put(128 * c + 64 + at, -(sin * cos_k + cos * way))
            for at in (48, 112):
                rows = pl.ds(pl.multiple_of(128 * c + at, 16), 16)
                table_ref[rows, 0:128] = nothing
                table_ref[rows, 128:256] = nothing

    cos, sin = first_ref[0, 95:96, :], first_ref[1, 95:96, :]
    end = jnp.where(iota((16, 128), 1) % 2 == 0, 1.0, -1.0)
    put(128 * 31 + 16, jnp.where(k < 15, cos * cos_k + sin * sin_k, end))
    put(128 * 31 + 80, jnp.where(k < 15, -(sin * cos_k - cos * sin_k), 0.0))

    lane = iota((BLOCKS, 128), 1)
    j, used = bin_of(iota((BLOCKS, 128), 0), lane)
    factor = jnp.where(used, scale, 0.0)
    signed = jnp.where(lane < 64, -factor, factor)
    for a in range(5):
        cos, sin = cos_sin((128 * a * j).astype(jnp.float32))
        if a < 4:
            powers_ref[0, 4 + a] = cos * factor
            powers_ref[1, 4 + a] = sin * signed
        if a > 0:
            powers_ref[0, 4 - a] = cos * factor
            powers_ref[1, 4 - a] = -sin * signed
    row = iota((8, 128), 0)
    low = row < 4
    slot = 4 * (2 * lax.axis_index("x") + lax.axis_index("core")) + row % 4
    live = jnp.where(slot < count_ref[0], 1.0, 0.0)

    @pl.loop(0, BLOCKS, unroll=4)
    def _(c):
        row = pl.ds(c, 1)
        for part in range(2):
            for q in range(4):
                two = jnp.where(low, powers_ref[part, 2 * q, row, :], powers_ref[part, 2 * q + 1, row, :])
                turn_ref[part, pl.ds(pl.multiple_of(32 * c + 8 * q, 8), 8), :] = two * live


def inverse(count, after):
    vmem = pl.BlockSpec(memory_space=pltpu.VMEM)
    return pl.pallas_call(
        inverse_kernel,
        out_shape=(
            jax.ShapeDtypeStruct((2, 32 * BLOCKS, 128), jnp.float32),
            jax.ShapeDtypeStruct((128 * BLOCKS, 256), jnp.bfloat16),
        ),
        in_specs=[pl.BlockSpec(memory_space=pltpu.SMEM), pl.BlockSpec(memory_space=pl.ANY)],
        out_specs=(vmem, vmem),
        scratch_shapes=[pltpu.VMEM((2, 96, 128), jnp.float32), pltpu.VMEM((2, 8, BLOCKS, 128), jnp.float32)],
        compiler_params=pltpu.CompilerParams(vmem_limit_bytes=12 * MB),
        cost_estimate=pl.CostEstimate(flops=10 * 10**6, bytes_accessed=3 * 10**6, transcendentals=0),
        name="inverse",
    )(count, after)


def total_kernel(own_ref, one_ref, two_ref, three_ref, after_ref, out_ref):
    out_ref[...] = own_ref[...] + one_ref[...] + two_ref[...] + three_ref[...]


def add_parts(own, parts, after):
    vmem = pl.BlockSpec(memory_space=pltpu.VMEM)
    return pl.pallas_call(
        total_kernel,
        out_shape=jax.ShapeDtypeStruct(own.shape, jnp.float32),
        in_specs=[vmem] * 4 + [pl.BlockSpec(memory_space=pl.ANY)],
        out_specs=vmem,
        compiler_params=pltpu.CompilerParams(vmem_limit_bytes=4 * MB),
        cost_estimate=pl.CostEstimate(flops=10**5, bytes_accessed=3 * 10**5, transcendentals=0),
        name="total",
    )(own, *parts, after)


def lags_kernel(got_ref, turn_ref, table_ref, out_ref, left_ref):
    for c in range(BLOCKS):
        slot = SLOT[c]
        two = got_ref[8 * (slot // 2):8 * (slot // 2) + 8, :]
        low = iota((8, 128), 0) < 4
        turned = pltpu.roll(two, 4, 0)
        total = jnp.where(low, two, turned) if slot % 2 == 0 else jnp.where(low, turned, two)
        total = jnp.concatenate([total] * 4, axis=0)
        at = slice(32 * c, 32 * c + 32)
        turned = total * turn_ref[0, at, :] + pltpu.roll(total, 64, 1) * turn_ref[1, at, :]
        coarse = turned.astype(jnp.bfloat16)
        left_ref[0:32, 128 * c:128 * c + 128] = coarse
        left_ref[32:64, 128 * c:128 * c + 128] = (turned - coarse.astype(jnp.float32)).astype(jnp.bfloat16)
    both = jnp.dot(left_ref[...], table_ref[...], preferred_element_type=jnp.float32)
    both = both[:32] + both[32:]
    both = both[:, :128] + both[:, 128:]
    for a in range(8):
        out_ref[:, 128 * a:128 * a + 128] = both[4 * a:4 * a + 4, :]


def lags(got, turn, table):
    vmem = pl.BlockSpec(memory_space=pltpu.VMEM)
    return pl.pallas_call(
        lags_kernel,
        out_shape=jax.ShapeDtypeStruct((4, LAGS), jnp.float32),
        in_specs=[vmem] * 3,
        out_specs=vmem,
        scratch_shapes=[pltpu.VMEM((64, 128 * BLOCKS), jnp.bfloat16)],
        compiler_params=pltpu.CompilerParams(vmem_limit_bytes=16 * MB),
        cost_estimate=pl.CostEstimate(flops=2 * 64 * 4096 * 256, bytes_accessed=4 * 10**6, transcendentals=0),
        name="lags",
    )(got, turn, table)


def shards(records, pair_source, pair_partner, pair_count):
    sent = transform(records.reshape(ROWS, N), pair_source, pair_partner, tables())
    got = lax.all_to_all(sent, "chan", 0, 0, axis_index_groups=[ORDER])
    away = cross(got, 1)
    near = lax.ppermute(away, "core", [(0, 1), (1, 0)])
    spectra = (cross(got, 0) + near).reshape(4, 4 * BLOCKS, 128)
    parts = [lax.ppermute(spectra[k], "x", [(x, (x + k) % 4) for x in range(4)]) for k in (1, 2, 3)]
    turn, table = inverse(pair_count, spectra)
    total = add_parts(spectra[0], parts, turn)
    last = lax.all_to_all(total.reshape(BLOCKS, 4, 128), "chan", 0, 0, axis_index_groups=[ORDER])
    return lags(last.reshape(4 * BLOCKS, 128), turn, table)


def solution(mesh):
    chips = Mesh(mesh.devices.reshape(BLOCKS, WINS // 2, 2), ("chan", "x", "core"))
    placed = (P("chan", ("x", "core"), None), P("chan", None), P("chan", None), P("chan"))
    return jax.shard_map(
        shards, mesh=chips, in_specs=placed, out_specs=P(("chan", "x", "core"), None), check_vma=False
    )
```

```python
import functools
import math

import jax
import jax.numpy as jnp
from jax import lax
from jax.experimental import pallas as pl
from jax.experimental.pallas import tpu as pltpu
from jax.sharding import Mesh
from jax.sharding import PartitionSpec as P

N = 3072
HALF = N // 2
BAND = 128
LAGS = 1024
QUARTER = N // 4
CHANS, WINS = 16, 8
ROWS = CHANS * WINS
BLOCKS = 32
PAIRS = 32
HALF_PAIRS = PAIRS // 2
DATA = 6 * CHANS
PIECE = DATA + 8
MB = 1024 * 1024


def cos_sin(phase):
    turn = jnp.floor(phase * (1.0 / QUARTER) + 0.5)
    t = (phase - QUARTER * turn) * (2.0 * math.pi / N)
    quadrant = turn - 4.0 * jnp.floor(turn * 0.25)
    u = t * t
    s = t * (1.0 + u * (-1 / 6 + u * (1 / 120 + u * (-1 / 5040 + u * (1 / 362880)))))
    c = 1.0 + u * (-1 / 2 + u * (1 / 24 + u * (-1 / 720 + u * (1 / 40320))))
    odd = (quadrant == 1.0) | (quadrant == 3.0)
    cos = jnp.where(odd, s, c)
    sin = jnp.where(odd, c, s)
    cos = jnp.where((quadrant == 1.0) | (quadrant == 2.0), -cos, cos)
    sin = jnp.where(quadrant >= 2.0, -sin, sin)
    return cos, sin


def iota(shape, axis):
    return lax.broadcasted_iota(jnp.int32, shape, axis)


ORDER = list(range(BLOCKS))[::-1]
SLOT = [ORDER.index(block) for block in range(BLOCKS)]


def tables_kernel(table_ref, base_ref, step_ref):
    bins = (iota((16, QUARTER), 1) + 1).astype(jnp.float32)
    row = iota((16, QUARTER), 0).astype(jnp.float32)
    base_ref[0], base_ref[1] = cos_sin((2.0 * row + 2.0) * bins)
    base_ref[2], base_ref[3] = cos_sin((2.0 * row + 1.0) * bins)
    for a in range(3):
        cos, sin = cos_sin(32.0 * (row + 16.0 * a) * bins)
        step_ref[0, 16 * a:16 * a + 16, :] = cos
        step_ref[1, 16 * a:16 * a + 16, :] = sin

    @pl.loop(0, 48)
    def _(a):
        cos = step_ref[0, pl.ds(a, 1), :]
        sin = step_ref[1, pl.ds(a, 1), :]
        rows = pl.ds(pl.multiple_of(16 * a, 16), 16)
        base_cos, base_sin = base_ref[0], base_ref[1]
        table_ref[0, rows, :] = (base_cos * cos - base_sin * sin).astype(jnp.bfloat16)
        table_ref[1, rows, :] = (base_sin * cos + base_cos * sin).astype(jnp.bfloat16)


def tables():
    vmem = pl.BlockSpec(memory_space=pltpu.VMEM)
    return pl.pallas_call(
        tables_kernel,
        out_shape=(
            jax.ShapeDtypeStruct((2, QUARTER, QUARTER), jnp.bfloat16),
            jax.ShapeDtypeStruct((4, 16, QUARTER), jnp.float32),
            jax.ShapeDtypeStruct((2, 48, QUARTER), jnp.float32),
        ),
        out_specs=(vmem,) * 3,
        compiler_params=pltpu.CompilerParams(vmem_limit_bytes=12 * MB),
        cost_estimate=pl.CostEstimate(flops=10**9, bytes_accessed=10**7, transcendentals=0),
        name="tables",
    )()


def transform_kernel(x_ref, source_ref, partner_ref, even_table_ref, base_ref, step_ref, out_ref,
                     odd_table_ref, even_ref, odd_ref, power_ref, white_ref, list_ref):
    lane = iota((ROWS, 128), 1)
    i = iota((256, 256), 0)
    k = iota((256, 256), 1)
    low = k < 128
    k = jnp.where(low, k, k - 128)
    ahead = jnp.where(low, 2 * ((k + 1) % 128), 2 * k + 1)
    back = jnp.where(low, 2 * (127 - k), 2 * (127 - k) + 1)
    ahead = jnp.where(i == ahead, 1.0, 0.0).astype(jnp.bfloat16)
    back = jnp.where(i == back, 1.0, 0.0).astype(jnp.bfloat16)
    rotated = []
    for t in range(6):
        part = jnp.dot(x_ref[:, 256 * t:256 * t + 256], ahead, preferred_element_type=jnp.float32)
        rotated.append(part[:, :128])
        odd_ref[0:ROWS, 128 * t:128 * t + 128] = part[:, 128:].astype(jnp.bfloat16)
        at = 256 * (11 - t)
        part = jnp.dot(x_ref[:, at:at + 256], back, preferred_element_type=jnp.float32)
        even_ref[ROWS:2 * ROWS, 128 * t:128 * t + 128] = part[:, :128].astype(jnp.bfloat16)
        odd_ref[ROWS:2 * ROWS, 128 * t:128 * t + 128] = part[:, 128:].astype(jnp.bfloat16)
    for t in range(6):
        following = rotated[t + 1] if t < 5 else 0.0
        even_ref[0:ROWS, 128 * t:128 * t + 128] = jnp.where(lane < 127, rotated[t], following).astype(jnp.bfloat16)
    first = jnp.sum(jnp.where(lane == 127, rotated[0], 0.0), axis=1, keepdims=True)

    last = jnp.zeros((ROWS, 128), jnp.float32)
    for t in range(24):
        last = last + x_ref[:, 128 * t:128 * t + 128].astype(jnp.float32)
    last = jnp.sum(jnp.where(lane % 2 == 0, last, -last), axis=1, keepdims=True)

    for a in range(48):
        cos, sin = step_ref[0, a:a + 1, :], step_ref[1, a:a + 1, :]
        base_cos, base_sin = base_ref[2], base_ref[3]
        odd_table_ref[0, 16 * a:16 * a + 16, :] = (base_cos * cos - base_sin * sin).astype(jnp.bfloat16)
        odd_table_ref[1, 16 * a:16 * a + 16, :] = (base_sin * cos + base_cos * sin).astype(jnp.bfloat16)

    for u in range(3):
        wide = slice(256 * u, 256 * u + 256)
        even_cos, even_sin, odd_cos, odd_sin = (
            jnp.dot(samples[...], table[which, :, wide], preferred_element_type=jnp.float32)
            for samples, table in ((even_ref, even_table_ref), (odd_ref, odd_table_ref))
            for which in range(2)
        )
        even_cos = even_cos[:ROWS] + even_cos[ROWS:] + first
        even_sin = even_sin[:ROWS] - even_sin[ROWS:]
        odd_cos = odd_cos[:ROWS] + odd_cos[ROWS:]
        odd_sin = odd_sin[:ROWS] - odd_sin[ROWS:]
        for t in (2 * u, 2 * u + 1):
            at = slice(128 * (t % 2), 128 * (t % 2) + 128)
            real, imag = even_cos[:, at] + odd_cos[:, at], -(even_sin[:, at] + odd_sin[:, at])
            real_back, imag_back = even_cos[:, at] - odd_cos[:, at], even_sin[:, at] - odd_sin[:, at]
            if t == 5:
                real_back = jnp.where(lane < 127, real_back, last)
                imag_back = jnp.where(lane < 127, imag_back, 0.0)
            white_ref[0, t], white_ref[1, t] = real, imag
            white_ref[0, 6 + t], white_ref[1, 6 + t] = real_back, imag_back
            power_ref[t] = real * real + imag * imag
            power_ref[6 + t] = real_back * real_back + imag_back * imag_back
    factor = []
    for t in range(12):
        power = power_ref[t]
        if t >= 6:
            power = jnp.where(lane < 127, power, power_ref[6 + (t - 7) % 6])
        mean = jnp.sum(power, axis=1, keepdims=True) * (1.0 / BAND)
        factor.append(lax.rsqrt(mean + 1e-06))

    segment = iota((CHANS, 128), 1) // 16
    for t in range(12):
        scale = factor[t]
        if t >= 6:
            scale = jnp.where(lane < 127, scale, factor[6 + (t - 5) % 6])
        for part in range(2):
            white_ref[part, t] = white_ref[part, t] * scale
            slabs = [
                white_ref[part, t, pl.ds(w, CHANS, stride=WINS), :].astype(jnp.bfloat16) for w in range(WINS)
            ]
            for bit in range(3):
                step = 1 << bit
                high = (segment // step) % 2 == 1
                mixed = [None] * WINS
                for w in range(WINS):
                    if w & step:
                        continue
                    one, two = slabs[w], slabs[w + step]
                    mixed[w] = jnp.where(high, pltpu.roll(two, 16 * step, 1), one)
                    mixed[w + step] = jnp.where(high, two, pltpu.roll(one, 128 - 16 * step, 1))
                slabs = mixed
            at = CHANS * (2 * (t % 3) + part)
            for s in range(8):
                out_ref[SLOT[8 * (t // 3) + s], at:at + CHANS, :] = slabs[s]

    partner = partner_ref[...]
    list_ref[...] = jnp.zeros((8, 128), jnp.float32)
    list_ref[0:1, 0:PAIRS] = (partner // CHANS).astype(jnp.float32)
    list_ref[1:2, 0:PAIRS] = (partner % CHANS).astype(jnp.float32)
    list_ref[2:3, 0:PAIRS] = source_ref[...].astype(jnp.float32)
    plain = list_ref[...]
    lane = iota((8, 128), 1)
    lists = jnp.zeros((8, 128), jnp.float32)
    for quad in range(8):
        at, to = 4 * quad, 16 * (quad % 2) + 4 * (quad // 2)
        moved = pltpu.roll(plain, (to - at) % 128, 1)
        lists = jnp.where((lane >= to) & (lane < to + 4), moved, lists)
    lists = lists.astype(jnp.bfloat16)
    for c in range(BLOCKS):
        out_ref[c, DATA:PIECE, :] = lists


def transform(x, source, partner, table):
    vmem = pl.BlockSpec(memory_space=pltpu.VMEM)
    return pl.pallas_call(
        transform_kernel,
        out_shape=jax.ShapeDtypeStruct((BLOCKS, PIECE, 128), jnp.bfloat16),
        in_specs=[vmem] * 6,
        out_specs=vmem,
        scratch_shapes=[
            pltpu.VMEM((2, QUARTER, QUARTER), jnp.bfloat16),
            pltpu.VMEM((2 * ROWS, QUARTER), jnp.bfloat16),
            pltpu.VMEM((2 * ROWS, QUARTER), jnp.bfloat16),
            pltpu.VMEM((12, ROWS, 128), jnp.float32),
            pltpu.VMEM((2, 12, ROWS, 128), jnp.float32),
            pltpu.VMEM((8, 128), jnp.float32),
        ],
        compiler_params=pltpu.CompilerParams(vmem_limit_bytes=20 * MB),
        cost_estimate=pl.CostEstimate(flops=2 * 4 * 2 * ROWS * QUARTER**2, bytes_accessed=2 * 10**6, transcendentals=0),
        name="transform",
    )(x, source, partner, *table)


def cross_kernel(away, got_ref, out_ref, data_ref, near_ref, far_ref, list_ref):
    for o in range(BLOCKS):
        for q in range(6):
            rows = slice(CHANS * o, CHANS * (o + 1))
            data_ref[rows, 128 * q:128 * q + 128] = got_ref[SLOT[o], CHANS * q:CHANS * (q + 1), :]
    lists = got_ref[:, DATA:PIECE, :].astype(jnp.float32)
    list_ref[...] = jnp.zeros((2, 128, 128), jnp.float32)
    list_ref[0, 0:BLOCKS, :] = lists[:, 0, :] * CHANS + lists[:, 1, :]
    list_ref[1, 0:BLOCKS, :] = lists[:, 2, :]
    partner = jnp.transpose(list_ref[0])
    source = jnp.transpose(list_ref[1])
    list_ref[0], list_ref[1] = partner, source
    core = (lax.axis_index("core") + away) % 2
    pick = pl.ds(pl.multiple_of(HALF_PAIRS * core, HALF_PAIRS), HALF_PAIRS)
    partner, source = list_ref[0, pick, :], list_ref[1, pick, :]
    channel = iota((HALF_PAIRS, BLOCKS * CHANS), 1).astype(jnp.float32)
    size = 256
    lane = iota((size, 128), 1)
    for m in range(2):
        for o in range(16 * m, 16 * m + 16):
            at = SLOT[o]
            rows = slice(HALF_PAIRS * o, HALF_PAIRS * (o + 1))
            far_ref[rows, :] = jnp.where(channel == partner[:, at:at + 1], 1.0, 0.0).astype(jnp.bfloat16)
            near = channel[:, :256] == source[:, at:at + 1] + float(CHANS * (o % 16))
            near_ref[rows, :] = jnp.where(near, 1.0, 0.0).astype(jnp.bfloat16)
        rows = slice(size * m, size * (m + 1))
        tiles = []
        low = lane < 64
        for t in range(3):
            at = slice(256 * t, 256 * t + 256)
            far = jnp.dot(far_ref[rows, :], data_ref[:, at], preferred_element_type=jnp.float32)
            near = jnp.dot(near_ref[rows, :], data_ref[rows, at], preferred_element_type=jnp.float32)
            a_re, a_im, b_re, b_im = near[:, :128], near[:, 128:], far[:, :128], far[:, 128:]
            real = a_re * b_re + a_im * b_im
            imag = a_im * b_re - a_re * b_im
            tiles.append(jnp.where(low, real, imag) + pltpu.roll(jnp.where(low, imag, real), 64, 1))
        low = lane // 32 % 2 == 0
        one = jnp.where(low, tiles[0] + pltpu.roll(tiles[0], 96, 1), tiles[1] + pltpu.roll(tiles[1], 32, 1))
        two = jnp.where(low, tiles[2] + pltpu.roll(tiles[2], 96, 1), 0.0)
        low = lane // 16 % 2 == 0
        packed = jnp.where(low, one + pltpu.roll(one, 112, 1), two + pltpu.roll(two, 16, 1))
        low = iota((8, 128), 0) < 4
        for o in range(0, 16, 2):
            slots = SLOT[16 * m + o], SLOT[16 * m + o + 1]
            for pair in range(2):
                one = packed[16 * o + 8 * pair:16 * o + 8 * pair + 8]
                two = packed[16 * o + 16 + 8 * pair:16 * o + 24 + 8 * pair]
                if slots[0] > slots[1]:
                    one, two = two, one
                for x, tile in (
                    (2 * pair, jnp.where(low, one, pltpu.roll(two, 4, 0))),
                    (2 * pair + 1, jnp.where(low, pltpu.roll(one, 4, 0), two)),
                ):
                    to = 4 * BLOCKS * ((x + 4 - lax.axis_index("x")) % 4) + 4 * min(slots)
                    out_ref[pl.ds(pl.multiple_of(to, 8), 8), :] = tile


def cross(got, away):
    vmem = pl.BlockSpec(memory_space=pltpu.VMEM)
    pairs = BLOCKS * HALF_PAIRS
    return pl.pallas_call(
        functools.partial(cross_kernel, away),
        out_shape=jax.ShapeDtypeStruct((pairs, 128), jnp.float32),
        in_specs=[vmem],
        out_specs=vmem,
        scratch_shapes=[
            pltpu.VMEM((BLOCKS * CHANS, 6 * 128), jnp.bfloat16),
            pltpu.VMEM((pairs, 256), jnp.bfloat16),
            pltpu.VMEM((pairs, BLOCKS * CHANS), jnp.bfloat16),
            pltpu.VMEM((2, 128, 128), jnp.float32),
        ],
        compiler_params=pltpu.CompilerParams(vmem_limit_bytes=16 * MB),
        cost_estimate=pl.CostEstimate(flops=2 * pairs * 768 * 768, bytes_accessed=2 * 10**6, transcendentals=0),
        name="cross",
    )(got)


def bin_of(block, lane):
    tile = 3 * (block // 8) + jnp.where(lane // 32 % 2 == 1, 1, jnp.where(lane // 16 % 2 == 1, 2, 0))
    place = 128 * tile + 16 * (block % 8) + lane % 16 + 1
    back = place - 768
    back = jnp.where(back == 768, 0, back)
    return jnp.where(tile < 6, place, HALF - back), lane // 16 % 4 != 3


def inverse_kernel(count_ref, after_ref, turn_ref, table_ref, first_ref, powers_ref):
    scale = 1.0 / math.sqrt(HALF * 64)
    b = iota((96, 128), 1)
    block, tile = iota((96, 128), 0) // 3, iota((96, 128), 0) % 3
    place = 128 * (3 * (block // 8) + tile) + 16 * (block % 8) + 1
    j0 = jnp.where(block < 16, place, HALF + 768 - place)
    first_ref[0], first_ref[1] = cos_sin((j0 * b).astype(jnp.float32))
    k = iota((16, 128), 0)
    cos_k, sin_k = cos_sin((k * iota((16, 128), 1)).astype(jnp.float32))
    nothing = jnp.zeros((16, 128), jnp.bfloat16)

    def put(at, value):
        coarse = value.astype(jnp.bfloat16)
        rows = pl.ds(pl.multiple_of(at, 16), 16)
        table_ref[rows, 0:128] = coarse
        table_ref[rows, 128:256] = (value - coarse.astype(jnp.float32)).astype(jnp.bfloat16)

    for back in range(2):
        way = -sin_k if back else sin_k

        @pl.loop(16 * back, 16 * back + 16, unroll=4)
        def _(c):
            for i, at in enumerate((0, 32, 16)):
                cos, sin = first_ref[0, pl.ds(3 * c + i, 1), :], first_ref[1, pl.ds(3 * c + i, 1), :]
                put(128 * c + at, cos * cos_k - sin * way)
                put(128 * c + 64 + at, -(sin * cos_k + cos * way))
            for at in (48, 112):
                rows = pl.ds(pl.multiple_of(128 * c + at, 16), 16)
                table_ref[rows, 0:128] = nothing
                table_ref[rows, 128:256] = nothing

    cos, sin = first_ref[0, 95:96, :], first_ref[1, 95:96, :]
    end = jnp.where(iota((16, 128), 1) % 2 == 0, 1.0, -1.0)
    put(128 * 31 + 16, jnp.where(k < 15, cos * cos_k + sin * sin_k, end))
    put(128 * 31 + 80, jnp.where(k < 15, -(sin * cos_k - cos * sin_k), 0.0))

    lane = iota((BLOCKS, 128), 1)
    j, used = bin_of(iota((BLOCKS, 128), 0), lane)
    factor = jnp.where(used, scale, 0.0)
    signed = jnp.where(lane < 64, -factor, factor)
    for a in range(5):
        cos, sin = cos_sin((128 * a * j).astype(jnp.float32))
        if a < 4:
            powers_ref[0, 4 + a] = cos * factor
            powers_ref[1, 4 + a] = sin * signed
        if a > 0:
            powers_ref[0, 4 - a] = cos * factor
            powers_ref[1, 4 - a] = -sin * signed
    row = iota((8, 128), 0)
    low = row < 4
    slot = 4 * (2 * lax.axis_index("x") + lax.axis_index("core")) + row % 4
    live = jnp.where(slot < count_ref[0], 1.0, 0.0)

    @pl.loop(0, BLOCKS, unroll=4)
    def _(c):
        row = pl.ds(c, 1)
        for part in range(2):
            for q in range(4):
                two = jnp.where(low, powers_ref[part, 2 * q, row, :], powers_ref[part, 2 * q + 1, row, :])
                turn_ref[part, pl.ds(pl.multiple_of(32 * c + 8 * q, 8), 8), :] = two * live


def inverse(count, after):
    vmem = pl.BlockSpec(memory_space=pltpu.VMEM)
    return pl.pallas_call(
        inverse_kernel,
        out_shape=(
            jax.ShapeDtypeStruct((2, 32 * BLOCKS, 128), jnp.float32),
            jax.ShapeDtypeStruct((128 * BLOCKS, 256), jnp.bfloat16),
        ),
        in_specs=[pl.BlockSpec(memory_space=pltpu.SMEM), pl.BlockSpec(memory_space=pl.ANY)],
        out_specs=(vmem, vmem),
        scratch_shapes=[pltpu.VMEM((2, 96, 128), jnp.float32), pltpu.VMEM((2, 8, BLOCKS, 128), jnp.float32)],
        compiler_params=pltpu.CompilerParams(vmem_limit_bytes=12 * MB),
        cost_estimate=pl.CostEstimate(flops=10 * 10**6, bytes_accessed=3 * 10**6, transcendentals=0),
        name="inverse",
    )(count, after)


def total_kernel(own_ref, one_ref, two_ref, three_ref, after_ref, out_ref):
    out_ref[...] = own_ref[...] + one_ref[...] + two_ref[...] + three_ref[...]


def add_parts(own, parts, after):
    vmem = pl.BlockSpec(memory_space=pltpu.VMEM)
    return pl.pallas_call(
        total_kernel,
        out_shape=jax.ShapeDtypeStruct(own.shape, jnp.float32),
        in_specs=[vmem] * 4 + [pl.BlockSpec(memory_space=pl.ANY)],
        out_specs=vmem,
        compiler_params=pltpu.CompilerParams(vmem_limit_bytes=4 * MB),
        cost_estimate=pl.CostEstimate(flops=10**5, bytes_accessed=3 * 10**5, transcendentals=0),
        name="total",
    )(own, *parts, after)


def lags_kernel(got_ref, turn_ref, table_ref, out_ref, left_ref):
    for c in range(BLOCKS):
        slot = SLOT[c]
        two = got_ref[8 * (slot // 2):8 * (slot // 2) + 8, :]
        low = iota((8, 128), 0) < 4
        turned = pltpu.roll(two, 4, 0)
        total = jnp.where(low, two, turned) if slot % 2 == 0 else jnp.where(low, turned, two)
        total = jnp.concatenate([total] * 4, axis=0)
        at = slice(32 * c, 32 * c + 32)
        turned = total * turn_ref[0, at, :] + pltpu.roll(total, 64, 1) * turn_ref[1, at, :]
        coarse = turned.astype(jnp.bfloat16)
        left_ref[0:32, 128 * c:128 * c + 128] = coarse
        left_ref[32:64, 128 * c:128 * c + 128] = (turned - coarse.astype(jnp.float32)).astype(jnp.bfloat16)
    both = jnp.dot(left_ref[...], table_ref[...], preferred_element_type=jnp.float32)
    both = both[:32] + both[32:]
    both = both[:, :128] + both[:, 128:]
    for a in range(8):
        out_ref[:, 128 * a:128 * a + 128] = both[4 * a:4 * a + 4, :]


def lags(got, turn, table):
    vmem = pl.BlockSpec(memory_space=pltpu.VMEM)
    return pl.pallas_call(
        lags_kernel,
        out_shape=jax.ShapeDtypeStruct((4, LAGS), jnp.float32),
        in_specs=[vmem] * 3,
        out_specs=vmem,
        scratch_shapes=[pltpu.VMEM((64, 128 * BLOCKS), jnp.bfloat16)],
        compiler_params=pltpu.CompilerParams(vmem_limit_bytes=16 * MB),
        cost_estimate=pl.CostEstimate(flops=2 * 64 * 4096 * 256, bytes_accessed=4 * 10**6, transcendentals=0),
        name="lags",
    )(got, turn, table)


def shards(records, pair_source, pair_partner, pair_count):
    sent = transform(records.reshape(ROWS, N), pair_source, pair_partner, tables())
    got = lax.all_to_all(sent, "chan", 0, 0, axis_index_groups=[ORDER])
    away = cross(got, 1)
    near = lax.ppermute(away, "core", [(0, 1), (1, 0)])
    spectra = (cross(got, 0) + near).reshape(4, 4 * BLOCKS, 128)
    parts = [lax.ppermute(spectra[k], "x", [(x, (x + k) % 4) for x in range(4)]) for k in (1, 3, 2)]
    turn, table = inverse(pair_count, spectra)
    total = add_parts(spectra[0], parts, turn)
    last = lax.all_to_all(total.reshape(BLOCKS, 4, 128), "chan", 0, 0, axis_index_groups=[ORDER])
    return lags(last.reshape(4 * BLOCKS, 128), turn, table)


def solution(mesh):
    chips = Mesh(mesh.devices.reshape(BLOCKS, WINS // 2, 2), ("chan", "x", "core"))
    placed = (P("chan", ("x", "core"), None), P("chan", None), P("chan", None), P("chan"))
    return jax.shard_map(
        shards, mesh=chips, in_specs=placed, out_specs=P(("chan", "x", "core"), None), check_vma=False
    )
```

```python
import math

import jax
import jax.numpy as jnp
from jax import lax
from jax.experimental import pallas as pl
from jax.experimental.pallas import tpu as pltpu
from jax.sharding import Mesh
from jax.sharding import PartitionSpec as P

N = 3072
HALF = N // 2
BAND = 128
LAGS = 1024
QUARTER = N // 4
CHANS, WINS = 16, 8
ROWS = CHANS * WINS
BLOCKS = 32
PAIRS = 32
HALF_PAIRS = PAIRS // 2
DATA = 6 * CHANS
PIECE = DATA + 2
MB = 1024 * 1024


def cos_sin(phase):
    turn = jnp.floor(phase * (1.0 / QUARTER) + 0.5)
    t = (phase - QUARTER * turn) * (2.0 * math.pi / N)
    quadrant = turn - 4.0 * jnp.floor(turn * 0.25)
    u = t * t
    s = t * (1.0 + u * (-1 / 6 + u * (1 / 120 + u * (-1 / 5040 + u * (1 / 362880)))))
    c = 1.0 + u * (-1 / 2 + u * (1 / 24 + u * (-1 / 720 + u * (1 / 40320))))
    odd = (quadrant == 1.0) | (quadrant == 3.0)
    cos = jnp.where(odd, s, c)
    sin = jnp.where(odd, c, s)
    cos = jnp.where((quadrant == 1.0) | (quadrant == 2.0), -cos, cos)
    sin = jnp.where(quadrant >= 2.0, -sin, sin)
    return cos, sin


def iota(shape, axis):
    return lax.broadcasted_iota(jnp.int32, shape, axis)


ORDER = list(range(BLOCKS))[::-1]
SLOT = [ORDER.index(block) for block in range(BLOCKS)]


def tables_kernel(table_ref, base_ref, step_ref):
    bins = (iota((16, QUARTER), 1) + 1).astype(jnp.float32)
    row = iota((16, QUARTER), 0).astype(jnp.float32)
    base_ref[0], base_ref[1] = cos_sin((2.0 * row + 2.0) * bins)
    base_ref[2], base_ref[3] = cos_sin((2.0 * row + 1.0) * bins)
    for a in range(3):
        cos, sin = cos_sin(32.0 * (row + 16.0 * a) * bins)
        step_ref[0, 16 * a:16 * a + 16, :] = cos
        step_ref[1, 16 * a:16 * a + 16, :] = sin

    @pl.loop(0, 48)
    def _(a):
        cos = step_ref[0, pl.ds(a, 1), :]
        sin = step_ref[1, pl.ds(a, 1), :]
        rows = pl.ds(pl.multiple_of(16 * a, 16), 16)
        base_cos, base_sin = base_ref[0], base_ref[1]
        table_ref[0, rows, :] = (base_cos * cos - base_sin * sin).astype(jnp.bfloat16)
        table_ref[1, rows, :] = (base_sin * cos + base_cos * sin).astype(jnp.bfloat16)


def tables():
    vmem = pl.BlockSpec(memory_space=pltpu.VMEM)
    return pl.pallas_call(
        tables_kernel,
        out_shape=(
            jax.ShapeDtypeStruct((2, QUARTER, QUARTER), jnp.bfloat16),
            jax.ShapeDtypeStruct((4, 16, QUARTER), jnp.float32),
            jax.ShapeDtypeStruct((2, 48, QUARTER), jnp.float32),
        ),
        out_specs=(vmem,) * 3,
        compiler_params=pltpu.CompilerParams(vmem_limit_bytes=12 * MB),
        cost_estimate=pl.CostEstimate(flops=10**9, bytes_accessed=10**7, transcendentals=0),
        name="tables",
    )()


def transform_kernel(x_ref, source_ref, partner_ref, even_table_ref, base_ref, step_ref, out_ref,
                     odd_table_ref, even_ref, odd_ref, power_ref, white_ref, list_ref):
    lane = iota((ROWS, 128), 1)
    i = iota((256, 256), 0)
    k = iota((256, 256), 1)
    low = k < 128
    k = jnp.where(low, k, k - 128)
    ahead = jnp.where(low, 2 * ((k + 1) % 128), 2 * k + 1)
    back = jnp.where(low, 2 * (127 - k), 2 * (127 - k) + 1)
    ahead = jnp.where(i == ahead, 1.0, 0.0).astype(jnp.bfloat16)
    back = jnp.where(i == back, 1.0, 0.0).astype(jnp.bfloat16)
    rotated = []
    for t in range(6):
        part = jnp.dot(x_ref[:, 256 * t:256 * t + 256], ahead, preferred_element_type=jnp.float32)
        rotated.append(part[:, :128])
        odd_ref[0:ROWS, 128 * t:128 * t + 128] = part[:, 128:].astype(jnp.bfloat16)
        at = 256 * (11 - t)
        part = jnp.dot(x_ref[:, at:at + 256], back, preferred_element_type=jnp.float32)
        even_ref[ROWS:2 * ROWS, 128 * t:128 * t + 128] = part[:, :128].astype(jnp.bfloat16)
        odd_ref[ROWS:2 * ROWS, 128 * t:128 * t + 128] = part[:, 128:].astype(jnp.bfloat16)
    for t in range(6):
        following = rotated[t + 1] if t < 5 else 0.0
        even_ref[0:ROWS, 128 * t:128 * t + 128] = jnp.where(lane < 127, rotated[t], following).astype(jnp.bfloat16)
    first = jnp.sum(jnp.where(lane == 127, rotated[0], 0.0), axis=1, keepdims=True)

    last = jnp.zeros((ROWS, 128), jnp.float32)
    for t in range(24):
        last = last + x_ref[:, 128 * t:128 * t + 128].astype(jnp.float32)
    last = jnp.sum(jnp.where(lane % 2 == 0, last, -last), axis=1, keepdims=True)

    for a in range(48):
        cos, sin = step_ref[0, a:a + 1, :], step_ref[1, a:a + 1, :]
        base_cos, base_sin = base_ref[2], base_ref[3]
        odd_table_ref[0, 16 * a:16 * a + 16, :] = (base_cos * cos - base_sin * sin).astype(jnp.bfloat16)
        odd_table_ref[1, 16 * a:16 * a + 16, :] = (base_sin * cos + base_cos * sin).astype(jnp.bfloat16)

    for u in range(3):
        wide = slice(256 * u, 256 * u + 256)
        even_cos, even_sin, odd_cos, odd_sin = (
            jnp.dot(samples[...], table[which, :, wide], preferred_element_type=jnp.float32)
            for samples, table in ((even_ref, even_table_ref), (odd_ref, odd_table_ref))
            for which in range(2)
        )
        even_cos = even_cos[:ROWS] + even_cos[ROWS:] + first
        even_sin = even_sin[:ROWS] - even_sin[ROWS:]
        odd_cos = odd_cos[:ROWS] + odd_cos[ROWS:]
        odd_sin = odd_sin[:ROWS] - odd_sin[ROWS:]
        for t in (2 * u, 2 * u + 1):
            at = slice(128 * (t % 2), 128 * (t % 2) + 128)
            real, imag = even_cos[:, at] + odd_cos[:, at], -(even_sin[:, at] + odd_sin[:, at])
            real_back, imag_back = even_cos[:, at] - odd_cos[:, at], even_sin[:, at] - odd_sin[:, at]
            if t == 5:
                real_back = jnp.where(lane < 127, real_back, last)
                imag_back = jnp.where(lane < 127, imag_back, 0.0)
            white_ref[0, t], white_ref[1, t] = real, imag
            white_ref[0, 6 + t], white_ref[1, 6 + t] = real_back, imag_back
            power_ref[t] = real * real + imag * imag
            power_ref[6 + t] = real_back * real_back + imag_back * imag_back
    factor = []
    for t in range(12):
        power = power_ref[t]
        if t >= 6:
            power = jnp.where(lane < 127, power, power_ref[6 + (t - 7) % 6])
        mean = jnp.sum(power, axis=1, keepdims=True) * (1.0 / BAND)
        factor.append(lax.rsqrt(mean + 1e-06))

    segment = iota((CHANS, 128), 1) // 16
    for t in range(12):
        scale = factor[t]
        if t >= 6:
            scale = jnp.where(lane < 127, scale, factor[6 + (t - 5) % 6])
        for part in range(2):
            white_ref[part, t] = white_ref[part, t] * scale
            slabs = [
                white_ref[part, t, pl.ds(w, CHANS, stride=WINS), :].astype(jnp.bfloat16) for w in range(WINS)
            ]
            for bit in range(3):
                step = 1 << bit
                high = (segment // step) % 2 == 1
                mixed = [None] * WINS
                for w in range(WINS):
                    if w & step:
                        continue
                    one, two = slabs[w], slabs[w + step]
                    mixed[w] = jnp.where(high, pltpu.roll(two, 16 * step, 1), one)
                    mixed[w + step] = jnp.where(high, two, pltpu.roll(one, 128 - 16 * step, 1))
                slabs = mixed
            at = CHANS * (2 * (t % 3) + part)
            for s in range(8):
                row = PIECE * SLOT[8 * (t // 3) + s] + at
                out_ref[row:row + CHANS, :] = slabs[s]

    partner = partner_ref[...]
    list_ref[...] = jnp.zeros((8, 128), jnp.float32)
    list_ref[0:1, 0:PAIRS] = (partner // CHANS).astype(jnp.float32)
    list_ref[1:2, 0:PAIRS] = (partner % CHANS).astype(jnp.float32)
    list_ref[2:3, 0:PAIRS] = source_ref[...].astype(jnp.float32)
    plain = list_ref[...]
    lane = iota((8, 128), 1)
    lists = jnp.zeros((8, 128), jnp.float32)
    for quad in range(8):
        at, to = 4 * quad, 16 * (quad % 2) + 4 * (quad // 2)
        moved = pltpu.roll(plain, (to - at) % 128, 1)
        lists = jnp.where((lane >= to) & (lane < to + 4), moved, lists)
    sources = pltpu.roll(pltpu.roll(lists, 6, 0), 64, 1)
    lists = jnp.where((iota((8, 128), 0) == 0) & (lane >= 64), sources, lists).astype(jnp.bfloat16)
    for c in range(BLOCKS):
        out_ref[PIECE * c + DATA:PIECE * (c + 1), :] = lists[:2]


def transform(x, source, partner, table):
    vmem = pl.BlockSpec(memory_space=pltpu.VMEM)
    return pl.pallas_call(
        transform_kernel,
        out_shape=jax.ShapeDtypeStruct((BLOCKS * PIECE, 128), jnp.bfloat16),
        in_specs=[vmem] * 6,
        out_specs=vmem,
        scratch_shapes=[
            pltpu.VMEM((2, QUARTER, QUARTER), jnp.bfloat16),
            pltpu.VMEM((2 * ROWS, QUARTER), jnp.bfloat16),
            pltpu.VMEM((2 * ROWS, QUARTER), jnp.bfloat16),
            pltpu.VMEM((12, ROWS, 128), jnp.float32),
            pltpu.VMEM((2, 12, ROWS, 128), jnp.float32),
            pltpu.VMEM((8, 128), jnp.float32),
        ],
        compiler_params=pltpu.CompilerParams(vmem_limit_bytes=20 * MB),
        cost_estimate=pl.CostEstimate(flops=2 * 4 * 2 * ROWS * QUARTER**2, bytes_accessed=2 * 10**6, transcendentals=0),
        name="transform",
    )(x, source, partner, *table)


def away_kernel(got_ref, out_ref, data_ref, list_ref, near_ref, far_ref):
    for o in range(BLOCKS):
        for q in range(6):
            rows = slice(CHANS * o, CHANS * (o + 1))
            row = PIECE * SLOT[o] + CHANS * q
            data_ref[rows, 128 * q:128 * q + 128] = got_ref[row:row + CHANS, :]
    list_ref[...] = jnp.zeros((2, 128, 128), jnp.float32)
    for k in range(BLOCKS):
        lists = got_ref[PIECE * k + DATA:PIECE * (k + 1), :].astype(jnp.float32)
        list_ref[0, k:k + 1, :] = lists[0:1] * CHANS + lists[1:2]
        list_ref[1, k:k + 1, :] = pltpu.roll(lists[0:1], 64, 1)
    partner = jnp.transpose(list_ref[0])
    source = jnp.transpose(list_ref[1])
    list_ref[0], list_ref[1] = partner, source
    cross_pairs(1, data_ref, list_ref, out_ref, near_ref, far_ref)


def keep_kernel(data_ref, list_ref, out_ref, near_ref, far_ref):
    cross_pairs(0, data_ref, list_ref, out_ref, near_ref, far_ref)


def cross_pairs(away, data_ref, list_ref, out_ref, near_ref, far_ref):
    core = (lax.axis_index("core") + away) % 2
    pick = pl.ds(pl.multiple_of(HALF_PAIRS * core, HALF_PAIRS), HALF_PAIRS)
    partner, source = list_ref[0, pick, :], list_ref[1, pick, :]
    channel = iota((HALF_PAIRS, BLOCKS * CHANS), 1).astype(jnp.float32)
    size = 256
    lane = iota((size, 128), 1)
    for m in range(2):
        for o in range(16 * m, 16 * m + 16):
            at = SLOT[o]
            rows = slice(HALF_PAIRS * o, HALF_PAIRS * (o + 1))
            far_ref[rows, :] = jnp.where(channel == partner[:, at:at + 1], 1.0, 0.0).astype(jnp.bfloat16)
            near = channel[:, :256] == source[:, at:at + 1] + float(CHANS * (o % 16))
            near_ref[rows, :] = jnp.where(near, 1.0, 0.0).astype(jnp.bfloat16)
        rows = slice(size * m, size * (m + 1))
        tiles = []
        low = lane < 64
        for t in range(3):
            at = slice(256 * t, 256 * t + 256)
            far = jnp.dot(far_ref[rows, :], data_ref[:, at], preferred_element_type=jnp.float32)
            near = jnp.dot(near_ref[rows, :], data_ref[rows, at], preferred_element_type=jnp.float32)
            a_re, a_im, b_re, b_im = near[:, :128], near[:, 128:], far[:, :128], far[:, 128:]
            real = a_re * b_re + a_im * b_im
            imag = a_im * b_re - a_re * b_im
            tiles.append(jnp.where(low, real, imag) + pltpu.roll(jnp.where(low, imag, real), 64, 1))
        low = lane // 32 % 2 == 0
        one = jnp.where(low, tiles[0] + pltpu.roll(tiles[0], 96, 1), tiles[1] + pltpu.roll(tiles[1], 32, 1))
        two = jnp.where(low, tiles[2] + pltpu.roll(tiles[2], 96, 1), 0.0)
        low = lane // 16 % 2 == 0
        packed = jnp.where(low, one + pltpu.roll(one, 112, 1), two + pltpu.roll(two, 16, 1))
        low = iota((8, 128), 0) < 4
        for o in range(0, 16, 2):
            slots = SLOT[16 * m + o], SLOT[16 * m + o + 1]
            for pair in range(2):
                one = packed[16 * o + 8 * pair:16 * o + 8 * pair + 8]
                two = packed[16 * o + 16 + 8 * pair:16 * o + 24 + 8 * pair]
                if slots[0] > slots[1]:
                    one, two = two, one
                for x, tile in (
                    (2 * pair, jnp.where(low, one, pltpu.roll(two, 4, 0))),
                    (2 * pair + 1, jnp.where(low, pltpu.roll(one, 4, 0), two)),
                ):
                    to = 4 * BLOCKS * ((x + 4 - lax.axis_index("x")) % 4) + 4 * min(slots)
                    out_ref[pl.ds(pl.multiple_of(to, 8), 8), :] = tile


def cross(kernel, *arrays):
    vmem = pl.BlockSpec(memory_space=pltpu.VMEM)
    pairs = BLOCKS * HALF_PAIRS
    shapes = [jax.ShapeDtypeStruct((pairs, 128), jnp.float32)]
    if len(arrays) == 1:
        shapes.append(jax.ShapeDtypeStruct((BLOCKS * CHANS, 6 * 128), jnp.bfloat16))
        shapes.append(jax.ShapeDtypeStruct((2, 128, 128), jnp.float32))
    return pl.pallas_call(
        kernel,
        out_shape=shapes,
        in_specs=[vmem] * len(arrays),
        out_specs=[vmem] * len(shapes),
        scratch_shapes=[
            pltpu.VMEM((pairs, 256), jnp.bfloat16),
            pltpu.VMEM((pairs, BLOCKS * CHANS), jnp.bfloat16),
        ],
        compiler_params=pltpu.CompilerParams(vmem_limit_bytes=16 * MB),
        cost_estimate=pl.CostEstimate(flops=2 * pairs * 768 * 768, bytes_accessed=2 * 10**6, transcendentals=0),
        name="cross",
    )(*arrays)


def bin_of(block, lane):
    tile = 3 * (block // 8) + jnp.where(lane // 32 % 2 == 1, 1, jnp.where(lane // 16 % 2 == 1, 2, 0))
    place = 128 * tile + 16 * (block % 8) + lane % 16 + 1
    back = place - 768
    back = jnp.where(back == 768, 0, back)
    return jnp.where(tile < 6, place, HALF - back), lane // 16 % 4 != 3


def inverse_kernel(count_ref, after_ref, turn_ref, table_ref, first_ref, powers_ref):
    scale = 1.0 / math.sqrt(HALF * 64)
    b = iota((96, 128), 1)
    block, tile = iota((96, 128), 0) // 3, iota((96, 128), 0) % 3
    place = 128 * (3 * (block // 8) + tile) + 16 * (block % 8) + 1
    j0 = jnp.where(block < 16, place, HALF + 768 - place)
    first_ref[0], first_ref[1] = cos_sin((j0 * b).astype(jnp.float32))
    k = iota((16, 128), 0)
    cos_k, sin_k = cos_sin((k * iota((16, 128), 1)).astype(jnp.float32))
    nothing = jnp.zeros((16, 128), jnp.bfloat16)

    def put(at, value):
        coarse = value.astype(jnp.bfloat16)
        rows = pl.ds(pl.multiple_of(at, 16), 16)
        table_ref[rows, 0:128] = coarse
        table_ref[rows, 128:256] = (value - coarse.astype(jnp.float32)).astype(jnp.bfloat16)

    for back in range(2):
        way = -sin_k if back else sin_k

        @pl.loop(16 * back, 16 * back + 16, unroll=4)
        def _(c):
            for i, at in enumerate((0, 32, 16)):
                cos, sin = first_ref[0, pl.ds(3 * c + i, 1), :], first_ref[1, pl.ds(3 * c + i, 1), :]
                put(128 * c + at, cos * cos_k - sin * way)
                put(128 * c + 64 + at, -(sin * cos_k + cos * way))
            for at in (48, 112):
                rows = pl.ds(pl.multiple_of(128 * c + at, 16), 16)
                table_ref[rows, 0:128] = nothing
                table_ref[rows, 128:256] = nothing

    cos, sin = first_ref[0, 95:96, :], first_ref[1, 95:96, :]
    end = jnp.where(iota((16, 128), 1) % 2 == 0, 1.0, -1.0)
    put(128 * 31 + 16, jnp.where(k < 15, cos * cos_k + sin * sin_k, end))
    put(128 * 31 + 80, jnp.where(k < 15, -(sin * cos_k - cos * sin_k), 0.0))

    lane = iota((BLOCKS, 128), 1)
    j, used = bin_of(iota((BLOCKS, 128), 0), lane)
    factor = jnp.where(used, scale, 0.0)
    signed = jnp.where(lane < 64, -factor, factor)
    for a in range(5):
        cos, sin = cos_sin((128 * a * j).astype(jnp.float32))
        if a < 4:
            powers_ref[0, 4 + a] = cos * factor
            powers_ref[1, 4 + a] = sin * signed
        if a > 0:
            powers_ref[0, 4 - a] = cos * factor
            powers_ref[1, 4 - a] = -sin * signed
    row = iota((8, 128), 0)
    low = row < 4
    slot = 4 * (2 * lax.axis_index("x") + lax.axis_index("core")) + row % 4
    live = jnp.where(slot < count_ref[0], 1.0, 0.0)

    @pl.loop(0, BLOCKS, unroll=4)
    def _(c):
        row = pl.ds(c, 1)
        for part in range(2):
            for q in range(4):
                two = jnp.where(low, powers_ref[part, 2 * q, row, :], powers_ref[part, 2 * q + 1, row, :])
                turn_ref[part, pl.ds(pl.multiple_of(32 * c + 8 * q, 8), 8), :] = two * live


def inverse(count, after):
    vmem = pl.BlockSpec(memory_space=pltpu.VMEM)
    return pl.pallas_call(
        inverse_kernel,
        out_shape=(
            jax.ShapeDtypeStruct((2, 32 * BLOCKS, 128), jnp.float32),
            jax.ShapeDtypeStruct((128 * BLOCKS, 256), jnp.bfloat16),
        ),
        in_specs=[pl.BlockSpec(memory_space=pltpu.SMEM), pl.BlockSpec(memory_space=pl.ANY)],
        out_specs=(vmem, vmem),
        scratch_shapes=[pltpu.VMEM((2, 96, 128), jnp.float32), pltpu.VMEM((2, 8, BLOCKS, 128), jnp.float32)],
        compiler_params=pltpu.CompilerParams(vmem_limit_bytes=12 * MB),
        cost_estimate=pl.CostEstimate(flops=10 * 10**6, bytes_accessed=3 * 10**6, transcendentals=0),
        name="inverse",
    )(count, after)


def total_kernel(own_ref, one_ref, two_ref, three_ref, after_ref, out_ref):
    out_ref[...] = own_ref[...] + one_ref[...] + two_ref[...] + three_ref[...]


def add_parts(own, parts, after):
    vmem = pl.BlockSpec(memory_space=pltpu.VMEM)
    return pl.pallas_call(
        total_kernel,
        out_shape=jax.ShapeDtypeStruct(own.shape, jnp.float32),
        in_specs=[vmem] * 4 + [pl.BlockSpec(memory_space=pl.ANY)],
        out_specs=vmem,
        compiler_params=pltpu.CompilerParams(vmem_limit_bytes=4 * MB),
        cost_estimate=pl.CostEstimate(flops=10**5, bytes_accessed=3 * 10**5, transcendentals=0),
        name="total",
    )(own, *parts, after)


def lags_kernel(got_ref, turn_ref, table_ref, out_ref, left_ref):
    for c in range(BLOCKS):
        slot = SLOT[c]
        two = got_ref[8 * (slot // 2):8 * (slot // 2) + 8, :]
        low = iota((8, 128), 0) < 4
        turned = pltpu.roll(two, 4, 0)
        total = jnp.where(low, two, turned) if slot % 2 == 0 else jnp.where(low, turned, two)
        total = jnp.concatenate([total] * 4, axis=0)
        at = slice(32 * c, 32 * c + 32)
        turned = total * turn_ref[0, at, :] + pltpu.roll(total, 64, 1) * turn_ref[1, at, :]
        coarse = turned.astype(jnp.bfloat16)
        left_ref[0:32, 128 * c:128 * c + 128] = coarse
        left_ref[32:64, 128 * c:128 * c + 128] = (turned - coarse.astype(jnp.float32)).astype(jnp.bfloat16)
    both = jnp.dot(left_ref[...], table_ref[...], preferred_element_type=jnp.float32)
    both = both[:32] + both[32:]
    both = both[:, :128] + both[:, 128:]
    for a in range(8):
        out_ref[:, 128 * a:128 * a + 128] = both[4 * a:4 * a + 4, :]


def lags(got, turn, table):
    vmem = pl.BlockSpec(memory_space=pltpu.VMEM)
    return pl.pallas_call(
        lags_kernel,
        out_shape=jax.ShapeDtypeStruct((4, LAGS), jnp.float32),
        in_specs=[vmem] * 3,
        out_specs=vmem,
        scratch_shapes=[pltpu.VMEM((64, 128 * BLOCKS), jnp.bfloat16)],
        compiler_params=pltpu.CompilerParams(vmem_limit_bytes=16 * MB),
        cost_estimate=pl.CostEstimate(flops=2 * 64 * 4096 * 256, bytes_accessed=4 * 10**6, transcendentals=0),
        name="lags",
    )(got, turn, table)


def shards(records, pair_source, pair_partner, pair_count):
    sent = transform(records.reshape(ROWS, N), pair_source, pair_partner, tables())
    rows = BLOCKS * PIECE
    got = lax.all_to_all(sent.reshape(rows // 2, 2, 128), "chan", 0, 0, tiled=True, axis_index_groups=[ORDER])
    got = got.reshape(rows, 128)
    away, data, lists = cross(away_kernel, got)
    near = lax.ppermute(away, "core", [(0, 1), (1, 0)])
    spectra = (cross(keep_kernel, data, lists)[0] + near).reshape(4, 4 * BLOCKS, 128)
    parts = [lax.ppermute(spectra[k], "x", [(x, (x + k) % 4) for x in range(4)]) for k in (2, 3, 1)]
    turn, table = inverse(pair_count, spectra)
    total = add_parts(spectra[0], parts, turn)
    last = lax.all_to_all(total.reshape(BLOCKS, 4, 128), "chan", 0, 0, axis_index_groups=[ORDER])
    return lags(last.reshape(4 * BLOCKS, 128), turn, table)


def solution(mesh):
    chips = Mesh(mesh.devices.reshape(BLOCKS, WINS // 2, 2), ("chan", "x", "core"))
    placed = (P("chan", ("x", "core"), None), P("chan", None), P("chan", None), P("chan"))
    return jax.shard_map(
        shards, mesh=chips, in_specs=placed, out_specs=P(("chan", "x", "core"), None), check_vma=False
    )
```

```python
import math

import jax
import jax.numpy as jnp
from jax import lax
from jax.experimental import pallas as pl
from jax.experimental.pallas import tpu as pltpu
from jax.sharding import Mesh
from jax.sharding import PartitionSpec as P

N = 3072
HALF = N // 2
BAND = 128
LAGS = 1024
QUARTER = N // 4
CHANS, WINS = 16, 8
ROWS = CHANS * WINS
BLOCKS = 32
PAIRS = 32
HALF_PAIRS = PAIRS // 2
DENSE = 96
DATA = 6 * CHANS
PIECE = DATA + 2
MB = 1024 * 1024


def cos_sin(phase):
    turn = jnp.floor(phase * (1.0 / QUARTER) + 0.5)
    t = (phase - QUARTER * turn) * (2.0 * math.pi / N)
    quadrant = turn - 4.0 * jnp.floor(turn * 0.25)
    u = t * t
    s = t * (1.0 + u * (-1 / 6 + u * (1 / 120 + u * (-1 / 5040 + u * (1 / 362880)))))
    c = 1.0 + u * (-1 / 2 + u * (1 / 24 + u * (-1 / 720 + u * (1 / 40320))))
    odd = (quadrant == 1.0) | (quadrant == 3.0)
    cos = jnp.where(odd, s, c)
    sin = jnp.where(odd, c, s)
    cos = jnp.where((quadrant == 1.0) | (quadrant == 2.0), -cos, cos)
    sin = jnp.where(quadrant >= 2.0, -sin, sin)
    return cos, sin


def iota(shape, axis):
    return lax.broadcasted_iota(jnp.int32, shape, axis)


ORDER = list(range(BLOCKS))[::-1]
SLOT = [ORDER.index(block) for block in range(BLOCKS)]


def tables_kernel(table_ref, base_ref, step_ref):
    bins = (iota((16, QUARTER), 1) + 1).astype(jnp.float32)
    row = iota((16, QUARTER), 0).astype(jnp.float32)
    base_ref[0], base_ref[1] = cos_sin((2.0 * row + 2.0) * bins)
    base_ref[2], base_ref[3] = cos_sin((2.0 * row + 1.0) * bins)
    for a in range(3):
        cos, sin = cos_sin(32.0 * (row + 16.0 * a) * bins)
        step_ref[0, 16 * a:16 * a + 16, :] = cos
        step_ref[1, 16 * a:16 * a + 16, :] = sin

    @pl.loop(0, 48)
    def _(a):
        cos = step_ref[0, pl.ds(a, 1), :]
        sin = step_ref[1, pl.ds(a, 1), :]
        rows = pl.ds(pl.multiple_of(16 * a, 16), 16)
        base_cos, base_sin = base_ref[0], base_ref[1]
        table_ref[0, rows, :] = (base_cos * cos - base_sin * sin).astype(jnp.bfloat16)
        table_ref[1, rows, :] = (base_sin * cos + base_cos * sin).astype(jnp.bfloat16)


def tables():
    vmem = pl.BlockSpec(memory_space=pltpu.VMEM)
    return pl.pallas_call(
        tables_kernel,
        out_shape=(
            jax.ShapeDtypeStruct((2, QUARTER, QUARTER), jnp.bfloat16),
            jax.ShapeDtypeStruct((4, 16, QUARTER), jnp.float32),
            jax.ShapeDtypeStruct((2, 48, QUARTER), jnp.float32),
        ),
        out_specs=(vmem,) * 3,
        compiler_params=pltpu.CompilerParams(vmem_limit_bytes=12 * MB),
        cost_estimate=pl.CostEstimate(flops=10**9, bytes_accessed=10**7, transcendentals=0),
        name="tables",
    )()


def transform_kernel(x_ref, source_ref, partner_ref, even_table_ref, base_ref, step_ref, out_ref,
                     odd_table_ref, even_ref, odd_ref, power_ref, white_ref, list_ref):
    lane = iota((ROWS, 128), 1)
    i = iota((256, 256), 0)
    k = iota((256, 256), 1)
    low = k < 128
    k = jnp.where(low, k, k - 128)
    ahead = jnp.where(low, 2 * ((k + 1) % 128), 2 * k + 1)
    back = jnp.where(low, 2 * (127 - k), 2 * (127 - k) + 1)
    ahead = jnp.where(i == ahead, 1.0, 0.0).astype(jnp.bfloat16)
    back = jnp.where(i == back, 1.0, 0.0).astype(jnp.bfloat16)
    rotated = []
    for t in range(6):
        part = jnp.dot(x_ref[:, 256 * t:256 * t + 256], ahead, preferred_element_type=jnp.float32)
        rotated.append(part[:, :128])
        odd_ref[0:ROWS, 128 * t:128 * t + 128] = part[:, 128:].astype(jnp.bfloat16)
        at = 256 * (11 - t)
        part = jnp.dot(x_ref[:, at:at + 256], back, preferred_element_type=jnp.float32)
        even_ref[ROWS:2 * ROWS, 128 * t:128 * t + 128] = part[:, :128].astype(jnp.bfloat16)
        odd_ref[ROWS:2 * ROWS, 128 * t:128 * t + 128] = part[:, 128:].astype(jnp.bfloat16)
    for t in range(6):
        following = rotated[t + 1] if t < 5 else 0.0
        even_ref[0:ROWS, 128 * t:128 * t + 128] = jnp.where(lane < 127, rotated[t], following).astype(jnp.bfloat16)
    first = jnp.sum(jnp.where(lane == 127, rotated[0], 0.0), axis=1, keepdims=True)

    last = jnp.zeros((ROWS, 128), jnp.float32)
    for t in range(24):
        last = last + x_ref[:, 128 * t:128 * t + 128].astype(jnp.float32)
    last = jnp.sum(jnp.where(lane % 2 == 0, last, -last), axis=1, keepdims=True)

    for a in range(48):
        cos, sin = step_ref[0, a:a + 1, :], step_ref[1, a:a + 1, :]
        base_cos, base_sin = base_ref[2], base_ref[3]
        odd_table_ref[0, 16 * a:16 * a + 16, :] = (base_cos * cos - base_sin * sin).astype(jnp.bfloat16)
        odd_table_ref[1, 16 * a:16 * a + 16, :] = (base_sin * cos + base_cos * sin).astype(jnp.bfloat16)

    for u in range(3):
        wide = slice(256 * u, 256 * u + 256)
        even_cos, even_sin, odd_cos, odd_sin = (
            jnp.dot(samples[...], table[which, :, wide], preferred_element_type=jnp.float32)
            for samples, table in ((even_ref, even_table_ref), (odd_ref, odd_table_ref))
            for which in range(2)
        )
        even_cos = even_cos[:ROWS] + even_cos[ROWS:] + first
        even_sin = even_sin[:ROWS] - even_sin[ROWS:]
        odd_cos = odd_cos[:ROWS] + odd_cos[ROWS:]
        odd_sin = odd_sin[:ROWS] - odd_sin[ROWS:]
        for t in (2 * u, 2 * u + 1):
            at = slice(128 * (t % 2), 128 * (t % 2) + 128)
            real, imag = even_cos[:, at] + odd_cos[:, at], -(even_sin[:, at] + odd_sin[:, at])
            real_back, imag_back = even_cos[:, at] - odd_cos[:, at], even_sin[:, at] - odd_sin[:, at]
            if t == 5:
                real_back = jnp.where(lane < 127, real_back, last)
                imag_back = jnp.where(lane < 127, imag_back, 0.0)
            white_ref[0, t], white_ref[1, t] = real, imag
            white_ref[0, 6 + t], white_ref[1, 6 + t] = real_back, imag_back
            power_ref[t] = real * real + imag * imag
            power_ref[6 + t] = real_back * real_back + imag_back * imag_back
    factor = []
    for t in range(12):
        power = power_ref[t]
        if t >= 6:
            power = jnp.where(lane < 127, power, power_ref[6 + (t - 7) % 6])
        mean = jnp.sum(power, axis=1, keepdims=True) * (1.0 / BAND)
        factor.append(lax.rsqrt(mean + 1e-06))

    segment = iota((CHANS, 128), 1) // 16
    for t in range(12):
        scale = factor[t]
        if t >= 6:
            scale = jnp.where(lane < 127, scale, factor[6 + (t - 5) % 6])
        for part in range(2):
            white_ref[part, t] = white_ref[part, t] * scale
            slabs = [
                white_ref[part, t, pl.ds(w, CHANS, stride=WINS), :].astype(jnp.bfloat16) for w in range(WINS)
            ]
            for bit in range(3):
                step = 1 << bit
                high = (segment // step) % 2 == 1
                mixed = [None] * WINS
                for w in range(WINS):
                    if w & step:
                        continue
                    one, two = slabs[w], slabs[w + step]
                    mixed[w] = jnp.where(high, pltpu.roll(two, 16 * step, 1), one)
                    mixed[w + step] = jnp.where(high, two, pltpu.roll(one, 128 - 16 * step, 1))
                slabs = mixed
            at = CHANS * (2 * (t % 3) + part)
            for s in range(8):
                row = PIECE * SLOT[8 * (t // 3) + s] + at
                out_ref[row:row + CHANS, :] = slabs[s]

    partner = partner_ref[...]
    list_ref[...] = jnp.zeros((8, 128), jnp.float32)
    list_ref[0:1, 0:PAIRS] = (partner // CHANS).astype(jnp.float32)
    list_ref[1:2, 0:PAIRS] = (partner % CHANS).astype(jnp.float32)
    list_ref[2:3, 0:PAIRS] = source_ref[...].astype(jnp.float32)
    plain = list_ref[...]
    lane = iota((8, 128), 1)
    lists = jnp.zeros((8, 128), jnp.float32)
    for quad in range(8):
        at, to = 4 * quad, 16 * (quad % 2) + 4 * (quad // 2)
        moved = pltpu.roll(plain, (to - at) % 128, 1)
        lists = jnp.where((lane >= to) & (lane < to + 4), moved, lists)
    sources = pltpu.roll(pltpu.roll(lists, 6, 0), 64, 1)
    lists = jnp.where((iota((8, 128), 0) == 0) & (lane >= 64), sources, lists).astype(jnp.bfloat16)
    for c in range(BLOCKS):
        out_ref[PIECE * c + DATA:PIECE * (c + 1), :] = lists[:2]


def transform(x, source, partner, table):
    vmem = pl.BlockSpec(memory_space=pltpu.VMEM)
    return pl.pallas_call(
        transform_kernel,
        out_shape=jax.ShapeDtypeStruct((BLOCKS * PIECE, 128), jnp.bfloat16),
        in_specs=[vmem] * 6,
        out_specs=vmem,
        scratch_shapes=[
            pltpu.VMEM((2, QUARTER, QUARTER), jnp.bfloat16),
            pltpu.VMEM((2 * ROWS, QUARTER), jnp.bfloat16),
            pltpu.VMEM((2 * ROWS, QUARTER), jnp.bfloat16),
            pltpu.VMEM((12, ROWS, 128), jnp.float32),
            pltpu.VMEM((2, 12, ROWS, 128), jnp.float32),
            pltpu.VMEM((8, 128), jnp.float32),
        ],
        compiler_params=pltpu.CompilerParams(vmem_limit_bytes=20 * MB),
        cost_estimate=pl.CostEstimate(flops=2 * 4 * 2 * ROWS * QUARTER**2, bytes_accessed=2 * 10**6, transcendentals=0),
        name="transform",
    )(x, source, partner, *table)


def away_kernel(got_ref, out_ref, data_ref, list_ref, near_ref, far_ref):
    for o in range(BLOCKS):
        for q in range(6):
            rows = slice(CHANS * o, CHANS * (o + 1))
            row = PIECE * SLOT[o] + CHANS * q
            data_ref[rows, 128 * q:128 * q + 128] = got_ref[row:row + CHANS, :]
    list_ref[...] = jnp.zeros((2, 128, 128), jnp.float32)
    for k in range(BLOCKS):
        lists = got_ref[PIECE * k + DATA:PIECE * (k + 1), :].astype(jnp.float32)
        list_ref[0, k:k + 1, :] = lists[0:1] * CHANS + lists[1:2]
        list_ref[1, k:k + 1, :] = pltpu.roll(lists[0:1], 64, 1)
    partner = jnp.transpose(list_ref[0])
    source = jnp.transpose(list_ref[1])
    list_ref[0], list_ref[1] = partner, source
    cross_pairs(1, data_ref, list_ref, out_ref, near_ref, far_ref)


def keep_kernel(data_ref, list_ref, out_ref, near_ref, far_ref):
    cross_pairs(0, data_ref, list_ref, out_ref, near_ref, far_ref)


def cross_pairs(away, data_ref, list_ref, out_ref, near_ref, far_ref):
    core = (lax.axis_index("core") + away) % 2
    pick = pl.ds(pl.multiple_of(HALF_PAIRS * core, HALF_PAIRS), HALF_PAIRS)
    partner, source = list_ref[0, pick, :], list_ref[1, pick, :]
    channel = iota((HALF_PAIRS, BLOCKS * CHANS), 1).astype(jnp.float32)
    size = 256
    lane = iota((size, 128), 1)
    held = {}
    for m in range(2):
        for o in range(16 * m, 16 * m + 16):
            at = SLOT[o]
            rows = slice(HALF_PAIRS * o, HALF_PAIRS * (o + 1))
            far_ref[rows, :] = jnp.where(channel == partner[:, at:at + 1], 1.0, 0.0).astype(jnp.bfloat16)
            near = channel[:, :256] == source[:, at:at + 1] + float(CHANS * (o % 16))
            near_ref[rows, :] = jnp.where(near, 1.0, 0.0).astype(jnp.bfloat16)
        rows = slice(size * m, size * (m + 1))
        tiles = []
        low = lane < 64
        for t in range(3):
            at = slice(256 * t, 256 * t + 256)
            far = jnp.dot(far_ref[rows, :], data_ref[:, at], preferred_element_type=jnp.float32)
            near = jnp.dot(near_ref[rows, :], data_ref[rows, at], preferred_element_type=jnp.float32)
            a_re, a_im, b_re, b_im = near[:, :128], near[:, 128:], far[:, :128], far[:, 128:]
            real = a_re * b_re + a_im * b_im
            imag = a_im * b_re - a_re * b_im
            tiles.append(jnp.where(low, real, imag) + pltpu.roll(jnp.where(low, imag, real), 64, 1))
        low = lane // 32 % 2 == 0
        one = jnp.where(low, tiles[0] + pltpu.roll(tiles[0], 96, 1), tiles[1] + pltpu.roll(tiles[1], 32, 1))
        two = jnp.where(low, tiles[2] + pltpu.roll(tiles[2], 96, 1), 0.0)
        low = lane // 16 % 2 == 0
        packed = jnp.where(low, one + pltpu.roll(one, 112, 1), two + pltpu.roll(two, 16, 1))
        low = iota((8, 128), 0) < 4
        for o in range(0, 16, 2):
            slots = SLOT[16 * m + o], SLOT[16 * m + o + 1]
            for pair in range(2):
                one = packed[16 * o + 8 * pair:16 * o + 8 * pair + 8]
                two = packed[16 * o + 16 + 8 * pair:16 * o + 24 + 8 * pair]
                if slots[0] > slots[1]:
                    one, two = two, one
                for x, tile in (
                    (2 * pair, jnp.where(low, one, pltpu.roll(two, 4, 0))),
                    (2 * pair + 1, jnp.where(low, pltpu.roll(one, 4, 0), two)),
                ):
                    at = 4 * min(slots)
                    if at >= DENSE:
                        held[x, at - DENSE] = tile
                        continue
                    filler = pltpu.roll(held[x, at % 32], (48, 16, 32)[at // 32], 1)
                    tile = jnp.where(iota((8, 128), 1) // 16 % 4 == 3, filler, tile)
                    to = DENSE * ((x + 4 - lax.axis_index("x")) % 4) + at
                    out_ref[pl.ds(pl.multiple_of(to, 8), 8), :] = tile


def cross(kernel, *arrays):
    vmem = pl.BlockSpec(memory_space=pltpu.VMEM)
    pairs = BLOCKS * HALF_PAIRS
    shapes = [jax.ShapeDtypeStruct((4 * DENSE, 128), jnp.float32)]
    if len(arrays) == 1:
        shapes.append(jax.ShapeDtypeStruct((BLOCKS * CHANS, 6 * 128), jnp.bfloat16))
        shapes.append(jax.ShapeDtypeStruct((2, 128, 128), jnp.float32))
    return pl.pallas_call(
        kernel,
        out_shape=shapes,
        in_specs=[vmem] * len(arrays),
        out_specs=[vmem] * len(shapes),
        scratch_shapes=[
            pltpu.VMEM((pairs, 256), jnp.bfloat16),
            pltpu.VMEM((pairs, BLOCKS * CHANS), jnp.bfloat16),
        ],
        compiler_params=pltpu.CompilerParams(vmem_limit_bytes=16 * MB),
        cost_estimate=pl.CostEstimate(flops=2 * pairs * 768 * 768, bytes_accessed=2 * 10**6, transcendentals=0),
        name="cross",
    )(*arrays)


def bin_of(block, lane):
    tile = 3 * (block // 8) + jnp.where(lane // 32 % 2 == 1, 1, jnp.where(lane // 16 % 2 == 1, 2, 0))
    place = 128 * tile + 16 * (block % 8) + lane % 16 + 1
    back = place - 768
    back = jnp.where(back == 768, 0, back)
    return jnp.where(tile < 6, place, HALF - back), lane // 16 % 4 != 3


def inverse_kernel(count_ref, after_ref, turn_ref, table_ref, first_ref, powers_ref):
    scale = 1.0 / math.sqrt(HALF * 64)
    b = iota((96, 128), 1)
    block, tile = iota((96, 128), 0) // 3, iota((96, 128), 0) % 3
    place = 128 * (3 * (block // 8) + tile) + 16 * (block % 8) + 1
    j0 = jnp.where(block < 16, place, HALF + 768 - place)
    first_ref[0], first_ref[1] = cos_sin((j0 * b).astype(jnp.float32))
    k = iota((16, 128), 0)
    cos_k, sin_k = cos_sin((k * iota((16, 128), 1)).astype(jnp.float32))
    nothing = jnp.zeros((16, 128), jnp.bfloat16)

    def put(at, value):
        coarse = value.astype(jnp.bfloat16)
        rows = pl.ds(pl.multiple_of(at, 16), 16)
        table_ref[rows, 0:128] = coarse
        table_ref[rows, 128:256] = (value - coarse.astype(jnp.float32)).astype(jnp.bfloat16)

    for back in range(2):
        way = -sin_k if back else sin_k

        @pl.loop(16 * back, 16 * back + 16, unroll=4)
        def _(c):
            for i, at in enumerate((0, 32, 16)):
                cos, sin = first_ref[0, pl.ds(3 * c + i, 1), :], first_ref[1, pl.ds(3 * c + i, 1), :]
                put(128 * c + at, cos * cos_k - sin * way)
                put(128 * c + 64 + at, -(sin * cos_k + cos * way))
            for at in (48, 112):
                rows = pl.ds(pl.multiple_of(128 * c + at, 16), 16)
                table_ref[rows, 0:128] = nothing
                table_ref[rows, 128:256] = nothing

    cos, sin = first_ref[0, 95:96, :], first_ref[1, 95:96, :]
    end = jnp.where(iota((16, 128), 1) % 2 == 0, 1.0, -1.0)
    put(128 * 31 + 16, jnp.where(k < 15, cos * cos_k + sin * sin_k, end))
    put(128 * 31 + 80, jnp.where(k < 15, -(sin * cos_k - cos * sin_k), 0.0))

    lane = iota((BLOCKS, 128), 1)
    j, used = bin_of(iota((BLOCKS, 128), 0), lane)
    factor = jnp.where(used, scale, 0.0)
    signed = jnp.where(lane < 64, -factor, factor)
    for a in range(5):
        cos, sin = cos_sin((128 * a * j).astype(jnp.float32))
        if a < 4:
            powers_ref[0, 4 + a] = cos * factor
            powers_ref[1, 4 + a] = sin * signed
        if a > 0:
            powers_ref[0, 4 - a] = cos * factor
            powers_ref[1, 4 - a] = -sin * signed
    row = iota((8, 128), 0)
    low = row < 4
    slot = 4 * (2 * lax.axis_index("x") + lax.axis_index("core")) + row % 4
    live = jnp.where(slot < count_ref[0], 1.0, 0.0)

    @pl.loop(0, BLOCKS, unroll=4)
    def _(c):
        row = pl.ds(c, 1)
        for part in range(2):
            for q in range(4):
                two = jnp.where(low, powers_ref[part, 2 * q, row, :], powers_ref[part, 2 * q + 1, row, :])
                turn_ref[part, pl.ds(pl.multiple_of(32 * c + 8 * q, 8), 8), :] = two * live


def inverse(count, after):
    vmem = pl.BlockSpec(memory_space=pltpu.VMEM)
    return pl.pallas_call(
        inverse_kernel,
        out_shape=(
            jax.ShapeDtypeStruct((2, 32 * BLOCKS, 128), jnp.float32),
            jax.ShapeDtypeStruct((128 * BLOCKS, 256), jnp.bfloat16),
        ),
        in_specs=[pl.BlockSpec(memory_space=pltpu.SMEM), pl.BlockSpec(memory_space=pl.ANY)],
        out_specs=(vmem, vmem),
        scratch_shapes=[pltpu.VMEM((2, 96, 128), jnp.float32), pltpu.VMEM((2, 8, BLOCKS, 128), jnp.float32)],
        compiler_params=pltpu.CompilerParams(vmem_limit_bytes=12 * MB),
        cost_estimate=pl.CostEstimate(flops=10 * 10**6, bytes_accessed=3 * 10**6, transcendentals=0),
        name="inverse",
    )(count, after)


def total_kernel(own_ref, one_ref, two_ref, three_ref, after_ref, out_ref):
    total = own_ref[...] + one_ref[...] + two_ref[...] + three_ref[...]
    out_ref[0:DENSE, :] = total
    group = iota((32, 128), 1) // 16 % 4
    first, second, third = (pltpu.roll(total[32 * t:32 * t + 32], 128 - (48, 16, 32)[t], 1) for t in range(3))
    rest = jnp.where(group == 0, first, jnp.where(group == 2, second, third))
    out_ref[DENSE:, :] = jnp.where(group == 3, 0.0, rest)


def add_parts(own, parts, after):
    vmem = pl.BlockSpec(memory_space=pltpu.VMEM)
    return pl.pallas_call(
        total_kernel,
        out_shape=jax.ShapeDtypeStruct((4 * BLOCKS, 128), jnp.float32),
        in_specs=[vmem] * 4 + [pl.BlockSpec(memory_space=pl.ANY)],
        out_specs=vmem,
        compiler_params=pltpu.CompilerParams(vmem_limit_bytes=4 * MB),
        cost_estimate=pl.CostEstimate(flops=10**5, bytes_accessed=3 * 10**5, transcendentals=0),
        name="total",
    )(own, *parts, after)


def lags_kernel(got_ref, turn_ref, table_ref, out_ref, left_ref):
    for c in range(BLOCKS):
        slot = SLOT[c]
        two = got_ref[8 * (slot // 2):8 * (slot // 2) + 8, :]
        low = iota((8, 128), 0) < 4
        turned = pltpu.roll(two, 4, 0)
        total = jnp.where(low, two, turned) if slot % 2 == 0 else jnp.where(low, turned, two)
        total = jnp.concatenate([total] * 4, axis=0)
        at = slice(32 * c, 32 * c + 32)
        turned = total * turn_ref[0, at, :] + pltpu.roll(total, 64, 1) * turn_ref[1, at, :]
        coarse = turned.astype(jnp.bfloat16)
        left_ref[0:32, 128 * c:128 * c + 128] = coarse
        left_ref[32:64, 128 * c:128 * c + 128] = (turned - coarse.astype(jnp.float32)).astype(jnp.bfloat16)
    both = jnp.dot(left_ref[...], table_ref[...], preferred_element_type=jnp.float32)
    both = both[:32] + both[32:]
    both = both[:, :128] + both[:, 128:]
    for a in range(8):
        out_ref[:, 128 * a:128 * a + 128] = both[4 * a:4 * a + 4, :]


def lags(got, turn, table):
    vmem = pl.BlockSpec(memory_space=pltpu.VMEM)
    return pl.pallas_call(
        lags_kernel,
        out_shape=jax.ShapeDtypeStruct((4, LAGS), jnp.float32),
        in_specs=[vmem] * 3,
        out_specs=vmem,
        scratch_shapes=[pltpu.VMEM((64, 128 * BLOCKS), jnp.bfloat16)],
        compiler_params=pltpu.CompilerParams(vmem_limit_bytes=16 * MB),
        cost_estimate=pl.CostEstimate(flops=2 * 64 * 4096 * 256, bytes_accessed=4 * 10**6, transcendentals=0),
        name="lags",
    )(got, turn, table)


def shards(records, pair_source, pair_partner, pair_count):
    sent = transform(records.reshape(ROWS, N), pair_source, pair_partner, tables())
    rows = BLOCKS * PIECE
    got = lax.all_to_all(sent.reshape(rows // 2, 2, 128), "chan", 0, 0, tiled=True, axis_index_groups=[ORDER])
    got = got.reshape(rows, 128)
    away, data, lists = cross(away_kernel, got)
    near = lax.ppermute(away, "core", [(0, 1), (1, 0)])
    spectra = (cross(keep_kernel, data, lists)[0] + near).reshape(4, DENSE, 128)
    parts = [lax.ppermute(spectra[k], "x", [(x, (x + k) % 4) for x in range(4)]) for k in (2, 3, 1)]
    turn, table = inverse(pair_count, spectra)
    total = add_parts(spectra[0], parts, turn)
    last = lax.all_to_all(total.reshape(BLOCKS, 4, 128), "chan", 0, 0, axis_index_groups=[ORDER])
    return lags(last.reshape(4 * BLOCKS, 128), turn, table)


def solution(mesh):
    chips = Mesh(mesh.devices.reshape(BLOCKS, WINS // 2, 2), ("chan", "x", "core"))
    placed = (P("chan", ("x", "core"), None), P("chan", None), P("chan", None), P("chan"))
    return jax.shard_map(
        shards, mesh=chips, in_specs=placed, out_specs=P(("chan", "x", "core"), None), check_vma=False
    )
```

```python
import math

import jax
import jax.numpy as jnp
from jax import lax
from jax.experimental import pallas as pl
from jax.experimental.pallas import tpu as pltpu
from jax.sharding import Mesh
from jax.sharding import PartitionSpec as P

N = 3072
HALF = N // 2
BAND = 128
LAGS = 1024
QUARTER = N // 4
CHANS, WINS = 16, 8
ROWS = CHANS * WINS
BLOCKS = 32
PAIRS = 32
HALF_PAIRS = PAIRS // 2
DENSE = 96
DATA = 6 * CHANS
PIECE = DATA + 2
MB = 1024 * 1024


def cos_sin(phase):
    turn = jnp.floor(phase * (1.0 / QUARTER) + 0.5)
    t = (phase - QUARTER * turn) * (2.0 * math.pi / N)
    quadrant = turn - 4.0 * jnp.floor(turn * 0.25)
    u = t * t
    s = t * (1.0 + u * (-1 / 6 + u * (1 / 120 + u * (-1 / 5040 + u * (1 / 362880)))))
    c = 1.0 + u * (-1 / 2 + u * (1 / 24 + u * (-1 / 720 + u * (1 / 40320))))
    odd = (quadrant == 1.0) | (quadrant == 3.0)
    cos = jnp.where(odd, s, c)
    sin = jnp.where(odd, c, s)
    cos = jnp.where((quadrant == 1.0) | (quadrant == 2.0), -cos, cos)
    sin = jnp.where(quadrant >= 2.0, -sin, sin)
    return cos, sin


def iota(shape, axis):
    return lax.broadcasted_iota(jnp.int32, shape, axis)


ORDER = list(range(BLOCKS))[::-1]
SLOT = [ORDER.index(block) for block in range(BLOCKS)]


def tables_kernel(table_ref, base_ref, step_ref):
    bins = (iota((16, QUARTER), 1) + 1).astype(jnp.float32)
    row = iota((16, QUARTER), 0).astype(jnp.float32)
    base_ref[0], base_ref[1] = cos_sin((2.0 * row + 2.0) * bins)
    base_ref[2], base_ref[3] = cos_sin((2.0 * row + 1.0) * bins)
    for a in range(3):
        cos, sin = cos_sin(32.0 * (row + 16.0 * a) * bins)
        step_ref[0, 16 * a:16 * a + 16, :] = cos
        step_ref[1, 16 * a:16 * a + 16, :] = sin

    @pl.loop(0, 48)
    def _(a):
        cos = step_ref[0, pl.ds(a, 1), :]
        sin = step_ref[1, pl.ds(a, 1), :]
        rows = pl.ds(pl.multiple_of(16 * a, 16), 16)
        base_cos, base_sin = base_ref[0], base_ref[1]
        table_ref[0, rows, :] = (base_cos * cos - base_sin * sin).astype(jnp.bfloat16)
        table_ref[1, rows, :] = (base_sin * cos + base_cos * sin).astype(jnp.bfloat16)


def tables():
    vmem = pl.BlockSpec(memory_space=pltpu.VMEM)
    return pl.pallas_call(
        tables_kernel,
        out_shape=(
            jax.ShapeDtypeStruct((2, QUARTER, QUARTER), jnp.bfloat16),
            jax.ShapeDtypeStruct((4, 16, QUARTER), jnp.float32),
            jax.ShapeDtypeStruct((2, 48, QUARTER), jnp.float32),
        ),
        out_specs=(vmem,) * 3,
        compiler_params=pltpu.CompilerParams(vmem_limit_bytes=12 * MB),
        cost_estimate=pl.CostEstimate(flops=10**9, bytes_accessed=10**7, transcendentals=0),
        name="tables",
    )()


def transform_kernel(x_ref, source_ref, partner_ref, even_table_ref, base_ref, step_ref, out_ref,
                     odd_table_ref, even_ref, odd_ref, power_ref, white_ref, list_ref):
    lane = iota((ROWS, 128), 1)
    i = iota((256, 256), 0)
    k = iota((256, 256), 1)
    low = k < 128
    k = jnp.where(low, k, k - 128)
    ahead = jnp.where(low, 2 * ((k + 1) % 128), 2 * k + 1)
    back = jnp.where(low, 2 * (127 - k), 2 * (127 - k) + 1)
    ahead = jnp.where(i == ahead, 1.0, 0.0).astype(jnp.bfloat16)
    back = jnp.where(i == back, 1.0, 0.0).astype(jnp.bfloat16)
    rotated = []
    for t in range(6):
        part = jnp.dot(x_ref[:, 256 * t:256 * t + 256], ahead, preferred_element_type=jnp.float32)
        rotated.append(part[:, :128])
        odd_ref[0:ROWS, 128 * t:128 * t + 128] = part[:, 128:].astype(jnp.bfloat16)
        at = 256 * (11 - t)
        part = jnp.dot(x_ref[:, at:at + 256], back, preferred_element_type=jnp.float32)
        even_ref[ROWS:2 * ROWS, 128 * t:128 * t + 128] = part[:, :128].astype(jnp.bfloat16)
        odd_ref[ROWS:2 * ROWS, 128 * t:128 * t + 128] = part[:, 128:].astype(jnp.bfloat16)
    for t in range(6):
        following = rotated[t + 1] if t < 5 else 0.0
        even_ref[0:ROWS, 128 * t:128 * t + 128] = jnp.where(lane < 127, rotated[t], following).astype(jnp.bfloat16)
    first = jnp.sum(jnp.where(lane == 127, rotated[0], 0.0), axis=1, keepdims=True)

    last = jnp.zeros((ROWS, 128), jnp.float32)
    for t in range(24):
        last = last + x_ref[:, 128 * t:128 * t + 128].astype(jnp.float32)
    last = jnp.sum(jnp.where(lane % 2 == 0, last, -last), axis=1, keepdims=True)

    for a in range(48):
        cos, sin = step_ref[0, a:a + 1, :], step_ref[1, a:a + 1, :]
        base_cos, base_sin = base_ref[2], base_ref[3]
        odd_table_ref[0, 16 * a:16 * a + 16, :] = (base_cos * cos - base_sin * sin).astype(jnp.bfloat16)
        odd_table_ref[1, 16 * a:16 * a + 16, :] = (base_sin * cos + base_cos * sin).astype(jnp.bfloat16)

    for u in range(3):
        wide = slice(256 * u, 256 * u + 256)
        even_cos, even_sin, odd_cos, odd_sin = (
            jnp.dot(samples[...], table[which, :, wide], preferred_element_type=jnp.float32)
            for samples, table in ((even_ref, even_table_ref), (odd_ref, odd_table_ref))
            for which in range(2)
        )
        even_cos = even_cos[:ROWS] + even_cos[ROWS:] + first
        even_sin = even_sin[:ROWS] - even_sin[ROWS:]
        odd_cos = odd_cos[:ROWS] + odd_cos[ROWS:]
        odd_sin = odd_sin[:ROWS] - odd_sin[ROWS:]
        for t in (2 * u, 2 * u + 1):
            at = slice(128 * (t % 2), 128 * (t % 2) + 128)
            real, imag = even_cos[:, at] + odd_cos[:, at], -(even_sin[:, at] + odd_sin[:, at])
            real_back, imag_back = even_cos[:, at] - odd_cos[:, at], even_sin[:, at] - odd_sin[:, at]
            if t == 5:
                real_back = jnp.where(lane < 127, real_back, last)
                imag_back = jnp.where(lane < 127, imag_back, 0.0)
            white_ref[0, t], white_ref[1, t] = real, imag
            white_ref[0, 6 + t], white_ref[1, 6 + t] = real_back, imag_back
            power_ref[t] = real * real + imag * imag
            power_ref[6 + t] = real_back * real_back + imag_back * imag_back
    factor = []
    for t in range(12):
        power = power_ref[t]
        if t >= 6:
            power = jnp.where(lane < 127, power, power_ref[6 + (t - 7) % 6])
        mean = jnp.sum(power, axis=1, keepdims=True) * (1.0 / BAND)
        factor.append(lax.rsqrt(mean + 1e-06))

    segment = iota((CHANS, 128), 1) // 16
    for t in range(12):
        scale = factor[t]
        if t >= 6:
            scale = jnp.where(lane < 127, scale, factor[6 + (t - 5) % 6])
        for part in range(2):
            white_ref[part, t] = white_ref[part, t] * scale
            slabs = [
                white_ref[part, t, pl.ds(w, CHANS, stride=WINS), :].astype(jnp.bfloat16) for w in range(WINS)
            ]
            for bit in range(3):
                step = 1 << bit
                high = (segment // step) % 2 == 1
                mixed = [None] * WINS
                for w in range(WINS):
                    if w & step:
                        continue
                    one, two = slabs[w], slabs[w + step]
                    mixed[w] = jnp.where(high, pltpu.roll(two, 16 * step, 1), one)
                    mixed[w + step] = jnp.where(high, two, pltpu.roll(one, 128 - 16 * step, 1))
                slabs = mixed
            at = CHANS * (2 * (t % 3) + part)
            for s in range(8):
                row = PIECE * SLOT[8 * (t // 3) + s] + at
                out_ref[row:row + CHANS, :] = slabs[s]

    partner = partner_ref[...]
    list_ref[...] = jnp.zeros((8, 128), jnp.float32)
    list_ref[0:1, 0:PAIRS] = (partner // CHANS).astype(jnp.float32)
    list_ref[1:2, 0:PAIRS] = (partner % CHANS).astype(jnp.float32)
    list_ref[2:3, 0:PAIRS] = source_ref[...].astype(jnp.float32)
    plain = list_ref[...]
    lane = iota((8, 128), 1)
    lists = jnp.zeros((8, 128), jnp.float32)
    for quad in range(8):
        at, to = 4 * quad, 16 * (quad % 2) + 4 * (quad // 2)
        moved = pltpu.roll(plain, (to - at) % 128, 1)
        lists = jnp.where((lane >= to) & (lane < to + 4), moved, lists)
    sources = pltpu.roll(pltpu.roll(lists, 6, 0), 64, 1)
    lists = jnp.where((iota((8, 128), 0) == 0) & (lane >= 64), sources, lists).astype(jnp.bfloat16)
    for c in range(BLOCKS):
        out_ref[PIECE * c + DATA:PIECE * (c + 1), :] = lists[:2]


def transform(x, source, partner, table):
    vmem = pl.BlockSpec(memory_space=pltpu.VMEM)
    return pl.pallas_call(
        transform_kernel,
        out_shape=jax.ShapeDtypeStruct((BLOCKS * PIECE, 128), jnp.bfloat16),
        in_specs=[vmem] * 6,
        out_specs=vmem,
        scratch_shapes=[
            pltpu.VMEM((2, QUARTER, QUARTER), jnp.bfloat16),
            pltpu.VMEM((2 * ROWS, QUARTER), jnp.bfloat16),
            pltpu.VMEM((2 * ROWS, QUARTER), jnp.bfloat16),
            pltpu.VMEM((12, ROWS, 128), jnp.float32),
            pltpu.VMEM((2, 12, ROWS, 128), jnp.float32),
            pltpu.VMEM((8, 128), jnp.float32),
        ],
        compiler_params=pltpu.CompilerParams(vmem_limit_bytes=20 * MB),
        cost_estimate=pl.CostEstimate(flops=2 * 4 * 2 * ROWS * QUARTER**2, bytes_accessed=2 * 10**6, transcendentals=0),
        name="transform",
    )(x, source, partner, *table)


def away_kernel(got_ref, out_ref, data_ref, list_ref, near_ref, far_ref):
    for o in range(BLOCKS):
        for q in range(6):
            rows = slice(CHANS * o, CHANS * (o + 1))
            row = PIECE * SLOT[o] + CHANS * q
            data_ref[rows, 128 * q:128 * q + 128] = got_ref[row:row + CHANS, :]
    list_ref[...] = jnp.zeros((2, 128, 128), jnp.float32)
    for k in range(BLOCKS):
        lists = got_ref[PIECE * k + DATA:PIECE * (k + 1), :].astype(jnp.float32)
        list_ref[0, k:k + 1, :] = lists[0:1] * CHANS + lists[1:2]
        list_ref[1, k:k + 1, :] = pltpu.roll(lists[0:1], 64, 1)
    partner = jnp.transpose(list_ref[0])
    source = jnp.transpose(list_ref[1])
    list_ref[0], list_ref[1] = partner, source
    cross_pairs(1, data_ref, list_ref, out_ref, near_ref, far_ref)


def keep_kernel(data_ref, list_ref, out_ref, near_ref, far_ref):
    cross_pairs(0, data_ref, list_ref, out_ref, near_ref, far_ref)


def cross_pairs(away, data_ref, list_ref, out_ref, near_ref, far_ref):
    core = (lax.axis_index("core") + away) % 2
    pick = pl.ds(pl.multiple_of(HALF_PAIRS * core, HALF_PAIRS), HALF_PAIRS)
    partner, source = list_ref[0, pick, :], list_ref[1, pick, :]
    channel = iota((HALF_PAIRS, BLOCKS * CHANS), 1).astype(jnp.float32)
    size = 256
    lane = iota((size, 128), 1)
    held = {}
    for m in range(2):
        for o in range(16 * m, 16 * m + 16):
            at = SLOT[o]
            rows = slice(HALF_PAIRS * o, HALF_PAIRS * (o + 1))
            far_ref[rows, :] = jnp.where(channel == partner[:, at:at + 1], 1.0, 0.0).astype(jnp.bfloat16)
            near = channel[:, :256] == source[:, at:at + 1] + float(CHANS * (o % 16))
            near_ref[rows, :] = jnp.where(near, 1.0, 0.0).astype(jnp.bfloat16)
        rows = slice(size * m, size * (m + 1))
        tiles = []
        low = lane < 64
        for t in range(3):
            at = slice(256 * t, 256 * t + 256)
            far = jnp.dot(far_ref[rows, :], data_ref[:, at], preferred_element_type=jnp.float32)
            near = jnp.dot(near_ref[rows, :], data_ref[rows, at], preferred_element_type=jnp.float32)
            a_re, a_im, b_re, b_im = near[:, :128], near[:, 128:], far[:, :128], far[:, 128:]
            real = a_re * b_re + a_im * b_im
            imag = a_im * b_re - a_re * b_im
            tiles.append(jnp.where(low, real, imag) + pltpu.roll(jnp.where(low, imag, real), 64, 1))
        low = lane // 32 % 2 == 0
        one = jnp.where(low, tiles[0] + pltpu.roll(tiles[0], 96, 1), tiles[1] + pltpu.roll(tiles[1], 32, 1))
        two = jnp.where(low, tiles[2] + pltpu.roll(tiles[2], 96, 1), 0.0)
        low = lane // 16 % 2 == 0
        packed = jnp.where(low, one + pltpu.roll(one, 112, 1), two + pltpu.roll(two, 16, 1))
        low = iota((8, 128), 0) < 4
        for o in range(0, 16, 2):
            slots = SLOT[16 * m + o], SLOT[16 * m + o + 1]
            for pair in range(2):
                one = packed[16 * o + 8 * pair:16 * o + 8 * pair + 8]
                two = packed[16 * o + 16 + 8 * pair:16 * o + 24 + 8 * pair]
                if slots[0] > slots[1]:
                    one, two = two, one
                for x, tile in (
                    (2 * pair, jnp.where(low, one, pltpu.roll(two, 4, 0))),
                    (2 * pair + 1, jnp.where(low, pltpu.roll(one, 4, 0), two)),
                ):
                    at = 4 * min(slots)
                    if at >= DENSE:
                        held[x, at - DENSE] = tile
                        continue
                    filler = pltpu.roll(held[x, at % 32], (48, 16, 32)[at // 32], 1)
                    tile = jnp.where(iota((8, 128), 1) // 16 % 4 == 3, filler, tile)
                    to = DENSE * ((x + 4 - lax.axis_index("x")) % 4) + at
                    out_ref[pl.ds(pl.multiple_of(to, 8), 8), :] = tile


def cross(kernel, *arrays):
    vmem = pl.BlockSpec(memory_space=pltpu.VMEM)
    pairs = BLOCKS * HALF_PAIRS
    shapes = [jax.ShapeDtypeStruct((4 * DENSE, 128), jnp.float32)]
    if len(arrays) == 1:
        shapes.append(jax.ShapeDtypeStruct((BLOCKS * CHANS, 6 * 128), jnp.bfloat16))
        shapes.append(jax.ShapeDtypeStruct((2, 128, 128), jnp.float32))
    return pl.pallas_call(
        kernel,
        out_shape=shapes,
        in_specs=[vmem] * len(arrays),
        out_specs=[vmem] * len(shapes),
        scratch_shapes=[
            pltpu.VMEM((pairs, 256), jnp.bfloat16),
            pltpu.VMEM((pairs, BLOCKS * CHANS), jnp.bfloat16),
        ],
        compiler_params=pltpu.CompilerParams(vmem_limit_bytes=16 * MB),
        cost_estimate=pl.CostEstimate(flops=2 * pairs * 768 * 768, bytes_accessed=2 * 10**6, transcendentals=0),
        name="cross",
    )(*arrays)


def bin_of(block, lane):
    tile = 3 * (block // 8) + jnp.where(lane // 32 % 2 == 1, 1, jnp.where(lane // 16 % 2 == 1, 2, 0))
    place = 128 * tile + 16 * (block % 8) + lane % 16 + 1
    back = place - 768
    back = jnp.where(back == 768, 0, back)
    return jnp.where(tile < 6, place, HALF - back), lane // 16 % 4 != 3


def inverse_kernel(count_ref, after_ref, turn_ref, table_ref, first_ref, powers_ref):
    scale = 1.0 / math.sqrt(HALF * 64)
    b = iota((96, 128), 1)
    block, tile = iota((96, 128), 0) // 3, iota((96, 128), 0) % 3
    place = 128 * (3 * (block // 8) + tile) + 16 * (block % 8) + 1
    j0 = jnp.where(block < 16, place, HALF + 768 - place)
    first_ref[0], first_ref[1] = cos_sin((j0 * b).astype(jnp.float32))
    k = iota((16, 128), 0)
    cos_k, sin_k = cos_sin((k * iota((16, 128), 1)).astype(jnp.float32))
    nothing = jnp.zeros((16, 128), jnp.bfloat16)

    def put(at, value):
        coarse = value.astype(jnp.bfloat16)
        rows = pl.ds(pl.multiple_of(at, 16), 16)
        table_ref[rows, 0:128] = coarse
        table_ref[rows, 128:256] = (value - coarse.astype(jnp.float32)).astype(jnp.bfloat16)

    for back in range(2):
        way = -sin_k if back else sin_k

        @pl.loop(16 * back, 16 * back + 16, unroll=4)
        def _(c):
            for i, at in enumerate((0, 32, 16)):
                cos, sin = first_ref[0, pl.ds(3 * c + i, 1), :], first_ref[1, pl.ds(3 * c + i, 1), :]
                put(128 * c + at, cos * cos_k - sin * way)
                put(128 * c + 64 + at, -(sin * cos_k + cos * way))
            for at in (48, 112):
                rows = pl.ds(pl.multiple_of(128 * c + at, 16), 16)
                table_ref[rows, 0:128] = nothing
                table_ref[rows, 128:256] = nothing

    cos, sin = first_ref[0, 95:96, :], first_ref[1, 95:96, :]
    end = jnp.where(iota((16, 128), 1) % 2 == 0, 1.0, -1.0)
    put(128 * 31 + 16, jnp.where(k < 15, cos * cos_k + sin * sin_k, end))
    put(128 * 31 + 80, jnp.where(k < 15, -(sin * cos_k - cos * sin_k), 0.0))

    lane = iota((BLOCKS, 128), 1)
    j, used = bin_of(iota((BLOCKS, 128), 0), lane)
    factor = jnp.where(used, scale, 0.0)
    signed = jnp.where(lane < 64, -factor, factor)
    for a in range(5):
        cos, sin = cos_sin((128 * a * j).astype(jnp.float32))
        if a < 4:
            powers_ref[0, 4 + a] = cos * factor
            powers_ref[1, 4 + a] = sin * signed
        if a > 0:
            powers_ref[0, 4 - a] = cos * factor
            powers_ref[1, 4 - a] = -sin * signed
    row = iota((8, 128), 0)
    low = row < 4
    slot = 4 * (2 * lax.axis_index("x") + lax.axis_index("core")) + row % 4
    live = jnp.where(slot < count_ref[0], 1.0, 0.0)

    @pl.loop(0, BLOCKS, unroll=4)
    def _(c):
        row = pl.ds(c, 1)
        for part in range(2):
            for q in range(4):
                two = jnp.where(low, powers_ref[part, 2 * q, row, :], powers_ref[part, 2 * q + 1, row, :])
                turn_ref[part, pl.ds(pl.multiple_of(32 * c + 8 * q, 8), 8), :] = two * live


def inverse(count, after):
    vmem = pl.BlockSpec(memory_space=pltpu.VMEM)
    return pl.pallas_call(
        inverse_kernel,
        out_shape=(
            jax.ShapeDtypeStruct((2, 32 * BLOCKS, 128), jnp.float32),
            jax.ShapeDtypeStruct((128 * BLOCKS, 256), jnp.bfloat16),
        ),
        in_specs=[pl.BlockSpec(memory_space=pltpu.SMEM), pl.BlockSpec(memory_space=pl.ANY)],
        out_specs=(vmem, vmem),
        scratch_shapes=[pltpu.VMEM((2, 96, 128), jnp.float32), pltpu.VMEM((2, 8, BLOCKS, 128), jnp.float32)],
        compiler_params=pltpu.CompilerParams(vmem_limit_bytes=12 * MB),
        cost_estimate=pl.CostEstimate(flops=10 * 10**6, bytes_accessed=3 * 10**6, transcendentals=0),
        name="inverse",
    )(count, after)


def total_kernel(own_ref, one_ref, two_ref, three_ref, after_ref, out_ref):
    total = own_ref[...] + one_ref[...] + two_ref[...] + three_ref[...]
    out_ref[0:DENSE, :] = total
    group = iota((32, 128), 1) // 16 % 4
    first, second, third = (pltpu.roll(total[32 * t:32 * t + 32], 128 - (48, 16, 32)[t], 1) for t in range(3))
    rest = jnp.where(group == 0, first, jnp.where(group == 2, second, third))
    out_ref[DENSE:, :] = jnp.where(group == 3, 0.0, rest)


def add_parts(own, parts, after):
    vmem = pl.BlockSpec(memory_space=pltpu.VMEM)
    return pl.pallas_call(
        total_kernel,
        out_shape=jax.ShapeDtypeStruct((4 * BLOCKS, 128), jnp.float32),
        in_specs=[vmem] * 4 + [pl.BlockSpec(memory_space=pl.ANY)],
        out_specs=vmem,
        compiler_params=pltpu.CompilerParams(vmem_limit_bytes=4 * MB),
        cost_estimate=pl.CostEstimate(flops=10**5, bytes_accessed=3 * 10**5, transcendentals=0),
        name="total",
    )(own, *parts, after)


def lags_kernel(got_ref, turn_ref, table_ref, out_ref, left_ref):
    for c in range(BLOCKS):
        slot = SLOT[c]
        two = got_ref[8 * (slot // 2):8 * (slot // 2) + 8, :]
        low = iota((8, 128), 0) < 4
        turned = pltpu.roll(two, 4, 0)
        total = jnp.where(low, two, turned) if slot % 2 == 0 else jnp.where(low, turned, two)
        total = jnp.concatenate([total] * 4, axis=0)
        at = slice(32 * c, 32 * c + 32)
        turned = total * turn_ref[0, at, :] + pltpu.roll(total, 64, 1) * turn_ref[1, at, :]
        coarse = turned.astype(jnp.bfloat16)
        left_ref[0:32, 128 * c:128 * c + 128] = coarse
        left_ref[32:64, 128 * c:128 * c + 128] = (turned - coarse.astype(jnp.float32)).astype(jnp.bfloat16)
    both = jnp.dot(left_ref[...], table_ref[...], preferred_element_type=jnp.float32)
    both = both[:32] + both[32:]
    both = both[:, :128] + both[:, 128:]
    for a in range(8):
        out_ref[:, 128 * a:128 * a + 128] = both[4 * a:4 * a + 4, :]


def lags(got, turn, table):
    vmem = pl.BlockSpec(memory_space=pltpu.VMEM)
    return pl.pallas_call(
        lags_kernel,
        out_shape=jax.ShapeDtypeStruct((4, LAGS), jnp.float32),
        in_specs=[vmem] * 3,
        out_specs=vmem,
        scratch_shapes=[pltpu.VMEM((64, 128 * BLOCKS), jnp.bfloat16)],
        compiler_params=pltpu.CompilerParams(vmem_limit_bytes=16 * MB),
        cost_estimate=pl.CostEstimate(flops=2 * 64 * 4096 * 256, bytes_accessed=4 * 10**6, transcendentals=0),
        name="lags",
    )(got, turn, table)


def shards(records, pair_source, pair_partner, pair_count):
    sent = transform(records.reshape(ROWS, N), pair_source, pair_partner, tables())
    rows = BLOCKS * PIECE
    got = lax.all_to_all(sent.reshape(rows // 2, 2, 128), "chan", 0, 0, tiled=True, axis_index_groups=[ORDER])
    got = got.reshape(rows, 128)
    away, data, lists = cross(away_kernel, got)
    near = lax.ppermute(away, "core", [(0, 1), (1, 0)])
    spectra = (cross(keep_kernel, data, lists)[0] + near).reshape(4, DENSE, 128)
    parts = [lax.ppermute(spectra[k], "x", [(x, (x + k) % 4) for x in range(4)]) for k in (1, 3, 2)]
    turn, table = inverse(pair_count, spectra)
    total = add_parts(spectra[0], parts, turn)
    last = lax.all_to_all(total.reshape(BLOCKS, 4, 128), "chan", 0, 0, axis_index_groups=[ORDER])
    return lags(last.reshape(4 * BLOCKS, 128), turn, table)


def solution(mesh):
    chips = Mesh(mesh.devices.reshape(BLOCKS, WINS // 2, 2), ("chan", "x", "core"))
    placed = (P("chan", ("x", "core"), None), P("chan", None), P("chan", None), P("chan"))
    return jax.shard_map(
        shards, mesh=chips, in_specs=placed, out_specs=P(("chan", "x", "core"), None), check_vma=False
    )
```
